32 devices in a mesh: fsdp: 16 (over z, y, core), tp: 2 (over x).
Axes of the slice: x: 2, y: 2, z: 4, core: 2. Of those that a mesh axis runs over, the one named last changes fastest.
Arguments:
- tokens: bfloat16 [4096, 2304], P(('fsdp', 'tp')), may hold values from -6 to 6
- seg_lengths: int32 [16, 13], P('fsdp'), may hold values from 1 to 64, 256 in all within a row
- parents: int32 [16, 13], P('fsdp'), may hold values from 0 to 11, as said below
- attn_gain: float32 [2304], replicated, may hold values from 0.1 to 1.9
- w_query: bfloat16 [2304, 2048], P('fsdp', 'tp'), may hold values from -0.1875 to 0.1875
- w_key: bfloat16 [2304, 1024], P('fsdp', 'tp'), may hold values from -0.1875 to 0.1875
- w_value: bfloat16 [2304, 1024], P('fsdp', 'tp'), may hold values from -0.125 to 0.125
- w_out: bfloat16 [2048, 2304], P('tp', 'fsdp'), may hold values from -0.125 to 0.125
- attn_post_gain: float32 [2304], replicated, may hold values from 0.1 to 1.9
- ffn_gain: float32 [2304], replicated, may hold values from 0.1 to 1.9
- w_gate: bfloat16 [2304, 9216], P('fsdp', 'tp'), may hold values from -0.125 to 0.125
- w_up: bfloat16 [2304, 9216], P('fsdp', 'tp'), may hold values from -0.125 to 0.125
- w_down: bfloat16 [9216, 2304], P('tp', 'fsdp'), may hold values from -0.0625 to 0.0625
- ffn_post_gain: float32 [2304], replicated, may hold values from 0.1 to 1.9
- out_grad: bfloat16 [4096, 2304], P(('fsdp', 'tp')), may hold values from -6 to 6
Outputs:
- mixed: bfloat16 [4096, 2304], P(('fsdp', 'tp'))
- grad_tokens: float32 [4096, 2304], P(('fsdp', 'tp'))
- grad_attn_gain: float32 [2304], P('fsdp')
- grad_query: float32 [2304, 2048], P('fsdp', 'tp')
- grad_key: float32 [2304, 1024], P('fsdp', 'tp')
- grad_value: float32 [2304, 1024], P('fsdp', 'tp')
- grad_out: float32 [2048, 2304], P('tp', 'fsdp')
- grad_attn_post_gain: float32 [2304], P('fsdp')
- grad_ffn_gain: float32 [2304], P('fsdp')
- grad_gate: float32 [2304, 9216], P('fsdp', 'tp')
- grad_up: float32 [2304, 9216], P('fsdp', 'tp')
- grad_down: float32 [9216, 2304], P('tp', 'fsdp')
- grad_ffn_post_gain: float32 [2304], P('fsdp')
The draws below stay inside these ranges and needn't reach their ends.
Inputs may be any that keep to these rules, and one draw needn't show every extreme that they name: `parents`: segment 0 of each tree is its root and its own parent; every other segment's parent is a lower-numbered segment of the same tree; the last segment's parent is the one before it. `seg_lengths`: each tree's 13 lengths add up to 256.
All inputs are finite; a program needn't handle non-finite values.
Results may differ from the reference program's by a relative error of at most 0.015.
The reference program's roundings to bfloat16 on the way count: a program that leaves them out, or rounds other values in their place, can miss the bound.
Values may be sent and summed in bfloat16 or wider, within the bound.
No kernel may reach another device: no remote copies, remote signals or barrier semaphores. Data moves between devices by JAX's collectives and lax.ppermute only.
A program may use at most 512 MiB of HBM per device.

```python
import math
import jax
import jax.numpy as jnp
import numpy as np
from jax import lax

D = 2304
H = 8
KV = 4
HD = 256
FF = 9216
NSEG = 13
TREE_LEN = 256
TREES = 16
TOKENS = 4096


def draw_parents(key, part):
    key = jax.random.fold_in(key, 7)
    seg_index = jnp.arange(NSEG, dtype=jnp.int32)
    raw_bits = jax.random.randint(key, (TREES, NSEG), 0, 1 << 30, dtype=jnp.int32)
    chosen = raw_bits % jnp.maximum(seg_index, 1)[None, :]
    return jnp.where(seg_index[None, :] == NSEG - 1, NSEG - 2, chosen).astype(jnp.int32)


def strengthened(result, key, source, target, parts, factor):
    def block_of(dim):
        return (jnp.arange(result.shape[dim]) // (result.shape[dim] // parts)).reshape((-1,) + (1,) * (result.ndim - 1 - dim))

    first = jax.random.permutation(key, parts)[block_of(target)]
    other_side = (block_of(target) + parts // 2) % parts
    return jnp.where((block_of(source) == first) | (block_of(source) == other_side), factor * result, result)


def shard_levels(rng, dims, pieces, smallest, top_value):
    level, own = 1.0, jax.random.fold_in(rng, 6)
    for position, parts in pieces:
        steps = jnp.exp(jax.random.uniform(jax.random.fold_in(own, position), (parts,), jnp.float32, smallest / len(pieces), top_value / len(pieces)))
        level = level * jnp.repeat(steps, dims[position] // parts).reshape([-1 if axis == position else 1 for axis in range(len(dims))])
    return level


def length_profile(number_of, total, limit, skew):
    loads = [(1 << 20) // math.isqrt(rank ** skew) + 1 for rank in range(2, number_of + 1)]
    surplus, holding = total - limit - (number_of - 1), [1] * (number_of - 1)
    while surplus > 0:
        candidates = [i for i in range(number_of - 1) if holding[i] < limit]
        pool, left = sum([loads[i] for i in candidates]), surplus
        for i in candidates:
            addition = min(limit - holding[i], max(1, left * loads[i] // pool), surplus)
            holding[i] = holding[i] + addition
            surplus = surplus - addition
    return np.array([limit] + holding)


def uneven(rng, number_of, total, limit, slope):
    if number_of == 2:
        one = jax.random.randint(rng, (), max(1, total - limit), min(limit, total - 1) + 1)
        return jnp.stack([one, total - one])
    lengths = jnp.asarray(length_profile(number_of, total, limit, slope), jnp.int32)
    twos = (number_of - 1) // 2
    giver, sink = lengths[1:1 + 2 * twos:2], lengths[2:2 + 2 * twos:2]
    margin = jnp.minimum(giver - 1, limit - sink)
    moved = jax.random.randint(jax.random.fold_in(rng, 1), (twos,), 0, 1 << 20) % (margin + 1)
    lengths = lengths.at[1:1 + 2 * twos:2].set(giver - moved).at[2:2 + 2 * twos:2].set(sink + moved)
    return lengths[jax.random.permutation(jax.random.fold_in(rng, 2), number_of)]


def centred(rng, shape, spread, reach, shards=(), held_as=jnp.bfloat16):
    loudness = shard_levels(rng, shape, shards, -0.22, 0.18) if shards else 1.0
    drawn = jax.random.normal(rng, shape, jnp.float32) * spread * loudness
    return jnp.minimum(jnp.maximum(drawn, -reach), reach).astype(held_as)


def gaussian_with(key, shape, scale, bound, cuts, heavy, kind=jnp.bfloat16):
    array = scale * jax.random.normal(key, shape, jnp.float32)
    if cuts:
        array = array * shard_levels(key, shape, cuts, -0.22, 0.18)
    return jnp.clip(strengthened(array, jax.random.fold_in(key, 3), *heavy), -bound, bound).astype(kind)


def setup_inputs(seed: int = 0) -> dict:
    streams_of = jax.random.split(jax.random.key(seed), 16)
    tokens = centred(streams_of[0], (TOKENS, D), 1.0, 6.0, ((0, 32),))
    seg_lengths = jax.vmap(lambda own: uneven(own, NSEG, TREE_LEN, TREE_LEN // 4, 1))(jax.random.split(streams_of[1], TREES)).reshape((TREES, NSEG)).astype(jnp.int32)
    parents = draw_parents(jax.random.fold_in(streams_of[15], 71), 0)
    attn_gain = jnp.clip(1.0 + 0.18 * jax.random.normal(streams_of[3], (D,), jnp.float32), 0.1, 1.9)
    w_query = centred(streams_of[4], (D, H * HD), (D // 2) ** -0.5, 0.1875, ((0, 16), (1, 2)))
    w_key = centred(streams_of[5], (D, KV * HD), (D // 2) ** -0.5, 0.1875, ((0, 16), (1, 2)))
    w_value = centred(streams_of[6], (D, KV * HD), D ** -0.5, 0.125, ((0, 16), (1, 2)))
    w_out = centred(streams_of[7], (H * HD, D), (H * HD) ** -0.5, 0.125, ((0, 2), (1, 16)))
    attn_post_gain = jnp.clip(1.0 + 0.18 * jax.random.normal(streams_of[8], (D,), jnp.float32), 0.1, 1.9)
    ffn_gain = jnp.clip(1.0 + 0.18 * jax.random.normal(streams_of[9], (D,), jnp.float32), 0.1, 1.9)
    w_gate = centred(streams_of[10], (D, FF), D ** -0.5, 0.125, ((0, 16), (1, 2)))
    w_up = centred(streams_of[11], (D, FF), D ** -0.5, 0.125, ((0, 16), (1, 2)))
    w_down = centred(streams_of[12], (FF, D), FF ** -0.5, 0.0625, ((0, 2), (1, 16)))
    ffn_post_gain = jnp.clip(1.0 + 0.18 * jax.random.normal(streams_of[13], (D,), jnp.float32), 0.1, 1.9)
    out_grad = gaussian_with(streams_of[14], (TOKENS, D), 1.0, 6.0, ((0, 32),), (0, 1, 32, 2.75))
    return dict(tokens=tokens, seg_lengths=seg_lengths, parents=parents, attn_gain=attn_gain, w_query=w_query, w_key=w_key, w_value=w_value, w_out=w_out, attn_post_gain=attn_post_gain, ffn_gain=ffn_gain, w_gate=w_gate, w_up=w_up, w_down=w_down, ffn_post_gain=ffn_post_gain, out_grad=out_grad)


NORM_EPS = 1e-06
SOFT_CAP = 50.0
ROPE_BASE = 10000.0
MASK_FILL = -1e+30

@jax.custom_vjp
def low(v):
    return lax.optimization_barrier(v.astype(jnp.bfloat16)).astype(jnp.float32)

@jax.custom_vjp
def low_back(v):
    return v

def low_keep(v):
    return (low(v), None)

def low_pass(kept, grad):
    return (grad,)

def back_keep(v):
    return (v, None)

def back_low(kept, grad):
    return (low(grad),)
low.defvjp(low_keep, low_pass)
low_back.defvjp(back_keep, back_low)

def multiply(operand, weight):
    return jnp.dot(operand, weight, precision=lax.Precision.HIGHEST, preferred_element_type=jnp.float32)

def norm_scale(values, gain):
    return values * lax.rsqrt(lax.optimization_barrier(jnp.mean(values * values, axis=-1, keepdims=True)) + NORM_EPS) * gain

def tree_tables(lengths_row, parents_row, row_total):
    seg_count = lengths_row.shape[0]
    seg_index = jnp.arange(seg_count, dtype=jnp.int32)
    ancestor = (seg_index[:, None] == seg_index[None, :]) | (parents_row[:, None] == seg_index[None, :])
    for repeat in range(seg_count.bit_length()):
        ancestor = jnp.any(ancestor[:, :, None] & ancestor[None, :, :], axis=1)
    seg_ends = jnp.cumsum(lengths_row).astype(jnp.int32)
    seg_starts = seg_ends - lengths_row
    token_index = jnp.arange(row_total, dtype=jnp.int32)
    segment = lax.optimization_barrier(jnp.sum((token_index[:, None] >= seg_ends[None, :]).astype(jnp.int32), axis=1))
    strict = ancestor & (seg_index[:, None] != seg_index[None, :])
    offsets = lax.optimization_barrier(jnp.sum(jnp.where(strict, lengths_row[None, :], 0), axis=1)).astype(jnp.int32)
    one_hot = segment[:, None] == seg_index[None, :]
    positions = lax.optimization_barrier(jnp.sum(jnp.where(one_hot, (offsets - seg_starts)[None, :], 0), axis=1)).astype(jnp.int32) + token_index
    reached = jnp.any(one_hot[:, :, None] & ancestor[None, :, :], axis=1)
    allowed = jnp.any(reached[:, None, :] & one_hot[None, :, :], axis=2) & (token_index[None, :] <= token_index[:, None])
    return (positions, allowed)

def rope_tables(positions, width):
    half_width = width // 2
    frequency = ROPE_BASE ** (-2.0 * jnp.arange(half_width, dtype=jnp.float32) / width)
    angles = positions.astype(jnp.float32)[:, None] * frequency[None, :]
    return (jnp.cos(angles), jnp.sin(angles))

def rotate(values, cosine_table, sine_table):
    half_width = values.shape[-1] // 2
    front_half = values[..., :half_width]
    back_half = values[..., half_width:]
    cos_heads = cosine_table[:, None, :]
    sin_heads = sine_table[:, None, :]
    return jnp.concatenate([front_half * cos_heads - back_half * sin_heads, back_half * cos_heads + front_half * sin_heads], axis=-1)

def tree_attention(packed):
    query_rows, key_rows, value_rows, allowed = packed
    scaling = query_rows.shape[-1] ** (-0.5)
    scores = low_back(jnp.einsum('qgrd,kgd->grqk', query_rows, key_rows, precision=lax.Precision.HIGHEST))
    capped = SOFT_CAP * jnp.tanh(scores * scaling / SOFT_CAP)
    masked = jnp.where(allowed[None, None], capped, MASK_FILL)
    highest = lax.optimization_barrier(jnp.max(masked, axis=-1, keepdims=True))
    weights = jnp.exp(masked - highest)
    probability = low(weights / lax.optimization_barrier(jnp.sum(weights, axis=-1, keepdims=True)))
    return jnp.einsum('grqk,kgd->qgrd', probability, value_rows, precision=lax.Precision.HIGHEST)

def reference(tokens, seg_lengths, parents, attn_gain, w_query, w_key, w_value, w_out, attn_post_gain, ffn_gain, w_gate, w_up, w_down, ffn_post_gain, out_grad):
    positions, allowed = jax.vmap(lambda lengths_row, parents_row: tree_tables(lengths_row, parents_row, TREE_LEN))(seg_lengths, parents)
    cosine_table, sine_table = rope_tables(positions.reshape(TOKENS), HD)
    group_size = H // KV
    attention = jax.checkpoint(tree_attention)

    def forward(state_in, gain_one, query_w, key_w, value_w, out_w, gain_two, gain_three, gate_w, up_w, down_w, gain_four):
        normed_one = low(norm_scale(state_in, gain_one))
        queries = low(rotate(low_back(multiply(normed_one, query_w)).reshape(TOKENS, H, HD), cosine_table, sine_table))
        key_all = low(rotate(low_back(multiply(normed_one, key_w)).reshape(TOKENS, KV, HD), cosine_table, sine_table))
        value_all = low(low_back(multiply(normed_one, value_w))).reshape(TOKENS, KV, HD)
        attended = lax.map(attention, (queries.reshape(TREES, TREE_LEN, KV, group_size, HD), key_all.reshape(TREES, TREE_LEN, KV, HD), value_all.reshape(TREES, TREE_LEN, KV, HD), allowed))
        attended = low(low_back(attended.reshape(TOKENS, H * HD)))
        branch = low_back(multiply(attended, out_w))
        hidden = state_in + norm_scale(branch, gain_two)
        normed_two = low(norm_scale(hidden, gain_three))
        gate_proj = low_back(multiply(normed_two, gate_w))
        upward = low_back(multiply(normed_two, up_w))
        activated = low(jax.nn.gelu(gate_proj, approximate=True) * upward)
        ffn_out = low_back(multiply(activated, down_w))
        return hidden + norm_scale(ffn_out, gain_four)
    mixed, pullback = jax.vjp(forward, tokens.astype(jnp.float32), attn_gain.astype(jnp.float32), w_query.astype(jnp.float32), w_key.astype(jnp.float32), w_value.astype(jnp.float32), w_out.astype(jnp.float32), attn_post_gain.astype(jnp.float32), ffn_gain.astype(jnp.float32), w_gate.astype(jnp.float32), w_up.astype(jnp.float32), w_down.astype(jnp.float32), ffn_post_gain.astype(jnp.float32))
    grads = pullback(out_grad.astype(jnp.float32))
    return (mixed.astype(jnp.bfloat16), grads[0], grads[1], grads[2], grads[3], grads[4], grads[5], grads[6], grads[7], grads[8], grads[9], grads[10], grads[11])
```

```python
import jax
import jax.numpy as jnp
from jax import lax
from jax.sharding import Mesh
from jax.sharding import PartitionSpec as P

HD = 256
NORM_EPS = 1e-06
SOFT_CAP = 50.0
ROPE_BASE = 10000.0
MASK_FILL = -1e30
BF = jnp.bfloat16
F32 = jnp.float32


def tree_tables(lengths_row, parents_row, row_total):
    seg_count = lengths_row.shape[0]
    seg_index = jnp.arange(seg_count, dtype=jnp.int32)
    ancestor = (seg_index[:, None] == seg_index[None, :]) | (
        parents_row[:, None] == seg_index[None, :]
    )
    for repeat in range(seg_count.bit_length()):
        ancestor = jnp.any(ancestor[:, :, None] & ancestor[None, :, :], axis=1)
    seg_ends = jnp.cumsum(lengths_row)
    seg_starts = seg_ends - lengths_row
    token_index = jnp.arange(row_total, dtype=jnp.int32)
    segment = jnp.sum((token_index[:, None] >= seg_ends[None, :]).astype(jnp.int32), axis=1)
    strict = ancestor & (seg_index[:, None] != seg_index[None, :])
    offsets = jnp.sum(jnp.where(strict, lengths_row[None, :], 0), axis=1)
    one_hot = segment[:, None] == seg_index[None, :]
    positions = (
        jnp.sum(jnp.where(one_hot, (offsets - seg_starts)[None, :], 0), axis=1) + token_index
    )
    reached = jnp.any(one_hot[:, :, None] & ancestor[None, :, :], axis=1)
    allowed = jnp.any(reached[:, None, :] & one_hot[None, :, :], axis=2) & (
        token_index[None, :] <= token_index[:, None]
    )
    return (positions, allowed)


def rope_tables(positions, width):
    half_width = width // 2
    frequency = ROPE_BASE ** (-2.0 * jnp.arange(half_width, dtype=F32) / width)
    angles = positions.astype(F32)[:, None] * frequency[None, :]
    return (jnp.cos(angles), jnp.sin(angles))


def rotate(values, cosine_table, sine_table):
    half_width = values.shape[-1] // 2
    front_half = values[..., :half_width]
    back_half = values[..., half_width:]
    cos_heads = cosine_table[:, None, :]
    sin_heads = sine_table[:, None, :]
    return jnp.concatenate(
        [
            front_half * cos_heads - back_half * sin_heads,
            back_half * cos_heads + front_half * sin_heads,
        ],
        axis=-1,
    )


def norm_back(grad_unit, unit, inverse):
    return inverse * (grad_unit - unit * jnp.mean(grad_unit * unit, axis=-1, keepdims=True))


def gating(gate_proj, upward):
    return jax.nn.gelu(gate_proj, approximate=True) * upward


def swap(values, axis, mask):
    size = lax.axis_size(axis)
    return lax.ppermute(values, axis, [(i, i ^ mask) for i in range(size)])


def rows_dot(left, right):
    return lax.dot_general(left, right, (((1,), (0,)), ((), ())), preferred_element_type=F32)


def cols_dot(left, right):
    return lax.dot_general(left, right, (((1,), (1,)), ((), ())), preferred_element_type=F32)


def outer_dot(left, right):
    return lax.dot_general(left, right, (((0,), (0,)), ((), ())), preferred_element_type=F32)


def pair_gather(values, axis):
    mine = lax.axis_index(axis)
    other = swap(values, axis, 1)
    first = jnp.where(mine == 0, values, other)
    second = jnp.where(mine == 0, other, values)
    return jnp.concatenate([first, second], axis=0)


def pair_sum(partial, axis):
    rows = partial.shape[0] // 2
    mine = lax.axis_index(axis)
    sent = lax.dynamic_slice_in_dim(partial, (1 - mine) * rows, rows, 0).astype(BF)
    kept = lax.dynamic_slice_in_dim(partial, mine * rows, rows, 0)
    return kept + swap(sent, axis, 1).astype(F32)


def line_gather(values):
    return jnp.concatenate([values] + [swap(values, "z", k) for k in (1, 2, 3)], axis=0)


def line_sum(partial):
    rows = partial.shape[0] // 4
    total = partial[:rows]
    for k in (1, 2, 3):
        total = total + swap(partial[k * rows : (k + 1) * rows].astype(BF), "z", k).astype(F32)
    return total


def line_exchange(weight):
    rows, parts, count, cols = weight.shape
    here = lax.axis_index("z")
    held = jnp.zeros((count, rows, parts * cols), weight.dtype)
    for k in range(count):
        piece = lax.dynamic_index_in_dim(weight, here ^ k, 2, keepdims=False).reshape(
            rows, parts * cols
        )
        piece = piece if k == 0 else swap(piece, "z", k)
        held = lax.dynamic_update_index_in_dim(held, piece, here ^ k, 0)
    return held.reshape(count * rows, parts * cols)


def attend_forward(query_grid, key_rows, value_rows, allowed):
    total_rows = query_grid.shape[0]
    scaling = query_grid.shape[-1] ** (-0.5)
    scores = jnp.einsum("qgrd,kgd->grqk", query_grid, key_rows, preferred_element_type=F32)
    capped = SOFT_CAP * jnp.tanh(scores * scaling / SOFT_CAP)
    masked = jnp.where(allowed[None, None], capped, MASK_FILL)
    highest = jnp.max(masked, axis=-1, keepdims=True)
    weights = jnp.exp(masked - highest)
    totals = jnp.sum(weights, axis=-1, keepdims=True)
    probability = weights / totals
    prob_low = probability.astype(BF)
    out = jnp.einsum("grqk,kgd->qgrd", prob_low, value_rows, preferred_element_type=F32)
    return (out.astype(BF).reshape(total_rows, -1), capped, probability)


def attend_backward(query_grid, key_rows, value_rows, capped, probability, grad_grid):
    scaling = query_grid.shape[-1] ** (-0.5)
    prob_low = probability.astype(BF)
    grad_prob = jnp.einsum("qgrd,kgd->grqk", grad_grid, value_rows, preferred_element_type=F32)
    inner = jnp.sum(probability * grad_prob, axis=-1, keepdims=True)
    grad_cap = probability * (grad_prob - inner)
    tanh_value = capped / SOFT_CAP
    grad_score = (grad_cap * scaling * (1.0 - tanh_value * tanh_value)).astype(BF)
    query_grad = jnp.einsum("grqk,kgd->qgrd", grad_score, key_rows, preferred_element_type=F32)
    key_grad = jnp.einsum("grqk,qgrd->kgd", grad_score, query_grid, preferred_element_type=F32)
    value_grad = jnp.einsum("grqk,qgrd->kgd", prob_low, grad_grid, preferred_element_type=F32)
    return (query_grad, key_grad, value_grad)


def row_sum(parts, axes):
    return lax.psum_scatter(parts, axes, scatter_dimension=0, tiled=True)


def gain_sum(parts):
    parts = lax.psum(parts, ("z", "y", "c", "x"))
    width = parts.shape[1] // (lax.axis_size("z") * lax.axis_size("y") * lax.axis_size("c"))
    at = (lax.axis_index("c") * lax.axis_size("y") + lax.axis_index("y")) * lax.axis_size(
        "z"
    ) + lax.axis_index("z")
    return lax.dynamic_slice_in_dim(parts, at * width, width, 1)


def on_device(
    tokens,
    seg_lengths,
    parents,
    attn_gain,
    w_query,
    w_key,
    w_value,
    w_out,
    attn_post_gain,
    ffn_gain,
    w_gate,
    w_up,
    w_down,
    ffn_post_gain,
    out_grad,
):
    local_rows, width = tokens.shape
    z_size, y_size, c_size = lax.axis_size("z"), lax.axis_size("y"), lax.axis_size("c")
    shard = width // (z_size * y_size * c_size)
    group_rows = local_rows * lax.axis_size("x")
    head_cols = w_query.shape[1]
    kv_cols = w_key.shape[1]
    heads_here = head_cols // HD
    kv_here = kv_cols // HD
    group_size = heads_here // kv_here
    ff_here = w_gate.shape[1]
    ff_cut = ff_here // z_size

    def inward(values):
        lead = values.shape[:-1]
        cut = values.reshape(lead + (z_size, y_size, c_size, shard))
        count = len(lead)
        order = tuple(range(count)) + (count + 2, count + 1, count, count + 3)
        return cut.transpose(order).reshape(lead + (width,))

    def outward(values):
        lead = values.shape[:-1]
        cut = values.reshape(lead + (c_size, y_size, z_size, shard))
        count = len(lead)
        order = tuple(range(count)) + (count + 2, count + 1, count, count + 3)
        return cut.transpose(order).reshape(lead + (width,))

    row_axes = ("c", "y", "z")
    positions, allowed = tree_tables(seg_lengths[0], parents[0], group_rows)
    cosine_table, sine_table = rope_tables(positions, HD)
    attn_gain, attn_post_gain = inward(attn_gain), inward(attn_post_gain)
    ffn_gain, ffn_post_gain = inward(ffn_gain), inward(ffn_post_gain)
    state_in = inward(tokens).astype(F32)
    out_cotan = inward(out_grad).astype(F32)

    qkv_here = jnp.concatenate([w_query, w_key, w_value], axis=1)
    qkv_weight = lax.all_gather(qkv_here, row_axes, axis=0, tiled=True)
    out_weight = lax.all_gather(w_out.T, row_axes, axis=0, tiled=True)
    up_here = jnp.stack([w_gate, w_up], axis=1).reshape(shard, 2, z_size, ff_cut)
    up_line = line_exchange(up_here)
    down_line = line_exchange(w_down.T.reshape(shard, 1, z_size, ff_cut))
    up_weight = lax.all_gather(up_line, ("x", "c", "y"), axis=0, tiled=True).reshape(
        2, width, 2 * ff_cut
    )
    down_weight = lax.all_gather(down_line, ("x", "c", "y"), axis=0, tiled=True).reshape(
        2, width, ff_cut
    )

    inverse_one = lax.rsqrt(jnp.mean(state_in * state_in, axis=-1, keepdims=True) + NORM_EPS)
    unit_one = state_in * inverse_one
    normed_one = pair_gather((unit_one * attn_gain).astype(BF), "x")
    qkv_proj = rows_dot(normed_one, qkv_weight)
    queries = rotate(
        qkv_proj[:, :head_cols].reshape(group_rows, heads_here, HD), cosine_table, sine_table
    ).astype(BF)
    key_rows = rotate(
        qkv_proj[:, head_cols : head_cols + kv_cols].reshape(group_rows, kv_here, HD),
        cosine_table,
        sine_table,
    ).astype(BF)
    value_rows = qkv_proj[:, head_cols + kv_cols :].astype(BF).reshape(group_rows, kv_here, HD)
    query_grid = queries.reshape(group_rows, kv_here, group_size, HD)
    attended, capped, probability = attend_forward(query_grid, key_rows, value_rows, allowed)
    branch = pair_sum(cols_dot(attended, out_weight), "x")
    inverse_two = lax.rsqrt(jnp.mean(branch * branch, axis=-1, keepdims=True) + NORM_EPS)
    unit_two = branch * inverse_two
    hidden = state_in + unit_two * attn_post_gain
    inverse_three = lax.rsqrt(jnp.mean(hidden * hidden, axis=-1, keepdims=True) + NORM_EPS)
    unit_three = hidden * inverse_three

    normed_two = line_gather((unit_three * ffn_gain).astype(BF))
    acts, pulls, ffn_part = [], [], 0.0
    for half in range(2):
        gate_up = rows_dot(normed_two, up_weight[half])
        act, pull = jax.vjp(gating, gate_up[:, :ff_cut], gate_up[:, ff_cut:])
        acts.append(act.astype(BF))
        pulls.append(pull)
        ffn_part = ffn_part + cols_dot(acts[half], down_weight[half])
    ffn_out = line_sum(ffn_part)
    inverse_four = lax.rsqrt(jnp.mean(ffn_out * ffn_out, axis=-1, keepdims=True) + NORM_EPS)
    unit_four = ffn_out * inverse_four
    mixed = (hidden + unit_four * ffn_post_gain).astype(BF)
    gain_four = jnp.sum(out_cotan * unit_four, axis=0)
    d_ffn = line_gather(
        norm_back(out_cotan * ffn_post_gain, unit_four, inverse_four).astype(BF)
    )
    d_ups, normed_part = [], 0.0
    for half in range(2):
        d_act = rows_dot(d_ffn, down_weight[half])
        d_ups.append(jnp.concatenate(pulls[half](d_act), axis=1).astype(BF))
        normed_part = normed_part + cols_dot(d_ups[half], up_weight[half])
    d_normed_two = line_sum(normed_part)
    grad_ffn = []
    for half in range(2):
        part = jnp.concatenate(
            [outer_dot(normed_two, d_ups[half]), outer_dot(d_ffn, acts[half])], axis=1
        ).astype(BF)
        grad_ffn.append(row_sum(part, ("c", "y")))
    x_here = lax.axis_index("x")
    grad_ffn = jnp.where(x_here == 0, grad_ffn[0], grad_ffn[1]).astype(F32) + swap(
        jnp.where(x_here == 0, grad_ffn[1], grad_ffn[0]), "x", 1
    ).astype(F32)
    grad_ffn = grad_ffn.astype(BF).reshape(z_size, shard, 3 * ff_cut)
    grad_cut = jnp.zeros((z_size, shard, 3 * ff_cut), F32)
    z_here = lax.axis_index("z")
    for k in range(z_size):
        piece = lax.dynamic_index_in_dim(grad_ffn, z_here ^ k, 0, keepdims=False)
        piece = piece if k == 0 else swap(piece, "z", k)
        grad_cut = lax.dynamic_update_index_in_dim(grad_cut, piece.astype(F32), z_here ^ k, 0)
    grad_cut = grad_cut.reshape(z_size, shard, 3, ff_cut).transpose(2, 1, 0, 3)
    grad_cut = grad_cut.reshape(3, shard, ff_here)

    gain_three = jnp.sum(d_normed_two * unit_three, axis=0)
    d_hidden = out_cotan + norm_back(d_normed_two * ffn_gain, unit_three, inverse_three)
    gain_two = jnp.sum(d_hidden * unit_two, axis=0)
    d_branch = pair_gather(
        norm_back(d_hidden * attn_post_gain, unit_two, inverse_two).astype(BF), "x"
    )
    d_attended = rows_dot(d_branch, out_weight).astype(BF)
    grad_grid = d_attended.reshape(group_rows, kv_here, group_size, HD)
    query_grad, key_grad, value_grad = attend_backward(
        query_grid, key_rows, value_rows, capped, probability, grad_grid
    )
    query_back = rotate(
        query_grad.reshape(group_rows, heads_here, HD), cosine_table, -sine_table
    ).astype(BF)
    key_back = rotate(key_grad, cosine_table, -sine_table).astype(BF)
    d_qkv = jnp.concatenate(
        [
            query_back.reshape(group_rows, head_cols),
            key_back.reshape(group_rows, kv_cols),
            value_grad.astype(BF).reshape(group_rows, kv_cols),
        ],
        axis=1,
    )
    d_normed_one = pair_sum(cols_dot(d_qkv, qkv_weight), "x")
    gain_one = jnp.sum(d_normed_one * unit_one, axis=0)
    grad_tokens = d_hidden + norm_back(d_normed_one * attn_gain, unit_one, inverse_one)
    grad_attn = jnp.concatenate(
        [outer_dot(normed_one, d_qkv), outer_dot(d_branch, attended)], axis=1
    ).astype(BF)
    grad_attn = row_sum(grad_attn, row_axes).astype(F32)
    gains = gain_sum(jnp.stack([gain_one, gain_two, gain_three, gain_four], axis=0))
    key_from, value_from = head_cols, head_cols + kv_cols
    out_from = head_cols + 2 * kv_cols
    return (
        outward(mixed),
        outward(grad_tokens),
        gains[0],
        grad_attn[:, :key_from],
        grad_attn[:, key_from:value_from],
        grad_attn[:, value_from:out_from],
        grad_attn[:, out_from:].T,
        gains[1],
        gains[2],
        grad_cut[0],
        grad_cut[1],
        grad_cut[2].T,
        gains[3],
    )


def solution(mesh):
    count, pair = mesh.devices.shape
    grid = Mesh(mesh.devices.reshape(4, count // 8, 2, pair), ("z", "y", "c", "x"))
    rows = ("z", "y", "c")
    return jax.shard_map(
        on_device,
        mesh=grid,
        in_specs=(
            P(rows + ("x",), None),
            P(rows, None),
            P(rows, None),
            P(),
            P(rows, "x"),
            P(rows, "x"),
            P(rows, "x"),
            P("x", rows),
            P(),
            P(),
            P(rows, "x"),
            P(rows, "x"),
            P("x", rows),
            P(),
            P(rows + ("x",), None),
        ),
        out_specs=(
            P(rows + ("x",), None),
            P(rows + ("x",), None),
            P(rows),
            P(rows, "x"),
            P(rows, "x"),
            P(rows, "x"),
            P("x", rows),
            P(rows),
            P(rows),
            P(rows, "x"),
            P(rows, "x"),
            P("x", rows),
            P(rows),
        ),
        check_vma=False,
    )
```

```python
import jax
import jax.numpy as jnp
from jax import lax
from jax.sharding import Mesh
from jax.sharding import PartitionSpec as P

HD = 256
NORM_EPS = 1e-06
SOFT_CAP = 50.0
ROPE_BASE = 10000.0
MASK_FILL = -1e30
BF = jnp.bfloat16
F32 = jnp.float32


def tree_tables(lengths_row, parents_row, row_total):
    seg_count = lengths_row.shape[0]
    seg_index = jnp.arange(seg_count, dtype=jnp.int32)
    ancestor = (seg_index[:, None] == seg_index[None, :]) | (
        parents_row[:, None] == seg_index[None, :]
    )
    for repeat in range(seg_count.bit_length()):
        ancestor = jnp.any(ancestor[:, :, None] & ancestor[None, :, :], axis=1)
    seg_ends = jnp.cumsum(lengths_row)
    seg_starts = seg_ends - lengths_row
    token_index = jnp.arange(row_total, dtype=jnp.int32)
    segment = jnp.sum((token_index[:, None] >= seg_ends[None, :]).astype(jnp.int32), axis=1)
    strict = ancestor & (seg_index[:, None] != seg_index[None, :])
    offsets = jnp.sum(jnp.where(strict, lengths_row[None, :], 0), axis=1)
    one_hot = segment[:, None] == seg_index[None, :]
    positions = (
        jnp.sum(jnp.where(one_hot, (offsets - seg_starts)[None, :], 0), axis=1) + token_index
    )
    reached = jnp.any(one_hot[:, :, None] & ancestor[None, :, :], axis=1)
    allowed = jnp.any(reached[:, None, :] & one_hot[None, :, :], axis=2) & (
        token_index[None, :] <= token_index[:, None]
    )
    return (positions, allowed)


def rope_tables(positions, width):
    half_width = width // 2
    frequency = ROPE_BASE ** (-2.0 * jnp.arange(half_width, dtype=F32) / width)
    angles = positions.astype(F32)[:, None] * frequency[None, :]
    return (jnp.cos(angles), jnp.sin(angles))


def rotate(values, cosine_table, sine_table):
    half_width = values.shape[-1] // 2
    front_half = values[..., :half_width]
    back_half = values[..., half_width:]
    cos_heads = cosine_table[:, None, :]
    sin_heads = sine_table[:, None, :]
    return jnp.concatenate(
        [
            front_half * cos_heads - back_half * sin_heads,
            back_half * cos_heads + front_half * sin_heads,
        ],
        axis=-1,
    )


def norm_back(grad_unit, unit, inverse):
    return inverse * (grad_unit - unit * jnp.mean(grad_unit * unit, axis=-1, keepdims=True))


def gating(gate_proj, upward):
    return jax.nn.gelu(gate_proj, approximate=True) * upward


def swap(values, axis, mask):
    size = lax.axis_size(axis)
    return lax.ppermute(values, axis, [(i, i ^ mask) for i in range(size)])


def rows_dot(left, right):
    return lax.dot_general(left, right, (((1,), (0,)), ((), ())), preferred_element_type=F32)


def cols_dot(left, right):
    return lax.dot_general(left, right, (((1,), (1,)), ((), ())), preferred_element_type=F32)


def outer_dot(left, right):
    return lax.dot_general(left, right, (((0,), (0,)), ((), ())), preferred_element_type=F32)


def pair_gather(values):
    mine = lax.axis_index("x")
    other = swap(values, "x", 1)
    first = jnp.where(mine == 0, values, other)
    second = jnp.where(mine == 0, other, values)
    return jnp.concatenate([first, second], axis=0)


def pair_sum(partial):
    rows = partial.shape[0] // 2
    mine = lax.axis_index("x")
    sent = lax.dynamic_slice_in_dim(partial, (1 - mine) * rows, rows, 0).astype(BF)
    kept = lax.dynamic_slice_in_dim(partial, mine * rows, rows, 0)
    return kept + swap(sent, "x", 1).astype(F32)


def masks(axis):
    return [1 << i for i in range(lax.axis_size(axis).bit_length() - 1)]


def fold(values, axis):
    for mask in reversed(masks(axis)):
        rows = values.shape[0] // 2
        values = add_low(values[:rows], swap(values[rows:], axis, mask))
    return values


def spread(values, axis):
    for mask in masks(axis):
        values = jnp.concatenate([values, swap(values, axis, mask)], axis=0)
    return values


def add_low(left, right):
    return (left.astype(F32) + right.astype(F32)).astype(BF)


def line_gather(values):
    return jnp.concatenate([values] + [swap(values, "z", k) for k in (1, 2, 3)], axis=0)


def line_sum(partial):
    rows = partial.shape[0] // 4
    total = partial[:rows]
    for k in (1, 2, 3):
        total = total + swap(partial[k * rows : (k + 1) * rows].astype(BF), "z", k).astype(F32)
    return total


def line_place(pieces):
    here = lax.axis_index("z")
    held = jnp.zeros((len(pieces),) + pieces[0].shape, pieces[0].dtype)
    for k, piece in enumerate(pieces):
        held = lax.dynamic_update_index_in_dim(held, piece, here ^ k, 0)
    return held


def line_exchange(weight):
    rows, cols = weight.shape
    here, cut = lax.axis_index("z"), cols // 4
    pieces = []
    for k in range(4):
        piece = lax.dynamic_slice_in_dim(weight, (here ^ k) * cut, cut, 1)
        pieces.append(piece if k == 0 else swap(piece, "z", k))
    return line_place(pieces).reshape(4 * rows, cut)


def line_return(grad):
    rows, cols = grad.shape[0] // 4, grad.shape[1]
    here = lax.axis_index("z")
    held = jnp.zeros((rows, 4 * cols), F32)
    for k in range(4):
        piece = lax.dynamic_slice_in_dim(grad, (here ^ k) * rows, rows, 0)
        piece = piece if k == 0 else swap(piece, "z", k)
        held = lax.dynamic_update_slice_in_dim(held, piece.astype(F32), (here ^ k) * cols, 1)
    return held


def line_fold(grad):
    rows = grad.shape[0] // 4
    here = lax.axis_index("z")
    total = lax.dynamic_slice_in_dim(grad, here * rows, rows, 0).astype(F32)
    for k in (1, 2, 3):
        piece = lax.dynamic_slice_in_dim(grad, (here ^ k) * rows, rows, 0)
        total = total + swap(piece, "z", k).astype(F32)
    return total


def gather_rows(weight):
    line = line_place([weight] + [swap(weight, "z", k) for k in (1, 2, 3)])
    return spread(spread(line.reshape(-1, weight.shape[1]), "y"), "c")


def gather_cut(weight, x_first):
    if x_first:
        halves = [weight, swap(weight, "x", 1)]
        halves = [spread(half, "y") for half in halves]
    else:
        mine = spread(weight, "y")
        halves = [mine, swap(mine, "x", 1)]
    return [spread(half, "c") for half in halves]


def fold_cut(mine, other, x_first):
    if x_first:
        return fold(add_low(mine, swap(other, "x", 1)), "y")
    mine, other = fold(mine, "y"), fold(other, "y")
    return add_low(mine, swap(other, "x", 1))


def outer_low(left, right):
    cut = left.shape[1] // 2
    sent = outer_dot(left[:, cut:], right).astype(BF)
    return (outer_dot(left[:, :cut], right) + swap(sent, "c", 1).astype(F32)).astype(BF)


def gain_sum(parts):
    count, width = parts.shape
    z_size = lax.axis_size("z")
    blocks = lax.axis_size("c") * lax.axis_size("y") * z_size
    parts = parts.reshape(count, blocks, width // blocks).transpose(1, 0, 2)
    parts = parts + swap(parts, "x", 1)
    for axis in ("c", "y"):
        for mask in reversed(masks(axis)):
            rows = parts.shape[0] // 2
            parts = parts[:rows] + swap(parts[rows:], axis, mask)
    here = lax.axis_index("z")
    total = lax.dynamic_index_in_dim(parts, here, 0, keepdims=False)
    for k in (1, 2, 3):
        total = total + swap(
            lax.dynamic_index_in_dim(parts, here ^ k, 0, keepdims=False), "z", k
        )
    return total


def attend_forward(query_grid, key_rows, value_rows, allowed):
    total_rows = query_grid.shape[0]
    scaling = query_grid.shape[-1] ** (-0.5)
    scores = jnp.einsum("qgrd,kgd->grqk", query_grid, key_rows, preferred_element_type=F32)
    capped = SOFT_CAP * jnp.tanh(scores * scaling / SOFT_CAP)
    masked = jnp.where(allowed[None, None], capped, MASK_FILL)
    highest = jnp.max(masked, axis=-1, keepdims=True)
    weights = jnp.exp(masked - highest)
    totals = jnp.sum(weights, axis=-1, keepdims=True)
    probability = weights / totals
    prob_low = probability.astype(BF)
    out = jnp.einsum("grqk,kgd->qgrd", prob_low, value_rows, preferred_element_type=F32)
    return (out.astype(BF).reshape(total_rows, -1), capped, probability)


def attend_backward(query_grid, key_rows, value_rows, capped, probability, grad_grid):
    scaling = query_grid.shape[-1] ** (-0.5)
    prob_low = probability.astype(BF)
    grad_prob = jnp.einsum("qgrd,kgd->grqk", grad_grid, value_rows, preferred_element_type=F32)
    inner = jnp.sum(probability * grad_prob, axis=-1, keepdims=True)
    grad_cap = probability * (grad_prob - inner)
    tanh_value = capped / SOFT_CAP
    grad_score = (grad_cap * scaling * (1.0 - tanh_value * tanh_value)).astype(BF)
    query_grad = jnp.einsum("grqk,kgd->qgrd", grad_score, key_rows, preferred_element_type=F32)
    key_grad = jnp.einsum("grqk,qgrd->kgd", grad_score, query_grid, preferred_element_type=F32)
    value_grad = jnp.einsum("grqk,qgrd->kgd", prob_low, grad_grid, preferred_element_type=F32)
    return (query_grad, key_grad, value_grad)


def on_device(
    tokens,
    seg_lengths,
    parents,
    attn_gain,
    w_query,
    w_key,
    w_value,
    w_out,
    attn_post_gain,
    ffn_gain,
    w_gate,
    w_up,
    w_down,
    ffn_post_gain,
    out_grad,
):
    local_rows, width = tokens.shape
    z_size, y_size, c_size = lax.axis_size("z"), lax.axis_size("y"), lax.axis_size("c")
    shard = width // (z_size * y_size * c_size)
    group_rows = local_rows * lax.axis_size("x")
    head_cols = w_query.shape[1]
    kv_cols = w_key.shape[1]
    heads_here = head_cols // HD
    kv_here = kv_cols // HD
    group_size = heads_here // kv_here

    def crossed(values, axis, at):
        here = lax.axis_index(axis)
        for mask in masks(axis):
            shape = values.shape
            halves = values.reshape(shape[:at] + (-1, 2, mask) + shape[at + 1 :])
            values = jnp.where((here & mask) != 0, jnp.flip(halves, at + 1), halves)
            values = values.reshape(shape)
        return values

    def inward(values):
        lead = values.shape[:-1]
        cut = values.reshape(lead + (z_size, y_size, c_size, shard))
        count = len(lead)
        order = tuple(range(count)) + (count + 2, count + 1, count, count + 3)
        cut = crossed(crossed(cut.transpose(order), "c", count), "y", count + 1)
        return cut.reshape(lead + (width,))

    def outward(values):
        lead = values.shape[:-1]
        cut = values.reshape(lead + (c_size, y_size, z_size, shard))
        count = len(lead)
        order = tuple(range(count)) + (count + 2, count + 1, count, count + 3)
        cut = crossed(crossed(cut, "c", count), "y", count + 1)
        return cut.transpose(order).reshape(lead + (width,))

    positions, allowed = tree_tables(seg_lengths[0], parents[0], group_rows)
    cosine_table, sine_table = rope_tables(positions, HD)
    attn_gain, attn_post_gain = inward(attn_gain), inward(attn_post_gain)
    ffn_gain, ffn_post_gain = inward(ffn_gain), inward(ffn_post_gain)
    state_in = inward(tokens).astype(F32)
    out_cotan = inward(out_grad).astype(F32)

    qkv_here = jnp.concatenate([w_query, w_key, w_value], axis=1)
    qkv_weight = gather_rows(qkv_here)
    out_weight = gather_rows(w_out.T)
    gate_weight = gather_cut(line_exchange(w_gate), True)
    up_weight = gather_cut(line_exchange(w_up), False)
    down_weight = gather_cut(line_exchange(w_down.T), False)

    inverse_one = lax.rsqrt(jnp.mean(state_in * state_in, axis=-1, keepdims=True) + NORM_EPS)
    unit_one = state_in * inverse_one
    normed_one = pair_gather((unit_one * attn_gain).astype(BF))
    qkv_proj = rows_dot(normed_one, qkv_weight)
    queries = rotate(
        qkv_proj[:, :head_cols].reshape(group_rows, heads_here, HD), cosine_table, sine_table
    ).astype(BF)
    key_rows = rotate(
        qkv_proj[:, head_cols : head_cols + kv_cols].reshape(group_rows, kv_here, HD),
        cosine_table,
        sine_table,
    ).astype(BF)
    value_rows = qkv_proj[:, head_cols + kv_cols :].astype(BF).reshape(group_rows, kv_here, HD)
    query_grid = queries.reshape(group_rows, kv_here, group_size, HD)
    attended, capped, probability = attend_forward(query_grid, key_rows, value_rows, allowed)
    branch = pair_sum(cols_dot(attended, out_weight))
    inverse_two = lax.rsqrt(jnp.mean(branch * branch, axis=-1, keepdims=True) + NORM_EPS)
    unit_two = branch * inverse_two
    hidden = state_in + unit_two * attn_post_gain
    inverse_three = lax.rsqrt(jnp.mean(hidden * hidden, axis=-1, keepdims=True) + NORM_EPS)
    unit_three = hidden * inverse_three

    normed_two = line_gather((unit_three * ffn_gain).astype(BF))
    acts, pulls, ffn_part = [], [], 0.0
    for half in range(2):
        gate = rows_dot(normed_two, gate_weight[half])
        up = rows_dot(normed_two, up_weight[half])
        act, pull = jax.vjp(gating, gate, up)
        acts.append(act.astype(BF))
        pulls.append(pull)
        ffn_part = ffn_part + cols_dot(acts[half], down_weight[half])
    ffn_out = line_sum(ffn_part)
    inverse_four = lax.rsqrt(jnp.mean(ffn_out * ffn_out, axis=-1, keepdims=True) + NORM_EPS)
    unit_four = ffn_out * inverse_four
    mixed = (hidden + unit_four * ffn_post_gain).astype(BF)
    gain_four = jnp.sum(out_cotan * unit_four, axis=0)
    d_ffn = line_gather(
        norm_back(out_cotan * ffn_post_gain, unit_four, inverse_four).astype(BF)
    )
    d_gates, d_ups, normed_part = [], [], 0.0
    for half in range(2):
        d_gate, d_up = pulls[half](rows_dot(d_ffn, down_weight[half]))
        d_gates.append(d_gate.astype(BF))
        d_ups.append(d_up.astype(BF))
        normed_part = normed_part + cols_dot(d_gates[half], gate_weight[half])
        normed_part = normed_part + cols_dot(d_ups[half], up_weight[half])
    d_normed_two = line_sum(normed_part)
    grad_down = line_return(fold_cut(*[outer_low(d_ffn, act) for act in acts], False))
    grad_up = line_return(fold_cut(*[outer_low(normed_two, d_up) for d_up in d_ups], True))
    grad_gate = line_return(fold_cut(*[outer_low(normed_two, d_gate) for d_gate in d_gates], True))

    gain_three = jnp.sum(d_normed_two * unit_three, axis=0)
    d_hidden = out_cotan + norm_back(d_normed_two * ffn_gain, unit_three, inverse_three)
    gain_two = jnp.sum(d_hidden * unit_two, axis=0)
    d_branch = pair_gather(
        norm_back(d_hidden * attn_post_gain, unit_two, inverse_two).astype(BF)
    )
    d_attended = rows_dot(d_branch, out_weight).astype(BF)
    grad_grid = d_attended.reshape(group_rows, kv_here, group_size, HD)
    query_grad, key_grad, value_grad = attend_backward(
        query_grid, key_rows, value_rows, capped, probability, grad_grid
    )
    query_back = rotate(
        query_grad.reshape(group_rows, heads_here, HD), cosine_table, -sine_table
    ).astype(BF)
    key_back = rotate(key_grad, cosine_table, -sine_table).astype(BF)
    d_qkv = jnp.concatenate(
        [
            query_back.reshape(group_rows, head_cols),
            key_back.reshape(group_rows, kv_cols),
            value_grad.astype(BF).reshape(group_rows, kv_cols),
        ],
        axis=1,
    )
    d_normed_one = pair_sum(cols_dot(d_qkv, qkv_weight))
    gain_one = jnp.sum(d_normed_one * unit_one, axis=0)
    grad_tokens = d_hidden + norm_back(d_normed_one * attn_gain, unit_one, inverse_one)
    grad_qkv = line_fold(fold(outer_low(normed_one, d_qkv), "y"))
    grad_out = line_fold(fold(outer_low(d_branch, attended), "y"))
    gains = gain_sum(jnp.stack([gain_one, gain_two, gain_three, gain_four], axis=0))
    key_from, value_from = head_cols, head_cols + kv_cols
    return (
        outward(mixed),
        outward(grad_tokens),
        gains[0],
        grad_qkv[:, :key_from],
        grad_qkv[:, key_from:value_from],
        grad_qkv[:, value_from:],
        grad_out.T,
        gains[1],
        gains[2],
        grad_gate,
        grad_up,
        grad_down.T,
        gains[3],
    )


def solution(mesh):
    count, pair = mesh.devices.shape
    grid = Mesh(mesh.devices.reshape(4, count // 8, 2, pair), ("z", "y", "c", "x"))
    rows = ("z", "y", "c")
    return jax.shard_map(
        on_device,
        mesh=grid,
        in_specs=(
            P(rows + ("x",), None),
            P(rows, None),
            P(rows, None),
            P(),
            P(rows, "x"),
            P(rows, "x"),
            P(rows, "x"),
            P("x", rows),
            P(),
            P(),
            P(rows, "x"),
            P(rows, "x"),
            P("x", rows),
            P(),
            P(rows + ("x",), None),
        ),
        out_specs=(
            P(rows + ("x",), None),
            P(rows + ("x",), None),
            P(rows),
            P(rows, "x"),
            P(rows, "x"),
            P(rows, "x"),
            P("x", rows),
            P(rows),
            P(rows),
            P(rows, "x"),
            P(rows, "x"),
            P("x", rows),
            P(rows),
        ),
        check_vma=False,
    )
```

```python
import jax
import jax.numpy as jnp
from jax import lax
from jax.sharding import Mesh
from jax.sharding import PartitionSpec as P

HD = 256
NORM_EPS = 1e-06
SOFT_CAP = 50.0
ROPE_BASE = 10000.0
MASK_FILL = -1e30
BF = jnp.bfloat16
F32 = jnp.float32


def tree_tables(lengths_row, parents_row, row_total):
    seg_count = lengths_row.shape[0]
    seg_index = jnp.arange(seg_count, dtype=jnp.int32)
    ancestor = (seg_index[:, None] == seg_index[None, :]) | (
        parents_row[:, None] == seg_index[None, :]
    )
    for repeat in range(seg_count.bit_length()):
        ancestor = jnp.any(ancestor[:, :, None] & ancestor[None, :, :], axis=1)
    seg_ends = jnp.cumsum(lengths_row)
    seg_starts = seg_ends - lengths_row
    token_index = jnp.arange(row_total, dtype=jnp.int32)
    segment = jnp.sum((token_index[:, None] >= seg_ends[None, :]).astype(jnp.int32), axis=1)
    strict = ancestor & (seg_index[:, None] != seg_index[None, :])
    offsets = jnp.sum(jnp.where(strict, lengths_row[None, :], 0), axis=1)
    one_hot = segment[:, None] == seg_index[None, :]
    positions = (
        jnp.sum(jnp.where(one_hot, (offsets - seg_starts)[None, :], 0), axis=1) + token_index
    )
    reached = jnp.any(one_hot[:, :, None] & ancestor[None, :, :], axis=1)
    allowed = jnp.any(reached[:, None, :] & one_hot[None, :, :], axis=2) & (
        token_index[None, :] <= token_index[:, None]
    )
    return (positions, allowed)


def rope_tables(positions, width):
    half_width = width // 2
    frequency = ROPE_BASE ** (-2.0 * jnp.arange(half_width, dtype=F32) / width)
    angles = positions.astype(F32)[:, None] * frequency[None, :]
    return (jnp.cos(angles), jnp.sin(angles))


def rotate(values, cosine_table, sine_table):
    half_width = values.shape[-1] // 2
    front_half = values[..., :half_width]
    back_half = values[..., half_width:]
    cos_heads = cosine_table[:, None, :]
    sin_heads = sine_table[:, None, :]
    return jnp.concatenate(
        [
            front_half * cos_heads - back_half * sin_heads,
            back_half * cos_heads + front_half * sin_heads,
        ],
        axis=-1,
    )


def norm_back(grad_unit, unit, inverse):
    return inverse * (grad_unit - unit * jnp.mean(grad_unit * unit, axis=-1, keepdims=True))


def gating(gate_proj, upward):
    return jax.nn.gelu(gate_proj, approximate=True) * upward


def swap(values, axis, mask):
    size = lax.axis_size(axis)
    return lax.ppermute(values, axis, [(i, i ^ mask) for i in range(size)])


def rows_dot(left, right):
    return lax.dot_general(left, right, (((1,), (0,)), ((), ())), preferred_element_type=F32)


def cols_dot(left, right):
    return lax.dot_general(left, right, (((1,), (1,)), ((), ())), preferred_element_type=F32)


def outer_dot(left, right):
    return lax.dot_general(left, right, (((0,), (0,)), ((), ())), preferred_element_type=F32)


def meet(*values):
    return lax.optimization_barrier(values)


def pair_gather(values, other):
    mine = lax.axis_index("x")
    first = jnp.where(mine == 0, values, other)
    second = jnp.where(mine == 0, other, values)
    return jnp.concatenate([first, second], axis=0)


def pair_parts(partial):
    rows = partial.shape[0] // 2
    mine = lax.axis_index("x")
    sent = lax.dynamic_slice_in_dim(partial, (1 - mine) * rows, rows, 0).astype(BF)
    return sent, lax.dynamic_slice_in_dim(partial, mine * rows, rows, 0)


def pair_sum(partial):
    sent, kept = pair_parts(partial)
    return kept + swap(sent, "x", 1).astype(F32)


def rows_sum(values, axis):
    size = lax.axis_size(axis)
    if size != 2:
        return lax.psum_scatter(values, axis, scatter_dimension=0, tiled=True)
    rows, mine = values.shape[0] // 2, lax.axis_index(axis)
    sent = lax.dynamic_slice_in_dim(values, (1 - mine) * rows, rows, 0)
    return add_low(lax.dynamic_slice_in_dim(values, mine * rows, rows, 0), swap(sent, axis, 1))


def placed(rows, *pieces):
    held = jnp.zeros((rows,) + pieces[0][1].shape[1:], pieces[0][1].dtype)
    for offset, piece in pieces:
        held = lax.dynamic_update_slice_in_dim(held, piece, offset, 0)
    return held


def add_low(left, right):
    return (left.astype(F32) + right.astype(F32)).astype(BF)


def line_gather(values):
    return jnp.concatenate([values] + [swap(values, "z", k) for k in (1, 2, 3)], axis=0)


def line_sum(partial):
    rows = partial.shape[0] // 4
    total = partial[:rows]
    for k in (1, 2, 3):
        total = total + swap(partial[k * rows : (k + 1) * rows].astype(BF), "z", k).astype(F32)
    return total


def line_place(pieces):
    here, rows = lax.axis_index("z"), pieces[0].shape[0]
    return placed(len(pieces) * rows, *[((here ^ k) * rows, p) for k, p in enumerate(pieces)])


def line_cuts(weight):
    here, cut = lax.axis_index("z"), weight.shape[1] // 4
    return [lax.dynamic_slice_in_dim(weight, (here ^ k) * cut, cut, 1) for k in range(4)]


def line_swaps(cuts):
    return [cuts[0]] + [swap(cuts[k], "z", k) for k in (1, 2, 3)]


def line_return(grad):
    rows, cols = grad.shape[0] // 4, grad.shape[1]
    here = lax.axis_index("z")
    held = jnp.zeros((rows, 4 * cols), F32)
    for k in range(4):
        piece = lax.dynamic_slice_in_dim(grad, (here ^ k) * rows, rows, 0)
        piece = piece if k == 0 else swap(piece, "z", k)
        held = lax.dynamic_update_slice_in_dim(held, piece.astype(F32), (here ^ k) * cols, 1)
    return held


def line_fold(grad):
    rows = grad.shape[0] // 4
    here = lax.axis_index("z")
    total = lax.dynamic_slice_in_dim(grad, here * rows, rows, 0).astype(F32)
    for k in (1, 2, 3):
        piece = lax.dynamic_slice_in_dim(grad, (here ^ k) * rows, rows, 0)
        total = total + swap(piece, "z", k).astype(F32)
    return total


def both_cores(rows):
    return pair_rows(rows, swap(rows, "c", 1), "c")


def pair_rows(mine, other, axis):
    rows, here = mine.shape[0], lax.axis_index(axis)
    return placed(2 * rows, (here * rows, mine), ((1 - here) * rows, other))


class Cut:
    def __init__(self, own):
        self.own, self.pairs = own, lax.axis_size("y") == 2

    def first(self):
        self.via_x = swap(self.own, "x", 1)
        if self.pairs:
            self.via_y = swap(self.own, "y", 1)
            return [self.via_x, self.via_y]
        return [self.via_x]

    def take(self, values):
        self.via_x = values[0]
        if self.pairs:
            self.via_y = values[1]

    def second(self, over_x):
        if not self.pairs:
            return []
        self.across = []
        if over_x:
            self.across.append(swap(self.via_y[:over_x], "x", 1))
        if over_x < self.own.shape[0]:
            self.across.append(swap(self.via_x[over_x:], "y", 1))
        return list(self.across)

    def take_second(self, values):
        self.across = list(values)

    def whole(self):
        if not self.pairs:
            halves = [lax.all_gather(v, "y", axis=0, tiled=True) for v in (self.own, self.via_x)]
            return [both_cores(half) for half in halves]
        rows, here = self.own.shape[0], lax.axis_index("y")
        mine = pair_rows(self.own, self.via_y, "y")
        pieces, at = [(here * rows, self.via_x)], (1 - here) * rows
        for piece in self.across:
            pieces.append((at, piece))
            at = at + piece.shape[0]
        return [both_cores(mine), both_cores(placed(2 * rows, *pieces))]


class Fold:
    def __init__(self, mine, other, over_x):
        self.mine, self.other, self.over_x = mine, other, over_x
        self.pairs = lax.axis_size("y") == 2

    def halves(self, values):
        rows, here = values.shape[0] // 2, lax.axis_index("y")
        return (
            lax.dynamic_slice_in_dim(values, here * rows, rows, 0),
            lax.dynamic_slice_in_dim(values, (1 - here) * rows, rows, 0),
        )

    def first(self):
        if not self.pairs:
            self.mine = rows_sum(self.mine, "y")
            self.other = rows_sum(self.other, "y")
            return []
        self.mine, self.mine_far = self.halves(self.mine)
        self.other, self.other_far = self.halves(self.other)
        self.got = []
        if self.over_x:
            self.got.append(swap(self.other_far[: self.over_x], "x", 1))
        if self.over_x < self.mine.shape[0]:
            self.got.append(swap(self.other_far[self.over_x :], "y", 1))
        return list(self.got)

    def take(self, values):
        self.got = list(values)

    def second(self):
        if self.pairs:
            got, at = list(self.got), self.over_x
            if at:
                piece = add_low(self.mine_far[:at], got.pop(0))
                self.mine_far = (
                    jnp.concatenate([piece, self.mine_far[at:]], axis=0) if got else piece
                )
            if got:
                piece = add_low(self.other[at:], got[0])
                self.other = jnp.concatenate([self.other[:at], piece], axis=0) if at else piece
            self.last = [swap(self.other, "x", 1), swap(self.mine_far, "y", 1)]
        else:
            self.last = [swap(self.other, "x", 1)]
        return list(self.last)

    def take_second(self, values):
        self.last = list(values)

    def whole(self):
        total = self.mine.astype(F32)
        for piece in self.last:
            total = total + piece.astype(F32)
        return total.astype(BF)


def outer_low(left, right):
    cut = left.shape[1] // 2
    here = lax.axis_index("c")
    theirs = lax.dynamic_slice_in_dim(left, (1 - here) * cut, cut, 1)
    mine = lax.dynamic_slice_in_dim(left, here * cut, cut, 1)
    sent = outer_dot(theirs, right).astype(BF)
    return (outer_dot(mine, right) + swap(sent, "c", 1).astype(F32)).astype(BF)


def gain_sum(parts):
    count, width = parts.shape
    blocks = lax.axis_size("c") * lax.axis_size("y") * lax.axis_size("z")
    parts = parts.reshape(count, blocks, width // blocks).transpose(1, 0, 2)
    parts = parts + swap(parts, "x", 1)
    here, rows = lax.axis_index("c"), blocks // 2
    parts = lax.dynamic_slice_in_dim(parts, here * rows, rows, 0) + swap(
        lax.dynamic_slice_in_dim(parts, (1 - here) * rows, rows, 0), "c", 1
    )
    if lax.axis_size("y") == 2:
        here, rows = lax.axis_index("y"), blocks // 4
        parts = lax.dynamic_slice_in_dim(parts, here * rows, rows, 0) + swap(
            lax.dynamic_slice_in_dim(parts, (1 - here) * rows, rows, 0), "y", 1
        )
    else:
        parts = lax.psum_scatter(parts, "y", scatter_dimension=0, tiled=True)
    here = lax.axis_index("z")
    total = lax.dynamic_index_in_dim(parts, here, 0, keepdims=False)
    for k in (1, 2, 3):
        total = total + swap(
            lax.dynamic_index_in_dim(parts, here ^ k, 0, keepdims=False), "z", k
        )
    return total


def attend_weights(query_grid, key_rows, allowed):
    scaling = query_grid.shape[-1] ** (-0.5)
    scores = jnp.einsum("qgrd,kgd->grqk", query_grid, key_rows, preferred_element_type=F32)
    capped = SOFT_CAP * jnp.tanh(scores * scaling / SOFT_CAP)
    masked = jnp.where(allowed[None, None], capped, MASK_FILL)
    highest = jnp.max(masked, axis=-1, keepdims=True)
    weights = jnp.exp(masked - highest)
    return (capped, weights / jnp.sum(weights, axis=-1, keepdims=True))


def attend_values(probability, value_rows):
    out = jnp.einsum(
        "grqk,kgd->qgrd", probability.astype(BF), value_rows, preferred_element_type=F32
    )
    return out.astype(BF).reshape(out.shape[0], -1)


def attend_backward(query_grid, key_rows, value_rows, capped, probability, grad_grid):
    scaling = query_grid.shape[-1] ** (-0.5)
    prob_low = probability.astype(BF)
    grad_prob = jnp.einsum("qgrd,kgd->grqk", grad_grid, value_rows, preferred_element_type=F32)
    inner = jnp.sum(probability * grad_prob, axis=-1, keepdims=True)
    grad_cap = probability * (grad_prob - inner)
    tanh_value = capped / SOFT_CAP
    grad_score = (grad_cap * scaling * (1.0 - tanh_value * tanh_value)).astype(BF)
    query_grad = jnp.einsum("grqk,kgd->qgrd", grad_score, key_rows, preferred_element_type=F32)
    key_grad = jnp.einsum("grqk,qgrd->kgd", grad_score, query_grid, preferred_element_type=F32)
    value_grad = jnp.einsum("grqk,qgrd->kgd", prob_low, grad_grid, preferred_element_type=F32)
    return (query_grad, key_grad, value_grad)


def attend_forward(query_grid, key_rows, value_rows, allowed):
    total_rows = query_grid.shape[0]
    scaling = query_grid.shape[-1] ** (-0.5)
    scores = jnp.einsum("qgrd,kgd->grqk", query_grid, key_rows, preferred_element_type=F32)
    capped = SOFT_CAP * jnp.tanh(scores * scaling / SOFT_CAP)
    masked = jnp.where(allowed[None, None], capped, MASK_FILL)
    highest = jnp.max(masked, axis=-1, keepdims=True)
    weights = jnp.exp(masked - highest)
    totals = jnp.sum(weights, axis=-1, keepdims=True)
    probability = weights / totals
    prob_low = probability.astype(BF)
    out = jnp.einsum("grqk,kgd->qgrd", prob_low, value_rows, preferred_element_type=F32)
    return (out.astype(BF).reshape(total_rows, -1), capped, probability)


def attend_backward(query_grid, key_rows, value_rows, capped, probability, grad_grid):
    scaling = query_grid.shape[-1] ** (-0.5)
    prob_low = probability.astype(BF)
    grad_prob = jnp.einsum("qgrd,kgd->grqk", grad_grid, value_rows, preferred_element_type=F32)
    inner = jnp.sum(probability * grad_prob, axis=-1, keepdims=True)
    grad_cap = probability * (grad_prob - inner)
    tanh_value = capped / SOFT_CAP
    grad_score = (grad_cap * scaling * (1.0 - tanh_value * tanh_value)).astype(BF)
    query_grad = jnp.einsum("grqk,kgd->qgrd", grad_score, key_rows, preferred_element_type=F32)
    key_grad = jnp.einsum("grqk,qgrd->kgd", grad_score, query_grid, preferred_element_type=F32)
    value_grad = jnp.einsum("grqk,qgrd->kgd", prob_low, grad_grid, preferred_element_type=F32)
    return (query_grad, key_grad, value_grad)


def on_device(
    tokens,
    seg_lengths,
    parents,
    attn_gain,
    w_query,
    w_key,
    w_value,
    w_out,
    attn_post_gain,
    ffn_gain,
    w_gate,
    w_up,
    w_down,
    ffn_post_gain,
    out_grad,
):
    local_rows, width = tokens.shape
    z_size, y_size, c_size = lax.axis_size("z"), lax.axis_size("y"), lax.axis_size("c")
    shard = width // (z_size * y_size * c_size)
    group_rows = local_rows * lax.axis_size("x")
    head_cols = w_query.shape[1]
    kv_cols = w_key.shape[1]
    heads_here = head_cols // HD
    kv_here = kv_cols // HD
    group_size = heads_here // kv_here

    def inward(values):
        lead = values.shape[:-1]
        cut = values.reshape(lead + (z_size, y_size, c_size, shard))
        count = len(lead)
        order = tuple(range(count)) + (count + 2, count + 1, count, count + 3)
        return cut.transpose(order).reshape(lead + (width,))

    def outward(values):
        lead = values.shape[:-1]
        cut = values.reshape(lead + (c_size, y_size, z_size, shard))
        count = len(lead)
        order = tuple(range(count)) + (count + 2, count + 1, count, count + 3)
        return cut.transpose(order).reshape(lead + (width,))

    row_axes = ("c", "y", "z")
    positions, allowed = tree_tables(seg_lengths[0], parents[0], group_rows)
    cosine_table, sine_table = rope_tables(positions, HD)
    attn_gain, attn_post_gain = inward(attn_gain), inward(attn_post_gain)
    ffn_gain, ffn_post_gain = inward(ffn_gain), inward(ffn_post_gain)
    state_in = inward(tokens).astype(F32)
    out_cotan = inward(out_grad).astype(F32)

    qkv_here = jnp.concatenate([w_query, w_key, w_value], axis=1)
    inverse_one = lax.rsqrt(jnp.mean(state_in * state_in, axis=-1, keepdims=True) + NORM_EPS)
    unit_one = state_in * inverse_one
    normed_here = (unit_one * attn_gain).astype(BF)

    qkv_weight = lax.all_gather(qkv_here, row_axes, axis=0, tiled=True)
    out_weight = lax.all_gather(w_out.T, row_axes, axis=0, tiled=True)

    gate_z, normed_other = line_swaps(line_cuts(w_gate)), swap(normed_here, "x", 1)
    met = meet(normed_other, *gate_z, *line_cuts(w_up), *line_cuts(w_down.T))
    normed_other, gate_z, up_cuts, down_cuts = met[0], met[1:5], met[5:9], met[9:]

    normed_one = pair_gather(normed_here, normed_other)
    gate = Cut(line_place(gate_z))
    gate_got = gate.first()
    up_z = line_swaps(up_cuts)
    met = meet(normed_one, *up_z, *down_cuts, *gate_got)
    normed_one, up_z, down_cuts = met[0], met[1:5], met[5:9]
    gate.take(met[9:])

    up = Cut(line_place(up_z))
    up_got = up.first()
    down_z = line_swaps(down_cuts)
    met = meet(normed_one, qkv_weight, *down_z, *up_got)
    normed_one, qkv_weight, down_z = met[0], met[1], met[2:6]
    up.take(met[6:])

    down = Cut(line_place(down_z))
    gate_got, up_got = gate.second(2 * shard), up.second(2 * shard)
    qkv_proj = rows_dot(normed_one, qkv_weight)
    queries = rotate(
        qkv_proj[:, :head_cols].reshape(group_rows, heads_here, HD), cosine_table, sine_table
    ).astype(BF)
    key_rows = rotate(
        qkv_proj[:, head_cols : head_cols + kv_cols].reshape(group_rows, kv_here, HD),
        cosine_table,
        sine_table,
    ).astype(BF)
    value_rows = qkv_proj[:, head_cols + kv_cols :].astype(BF).reshape(group_rows, kv_here, HD)
    query_grid = queries.reshape(group_rows, kv_here, group_size, HD)
    capped, probability = attend_weights(query_grid, key_rows, allowed)
    attended = attend_values(probability, value_rows)
    met = meet(attended, down.own, *gate_got, *up_got)
    attended, down.own, met = met[0], met[1], met[2:]
    gate.take_second(met[: len(gate_got)])
    up.take_second(met[len(gate_got) :])

    down_got = down.first()
    branch_sent, branch_kept = pair_parts(cols_dot(attended, out_weight))
    met = meet(branch_kept, swap(branch_sent, "x", 1), *down_got)
    branch = met[0] + met[1].astype(F32)
    down.take(met[2:])
    inverse_two = lax.rsqrt(jnp.mean(branch * branch, axis=-1, keepdims=True) + NORM_EPS)
    unit_two = branch * inverse_two
    hidden = state_in + unit_two * attn_post_gain
    inverse_three = lax.rsqrt(jnp.mean(hidden * hidden, axis=-1, keepdims=True) + NORM_EPS)
    unit_three = hidden * inverse_three

    normed_two = (unit_three * ffn_gain).astype(BF)

    normed_two = line_gather(normed_two)
    down.second(2 * shard)
    gate_weight, up_weight, down_weight = gate.whole(), up.whole(), down.whole()
    acts, pulls, ffn_part = [], [], 0.0
    for half in range(2):
        gate = rows_dot(normed_two, gate_weight[half])
        up = rows_dot(normed_two, up_weight[half])
        act, pull = jax.vjp(gating, gate, up)
        acts.append(act.astype(BF))
        pulls.append(pull)
        ffn_part = ffn_part + cols_dot(acts[half], down_weight[half])
    ffn_out = line_sum(ffn_part)
    inverse_four = lax.rsqrt(jnp.mean(ffn_out * ffn_out, axis=-1, keepdims=True) + NORM_EPS)
    unit_four = ffn_out * inverse_four
    mixed = (hidden + unit_four * ffn_post_gain).astype(BF)
    gain_four = jnp.sum(out_cotan * unit_four, axis=0)
    d_ffn = line_gather(
        norm_back(out_cotan * ffn_post_gain, unit_four, inverse_four).astype(BF)
    )
    d_gates, d_ups, normed_part = [], [], 0.0
    for half in range(2):
        d_gate, d_up = pulls[half](rows_dot(d_ffn, down_weight[half]))
        d_gates.append(d_gate.astype(BF))
        d_ups.append(d_up.astype(BF))
        normed_part = normed_part + cols_dot(d_gates[half], gate_weight[half])
        normed_part = normed_part + cols_dot(d_ups[half], up_weight[half])
    d_normed_two = line_sum(normed_part)
    tails = [
        Fold(outer_low(d_ffn, acts[0]), outer_low(d_ffn, acts[1]), 2 * shard),
        Fold(outer_low(normed_two, d_ups[0]), outer_low(normed_two, d_ups[1]), 2 * shard),
        Fold(outer_low(normed_two, d_gates[0]), outer_low(normed_two, d_gates[1]), 4 * shard),
    ]
    grads, earlier = [], []
    for tail in tails:
        if earlier:
            tail.mine, tail.other, *_ = meet(tail.mine, tail.other, *earlier)
        met = tail.first()
        tail.take(meet(*met) if met else [])
        earlier = tail.second()
        tail.take_second(earlier)
        grads.append(line_return(tail.whole()))
    grad_down, grad_up, grad_gate = grads

    gain_three = jnp.sum(d_normed_two * unit_three, axis=0)
    d_hidden = out_cotan + norm_back(d_normed_two * ffn_gain, unit_three, inverse_three)
    gain_two = jnp.sum(d_hidden * unit_two, axis=0)
    d_branch = norm_back(d_hidden * attn_post_gain, unit_two, inverse_two).astype(BF)
    d_branch = pair_gather(d_branch, swap(d_branch, "x", 1))
    d_attended = rows_dot(d_branch, out_weight).astype(BF)
    grad_grid = d_attended.reshape(group_rows, kv_here, group_size, HD)
    query_grad, key_grad, value_grad = attend_backward(
        query_grid, key_rows, value_rows, capped, probability, grad_grid
    )
    query_back = rotate(
        query_grad.reshape(group_rows, heads_here, HD), cosine_table, -sine_table
    ).astype(BF)
    key_back = rotate(key_grad, cosine_table, -sine_table).astype(BF)
    d_qkv = jnp.concatenate(
        [
            query_back.reshape(group_rows, head_cols),
            key_back.reshape(group_rows, kv_cols),
            value_grad.astype(BF).reshape(group_rows, kv_cols),
        ],
        axis=1,
    )
    d_normed_one = pair_sum(cols_dot(d_qkv, qkv_weight))
    gain_one = jnp.sum(d_normed_one * unit_one, axis=0)
    grad_tokens = d_hidden + norm_back(d_normed_one * attn_gain, unit_one, inverse_one)
    grad_qkv = line_fold(rows_sum(outer_low(normed_one, d_qkv), "y"))
    grad_out = line_fold(rows_sum(outer_low(d_branch, attended), "y"))
    gains = gain_sum(jnp.stack([gain_one, gain_two, gain_three, gain_four], axis=0))
    key_from, value_from = head_cols, head_cols + kv_cols
    return (
        outward(mixed),
        outward(grad_tokens),
        gains[0],
        grad_qkv[:, :key_from],
        grad_qkv[:, key_from:value_from],
        grad_qkv[:, value_from:],
        grad_out.T,
        gains[1],
        gains[2],
        grad_gate,
        grad_up,
        grad_down.T,
        gains[3],
    )


def solution(mesh):
    count, pair = mesh.devices.shape
    grid = Mesh(mesh.devices.reshape(4, count // 8, 2, pair), ("z", "y", "c", "x"))
    rows = ("z", "y", "c")
    return jax.shard_map(
        on_device,
        mesh=grid,
        in_specs=(
            P(rows + ("x",), None),
            P(rows, None),
            P(rows, None),
            P(),
            P(rows, "x"),
            P(rows, "x"),
            P(rows, "x"),
            P("x", rows),
            P(),
            P(),
            P(rows, "x"),
            P(rows, "x"),
            P("x", rows),
            P(),
            P(rows + ("x",), None),
        ),
        out_specs=(
            P(rows + ("x",), None),
            P(rows + ("x",), None),
            P(rows),
            P(rows, "x"),
            P(rows, "x"),
            P(rows, "x"),
            P("x", rows),
            P(rows),
            P(rows),
            P(rows, "x"),
            P(rows, "x"),
            P("x", rows),
            P(rows),
        ),
        check_vma=False,
    )
```

```python
import functools

import jax
import jax.numpy as jnp
from jax import lax
from jax.experimental import pallas as pl
from jax.experimental.pallas import tpu as pltpu
from jax.sharding import Mesh
from jax.sharding import PartitionSpec as P

HD = 256
NORM_EPS = 1e-06
SOFT_CAP = 50.0
ROPE_BASE = 10000.0
MASK_FILL = -1e30
BF = jnp.bfloat16
F32 = jnp.float32


def tree_tables(lengths_row, parents_row, row_total):
    seg_count = lengths_row.shape[0]
    seg_index = jnp.arange(seg_count, dtype=jnp.int32)
    ancestor = (seg_index[:, None] == seg_index[None, :]) | (
        parents_row[:, None] == seg_index[None, :]
    )
    for repeat in range(seg_count.bit_length()):
        ancestor = jnp.any(ancestor[:, :, None] & ancestor[None, :, :], axis=1)
    seg_ends = jnp.cumsum(lengths_row)
    seg_starts = seg_ends - lengths_row
    token_index = jnp.arange(row_total, dtype=jnp.int32)
    segment = jnp.sum((token_index[:, None] >= seg_ends[None, :]).astype(jnp.int32), axis=1)
    strict = ancestor & (seg_index[:, None] != seg_index[None, :])
    offsets = jnp.sum(jnp.where(strict, lengths_row[None, :], 0), axis=1)
    one_hot = segment[:, None] == seg_index[None, :]
    positions = (
        jnp.sum(jnp.where(one_hot, (offsets - seg_starts)[None, :], 0), axis=1) + token_index
    )
    reached = jnp.any(one_hot[:, :, None] & ancestor[None, :, :], axis=1)
    allowed = jnp.any(reached[:, None, :] & one_hot[None, :, :], axis=2) & (
        token_index[None, :] <= token_index[:, None]
    )
    return (positions, allowed)


def rope_tables(positions, width):
    half_width = width // 2
    frequency = ROPE_BASE ** (-2.0 * jnp.arange(half_width, dtype=F32) / width)
    angles = positions.astype(F32)[:, None] * frequency[None, :]
    return (jnp.cos(angles), jnp.sin(angles))


def norm_back(grad_unit, unit, inverse):
    return inverse * (grad_unit - unit * jnp.mean(grad_unit * unit, axis=-1, keepdims=True))


def gelu_parts(values):
    scale = (2.0 / jnp.pi) ** 0.5
    square = values * values
    bent = jnp.tanh(scale * (values + 0.044715 * values * square))
    half = 0.5 * (1.0 + bent)
    slope = half + 0.5 * values * (1.0 - bent * bent) * scale * (1.0 + 3 * 0.044715 * square)
    return values * half, slope


def tile_dot(left, right):
    return jnp.dot(left, right, preferred_element_type=F32)


def tile_dot_cols(left, right):
    return lax.dot_general(left, right, (((1,), (1,)), ((), ())), preferred_element_type=F32)


def spill(total, outs):
    rows = outs[0].shape[0]
    for k, out in enumerate(outs):
        out[...] = total[k * rows : (k + 1) * rows, :].astype(out.dtype)


class Weight:
    def __init__(self, *arrays):
        self.arrays, self.whole = arrays, len(arrays) == 1
        self.rows = arrays[0].shape[-2]

    def specs(self, tile):
        if not self.whole:
            return [pl.BlockSpec((self.rows, tile), lambda i, ids: (0, i))] * 2
        count = self.arrays[0].shape[-1] // tile
        return [
            pl.BlockSpec(
                (None, None, self.rows, tile), lambda i, ids, c=c: (i // count, c, 0, i % count)
            )
            for c in range(2)
        ]

    def operands(self):
        return self.arrays * 2 if self.whole else self.arrays

    def columns(self, ids):
        first, second = (0, self.rows) if self.whole else (ids[2] * self.rows, (1 - ids[2]) * self.rows)
        if not self.whole:
            first, second = (pl.multiple_of(at, 128) for at in (first, second))
        return pl.ds(first, self.rows), pl.ds(second, self.rows)


def inner(values, refs, columns):
    return sum(tile_dot(values[:, at], ref[...]) for ref, at in zip(refs, columns))


def outer_add(total, tile, refs, columns, fresh):
    for ref, at in zip(refs, columns):
        part = tile_dot_cols(tile, ref[...])
        total[:, at] = jnp.where(fresh, part, total[:, at] + part)


def forward_kernel(columns, ids, x, *refs):
    gate_w, up_w, down_w, (act, gate, up), outs, total = (
        refs[:2], refs[2:4], refs[4:6], refs[6:9], refs[9:13], refs[13]
    )
    gate_at, up_at, down_at = (find(ids) for find in columns)
    gate_tile, up_tile = inner(x, gate_w, gate_at), inner(x, up_w, up_at)
    gate[...], up[...] = gate_tile, up_tile
    act_tile = (gelu_parts(gate_tile)[0] * up_tile).astype(BF)
    act[...] = act_tile
    outer_add(total, act_tile, down_w, down_at, pl.program_id(0) == 0)

    @pl.when(pl.program_id(0) == pl.num_programs(0) - 1)
    def _():
        spill(total, outs)


def backward_kernel(columns, ids, d, *refs):
    gate_w, up_w, down_w, (gate, up), (d_gate, d_up), outs, total = (
        refs[:2], refs[2:4], refs[4:6], refs[6:8], refs[8:10], refs[10:14], refs[14]
    )
    gate_at, up_at, down_at = (find(ids) for find in columns)
    d_act = inner(d, down_w, down_at)
    bent, slope = gelu_parts(gate[...])
    gate_tile = (d_act * up[...] * slope).astype(BF)
    up_tile = (d_act * bent).astype(BF)
    d_gate[...], d_up[...] = gate_tile, up_tile
    outer_add(total, gate_tile, gate_w, gate_at, pl.program_id(0) == 0)
    outer_add(total, up_tile, up_w, up_at, False)

    @pl.when(pl.program_id(0) == pl.num_programs(0) - 1)
    def _():
        spill(total, outs)


def ffn_call(kernel, ids, values, weights, kept, made, tile):
    tokens, width = values.shape
    hidden = 2 * weights[-1].arrays[0].shape[-1] if weights[-1].whole else weights[-1].arrays[0].shape[-1]
    slot = tokens // 4
    across = pl.BlockSpec((tokens, tile), lambda i, ids: (0, i))
    whole = pl.BlockSpec((slot, width), lambda i, ids: (0, 0))
    return pl.pallas_call(
        functools.partial(kernel, [weight.columns for weight in weights]),
        grid_spec=pltpu.PrefetchScalarGridSpec(
            num_scalar_prefetch=1,
            grid=(hidden // tile,),
            in_specs=[pl.BlockSpec((tokens, width), lambda i, ids: (0, 0))]
            + [spec for weight in weights for spec in weight.specs(tile)]
            + [across] * len(kept),
            out_specs=[across] * len(made) + [whole] * 4,
            scratch_shapes=[pltpu.VMEM((tokens, width), F32)],
        ),
        out_shape=[jax.ShapeDtypeStruct((tokens, hidden), kind) for kind in made]
        + [jax.ShapeDtypeStruct((slot, width), kind) for kind in (F32, BF, BF, BF)],
        compiler_params=pltpu.CompilerParams(
            dimension_semantics=("arbitrary",), vmem_limit_bytes=58 * 2**20
        ),
        cost_estimate=pl.CostEstimate(flops=0, bytes_accessed=0, transcendentals=0),
    )(ids, values, *[array for weight in weights for array in weight.operands()], *kept)


def swap(values, axis, mask):
    size = lax.axis_size(axis)
    return lax.ppermute(values, axis, [(i, i ^ mask) for i in range(size)])


def rows_dot(left, right):
    return lax.dot_general(left, right, (((1,), (0,)), ((), ())), preferred_element_type=F32)


def cols_dot(left, right):
    return lax.dot_general(left, right, (((1,), (1,)), ((), ())), preferred_element_type=F32)


def outer_dot(left, right):
    return lax.dot_general(left, right, (((0,), (0,)), ((), ())), preferred_element_type=F32)


def close(live):
    return lax.optimization_barrier(live)


def pair_gather(values, other):
    mine = lax.axis_index("x")
    first = jnp.where(mine == 0, values, other)
    second = jnp.where(mine == 0, other, values)
    return jnp.concatenate([first, second], axis=0)


def pair_parts(partial):
    rows = partial.shape[0] // 2
    mine = lax.axis_index("x")
    sent = lax.dynamic_slice_in_dim(partial, (1 - mine) * rows, rows, 0).astype(BF)
    return sent, lax.dynamic_slice_in_dim(partial, mine * rows, rows, 0)


def pair_sum(partial):
    sent, kept = pair_parts(partial)
    return kept + swap(sent, "x", 1).astype(F32)


def rows_sum(values, axis):
    size = lax.axis_size(axis)
    if size != 2:
        return lax.psum_scatter(values, axis, scatter_dimension=0, tiled=True)
    rows, mine = values.shape[0] // 2, lax.axis_index(axis)
    sent = lax.dynamic_slice_in_dim(values, (1 - mine) * rows, rows, 0)
    return add_low(lax.dynamic_slice_in_dim(values, mine * rows, rows, 0), swap(sent, axis, 1))


def placed(rows, *pieces):
    held = jnp.zeros((rows,) + pieces[0][1].shape[1:], pieces[0][1].dtype)
    for offset, piece in pieces:
        held = lax.dynamic_update_slice_in_dim(held, piece, offset, 0)
    return held


def add_low(left, right):
    return (left.astype(F32) + right.astype(F32)).astype(BF)


def line_gather(values):
    return jnp.concatenate([values] + [swap(values, "z", k) for k in (1, 2, 3)], axis=0)


def line_parts(partial):
    rows = partial.shape[0] // 4
    parts = [partial[k * rows : (k + 1) * rows] for k in range(4)]
    return [parts[0]] + [part.astype(BF) for part in parts[1:]]


def line_place(pieces):
    here, (rows, cols) = lax.axis_index("z"), pieces[0].shape
    if rows % 16 == 0:
        return assemble(
            (len(pieces) * rows, cols), (rows, cols), [(here ^ k, 0, p) for k, p in enumerate(pieces)]
        )
    return placed(len(pieces) * rows, *[((here ^ k) * rows, p) for k, p in enumerate(pieces)])


def line_cuts(weight):
    here, cut = lax.axis_index("z"), weight.shape[1] // 4
    return [lax.dynamic_slice_in_dim(weight, (here ^ k) * cut, cut, 1) for k in range(4)]


def line_swaps(cuts):
    return [cuts[0]] + [swap(cuts[k], "z", k) for k in (1, 2, 3)]


def line_chunks(grad):
    rows, here = grad.shape[0] // 4, lax.axis_index("z")
    return [lax.dynamic_slice_in_dim(grad, (here ^ k) * rows, rows, 0) for k in range(4)]


def line_columns(pieces):
    here, (rows, cols) = lax.axis_index("z"), pieces[0].shape
    spots = [(0, here ^ k, piece) for k, piece in enumerate(pieces)]
    return assemble((rows, 4 * cols), (rows, cols), spots, F32)


def line_total(pieces):
    total = pieces[0].astype(F32)
    for piece in pieces[1:]:
        total = total + piece.astype(F32)
    return total


def y_chunks(grad):
    rows, y, z = grad.shape[0] // 8, lax.axis_index("y"), lax.axis_index("z")
    return [
        tuple(
            lax.dynamic_slice_in_dim(grad, (4 * side + (z ^ k)) * rows, rows, 0)
            for side in (y, 1 - y)
        )
        for k in range(4)
    ]


def pair_rows(mine, other, axis):
    rows, here = mine.shape[0], lax.axis_index(axis)
    return placed(2 * rows, (here * rows, mine), ((1 - here) * rows, other))


def pair_halves(values, axis):
    rows, here = values.shape[0] // 2, lax.axis_index(axis)
    return (
        lax.dynamic_slice_in_dim(values, here * rows, rows, 0),
        lax.dynamic_slice_in_dim(values, (1 - here) * rows, rows, 0),
    )


def cut_first(own):
    got = {"own": own, "x": swap(own, "x", 1)}
    if lax.axis_size("y") == 2:
        got["y"] = swap(own, "y", 1)
    return got


def cut_over_x(got):
    rows = got["own"].shape[0] // 2
    return {"over_x": swap(got["y"][:rows], "x", 1)} if "y" in got else {}


def cut_over_y(got):
    rows = got["own"].shape[0] // 2
    return {"over_y": swap(got["x"][rows:], "y", 1)} if "y" in got else {}


def cut_half(got):
    own = got["own"]
    rows, cols = own.shape
    if "y" not in got:
        both = jnp.where(
            lax.axis_index("x") == 0,
            jnp.concatenate([own, got["x"]], axis=1),
            jnp.concatenate([got["x"], own], axis=1),
        )
        return lax.all_gather(both, "y", axis=0, tiled=True)
    here, half = lax.axis_index("y"), lax.axis_index("x")
    mine, far = 2 * here, 2 * (1 - here)
    spots = [
        (mine, half, own),
        (far, half, got["y"]),
        (mine, 1 - half, got["x"]),
        (far, 1 - half, got["over_x"]),
        (far + 1, 1 - half, got["over_y"]),
    ]
    return assemble((2 * rows, 2 * cols), (rows // 2, cols), spots)


def fold_parts(both):
    cols, here = both.shape[1] // 2, lax.axis_index("x")
    mine = lax.dynamic_slice_in_dim(both, here * cols, cols, 1)
    other = lax.dynamic_slice_in_dim(both, (1 - here) * cols, cols, 1)
    (own, over_y), (over_x, across) = pair_halves(mine, "y"), pair_halves(other, "y")
    return {"own": own, "x": over_x, "y": over_y, "across": across}


def fold_first(across):
    rows = across.shape[0] // 2
    return [swap(across[:rows], "x", 1), swap(across[rows:], "y", 1)]


def fold_join(parts, got):
    rows = got[0].shape[0]
    over_y = add_low(parts["y"][:rows], got[0])
    over_x = add_low(parts["x"][rows:], got[1])
    return (
        jnp.concatenate([parts["x"][:rows], over_x]),
        jnp.concatenate([over_y, parts["y"][rows:]]),
    )


def spread_ids():
    return jnp.stack([lax.axis_index(axis) for axis in ("z", "y", "c", "x")]).astype(jnp.int32)


LIGHT = pl.CostEstimate(flops=0, bytes_accessed=0, transcendentals=0)


def kernel_params(megabytes=50):
    return pltpu.CompilerParams(
        dimension_semantics=("arbitrary",), vmem_limit_bytes=megabytes * 2**20
    )


def turned(values, cosine, sine):
    half = values.shape[1] // 2
    front, back = values[:, :half], values[:, half:]
    return jnp.concatenate([front * cosine - back * sine, back * cosine + front * sine], axis=1)


def head_probs(query, key, allowed):
    scores = tile_dot_cols(query, key)
    bent = jnp.tanh(scores * (HD**-0.5 / SOFT_CAP))
    masked = jnp.where(allowed != 0, SOFT_CAP * bent, MASK_FILL)
    weights = jnp.exp(masked - jnp.max(masked, axis=1, keepdims=True))
    return bent, weights / jnp.sum(weights, axis=1, keepdims=True)


def attention_kernel(x, weight, cosine, sine, allowed, query, key, value, attended):
    heads = query.shape[1] // HD
    proj = tile_dot(x[...], weight[...])
    key_here = turned(proj[:, heads * HD : (heads + 1) * HD], cosine[...], sine[...]).astype(BF)
    value_here = proj[:, (heads + 1) * HD :].astype(BF)
    key[...], value[...] = key_here, value_here
    for head in range(heads):
        at = slice(head * HD, (head + 1) * HD)
        query_here = turned(proj[:, at], cosine[...], sine[...]).astype(BF)
        query[:, at] = query_here
        probs = head_probs(query_here, key_here, allowed[...])[1].astype(BF)
        attended[:, at] = tile_dot(probs, value_here).astype(BF)


def attention_call(x, weight, cosine, sine, allowed, groups):
    tokens, width = x.shape
    cols = weight.shape[1] // groups
    heads = cols // HD - 2

    def here(cut):
        return pl.BlockSpec((tokens, cut), lambda g: (0, g))

    def whole(values):
        return pl.BlockSpec(values.shape, lambda g: (0, 0))

    cuts = [heads * HD, HD, HD, heads * HD]
    return pl.pallas_call(
        attention_kernel,
        grid=(groups,),
        in_specs=[
            whole(x),
            pl.BlockSpec((width, cols), lambda g: (0, g)),
            whole(cosine),
            whole(sine),
            whole(allowed),
        ],
        out_specs=[here(cut) for cut in cuts],
        out_shape=[jax.ShapeDtypeStruct((tokens, groups * cut), BF) for cut in cuts],
        compiler_params=kernel_params(),
        cost_estimate=LIGHT,
    )(x, weight, cosine, sine, allowed)


def share(ids, total, sent, kept):
    rows = sent.shape[0]
    here = ids[3]
    sent[...] = total[pl.ds(pl.multiple_of((1 - here) * rows, rows), rows), :].astype(BF)
    kept[...] = total[pl.ds(pl.multiple_of(here * rows, rows), rows), :]


def branch_kernel(ids, attended, weight, sent, kept, total):
    part = tile_dot_cols(attended[...], weight[...])
    total[...] = jnp.where(pl.program_id(0) == 0, part, total[...] + part)

    @pl.when(pl.program_id(0) == pl.num_programs(0) - 1)
    def _():
        share(ids, total, sent, kept)


def branch_call(ids, attended, weight):
    tokens, cols = attended.shape
    width = weight.shape[0]
    tile = 512
    half = pl.BlockSpec((tokens // 2, width), lambda g, ids: (0, 0))
    return pl.pallas_call(
        branch_kernel,
        grid_spec=pltpu.PrefetchScalarGridSpec(
            num_scalar_prefetch=1,
            grid=(cols // tile,),
            in_specs=[
                pl.BlockSpec((tokens, tile), lambda g, ids: (0, g)),
                pl.BlockSpec((width, tile), lambda g, ids: (0, g)),
            ],
            out_specs=[half, half],
            scratch_shapes=[pltpu.VMEM((tokens, width), F32)],
        ),
        out_shape=[jax.ShapeDtypeStruct((tokens // 2, width), kind) for kind in (BF, F32)],
        compiler_params=kernel_params(),
        cost_estimate=LIGHT,
    )(ids, attended, weight)


def attention_back_kernel(
    ids, d, out, weight, query, key, value, cosine, sine, allowed, d_qkv, sent, kept, total
):
    heads = query.shape[1] // HD
    key_here, value_here = key[...], value[...]
    d_attended = tile_dot(d[...], out[...]).astype(BF)
    d_key = d_value = 0.0
    pieces = []
    for head in range(heads):
        at = slice(head * HD, (head + 1) * HD)
        query_here, d_here = query[:, at], d_attended[:, at]
        bent, probs = head_probs(query_here, key_here, allowed[...])
        d_probs = tile_dot_cols(d_here, value_here)
        inner = jnp.sum(probs * d_probs, axis=1, keepdims=True)
        d_scores = probs * (d_probs - inner) * (HD**-0.5) * (1.0 - bent * bent)
        d_scores = d_scores.astype(BF)
        d_query = tile_dot(d_scores, key_here)
        pieces.append(turned(d_query, cosine[...], -sine[...]).astype(BF))
        d_key = d_key + outer_dot(d_scores, query_here)
        d_value = d_value + outer_dot(probs.astype(BF), d_here)
    pieces.append(turned(d_key, cosine[...], -sine[...]).astype(BF))
    pieces.append(d_value.astype(BF))
    made = jnp.concatenate(pieces, axis=1)
    d_qkv[...] = made
    part = tile_dot_cols(made, weight[...])
    total[...] = jnp.where(pl.program_id(0) == 0, part, total[...] + part)

    @pl.when(pl.program_id(0) == pl.num_programs(0) - 1)
    def _():
        share(ids, total, sent, kept)


def attention_back_call(ids, d, out, weight, query, key, value, cosine, sine, allowed, groups):
    tokens, width = d.shape
    cols = weight.shape[1] // groups
    heads = cols // HD - 2

    def here(rows, cut):
        return pl.BlockSpec((rows, cut), lambda g, ids: (0, g))

    def whole(values):
        return pl.BlockSpec(values.shape, lambda g, ids: (0, 0))

    half = pl.BlockSpec((tokens // 2, width), lambda g, ids: (0, 0))
    return pl.pallas_call(
        attention_back_kernel,
        grid_spec=pltpu.PrefetchScalarGridSpec(
            num_scalar_prefetch=1,
            grid=(groups,),
            in_specs=[
                whole(d),
                here(width, heads * HD),
                here(width, cols),
                here(tokens, heads * HD),
                here(tokens, HD),
                here(tokens, HD),
                whole(cosine),
                whole(sine),
                whole(allowed),
            ],
            out_specs=[here(tokens, cols), half, half],
            scratch_shapes=[pltpu.VMEM((tokens, width), F32)],
        ),
        out_shape=[
            jax.ShapeDtypeStruct((tokens, groups * cols), BF),
            jax.ShapeDtypeStruct((tokens // 2, width), BF),
            jax.ShapeDtypeStruct((tokens // 2, width), F32),
        ],
        compiler_params=kernel_params(),
        cost_estimate=LIGHT,
    )(ids, d, out, weight, query, key, value, cosine, sine, allowed)


def outer_kernel(which, left, right, *rest):
    got, (made, flipped) = rest[:-2], rest[-2:]

    @pl.when(pl.program_id(0) == 0)
    def _():
        flipped[...] = left[...].T

    total = tile_dot(flipped[...], right[...])
    for piece in got:
        total = total + piece[...].astype(F32)
    made[...] = total.astype(BF)


def outer_call(left, right, which, *got):
    tokens, cut, cols = left.shape[0], left.shape[1] // 2, right.shape[1]
    tile = cols // 2
    across = pl.BlockSpec((cut, tile), lambda i, which: (0, i))
    return pl.pallas_call(
        outer_kernel,
        grid_spec=pltpu.PrefetchScalarGridSpec(
            num_scalar_prefetch=1,
            grid=(cols // tile,),
            in_specs=[
                pl.BlockSpec((tokens, cut), lambda i, which: (0, which[0])),
                pl.BlockSpec((tokens, tile), lambda i, which: (0, i)),
            ]
            + [across] * len(got),
            out_specs=across,
            scratch_shapes=[pltpu.VMEM((cut, tokens), BF)],
        ),
        out_shape=jax.ShapeDtypeStruct((cut, cols), BF),
        compiler_params=kernel_params(),
        cost_estimate=LIGHT,
    )(which, left, right, *got)


def outer_halves_kernel(left, right, made, flipped):
    @pl.when(pl.program_id(0) == 0)
    def _():
        flipped[...] = left[...].T

    made[...] = tile_dot(flipped[...], right[...]).astype(BF)


def outer_halves(left, right):
    tokens, width = left.shape
    cols = right.shape[1] // 2
    tile = 384
    count = cols // tile
    return pl.pallas_call(
        outer_halves_kernel,
        grid=(2 * count,),
        in_specs=[
            pl.BlockSpec((tokens, width), lambda i: (0, 0)),
            pl.BlockSpec((tokens, tile), lambda i: (0, i)),
        ],
        out_specs=pl.BlockSpec((None, width, tile), lambda i: (i // count, 0, i % count)),
        out_shape=jax.ShapeDtypeStruct((2, width, cols), BF),
        scratch_shapes=[pltpu.VMEM((width, tokens), BF)],
        compiler_params=kernel_params(),
        cost_estimate=LIGHT,
    )(left, right)


def sum_cut(grad):
    width, cols = grad.shape[1:]
    blocks = 2 * lax.axis_size("c") * lax.axis_size("y")
    grad = grad.reshape(blocks, 2 * width // blocks, cols)
    return lax.psum_scatter(grad, ("x", "c", "y"), scatter_dimension=0, tiled=True)[0]


def gather_cut(own):
    whole = lax.all_gather(own, ("x", "c", "y"), axis=0, tiled=True)
    return whole.reshape(2, 2, -1, own.shape[1])


def outer_low(left, right, mine, theirs):
    sent = outer_call(left, right, theirs)
    return outer_call(left, right, mine, swap(sent, "c", 1))


def assemble_kernel(counts, rows, cols, *refs):
    pieces, made = refs[:-1], refs[-1]
    step, first = pl.program_id(0), 0
    for piece, count in zip(pieces, counts):

        @pl.when((step >= first) & (step < first + count))
        def _(piece=piece):
            made[...] = piece[...].astype(made.dtype)

        first += count


def assemble(shape, block, placed, kind=BF):
    counts = [array.shape[0] // block[0] for _, _, array in placed]
    steps = [(row + k, col) for (row, col, _), n in zip(placed, counts) for k in range(n)]
    rows, cols = (jnp.stack([jnp.asarray(s[i], jnp.int32) for s in steps]) for i in range(2))
    specs, first = [], 0
    for count in counts:

        def at(step, rows, cols, first=first, count=count):
            return (jnp.clip(step - first, 0, count - 1), 0)

        specs.append(pl.BlockSpec(block, at))
        first += count
    return pl.pallas_call(
        functools.partial(assemble_kernel, counts),
        grid_spec=pltpu.PrefetchScalarGridSpec(
            num_scalar_prefetch=2,
            grid=(len(steps),),
            in_specs=specs,
            out_specs=pl.BlockSpec(block, lambda step, rows, cols: (rows[step], cols[step])),
        ),
        out_shape=jax.ShapeDtypeStruct(shape, kind),
        compiler_params=kernel_params(),
        cost_estimate=LIGHT,
    )(rows, cols, *[array for _, _, array in placed])


def gain_sum(parts):
    count, width = parts.shape
    blocks = lax.axis_size("c") * lax.axis_size("y") * lax.axis_size("z")
    parts = parts.reshape(count, blocks, width // blocks).transpose(1, 0, 2)
    parts = parts + swap(parts, "x", 1)
    here, rows = lax.axis_index("c"), blocks // 2
    parts = lax.dynamic_slice_in_dim(parts, here * rows, rows, 0) + swap(
        lax.dynamic_slice_in_dim(parts, (1 - here) * rows, rows, 0), "c", 1
    )
    if lax.axis_size("y") == 2:
        here, rows = lax.axis_index("y"), blocks // 4
        parts = lax.dynamic_slice_in_dim(parts, here * rows, rows, 0) + swap(
            lax.dynamic_slice_in_dim(parts, (1 - here) * rows, rows, 0), "y", 1
        )
    else:
        parts = lax.psum_scatter(parts, "y", scatter_dimension=0, tiled=True)
    here = lax.axis_index("z")
    total = lax.dynamic_index_in_dim(parts, here, 0, keepdims=False)
    for k in (1, 2, 3):
        total = total + swap(
            lax.dynamic_index_in_dim(parts, here ^ k, 0, keepdims=False), "z", k
        )
    return total


def on_device(
    tokens,
    seg_lengths,
    parents,
    attn_gain,
    w_query,
    w_key,
    w_value,
    w_out,
    attn_post_gain,
    ffn_gain,
    w_gate,
    w_up,
    w_down,
    ffn_post_gain,
    out_grad,
):
    local_rows, width = tokens.shape
    z_size, y_size, c_size = lax.axis_size("z"), lax.axis_size("y"), lax.axis_size("c")
    shard = width // (z_size * y_size * c_size)
    group_rows = local_rows * lax.axis_size("x")
    head_cols = w_query.shape[1]
    kv_cols = w_key.shape[1]
    kv_here = kv_cols // HD
    ids = spread_ids()
    core_here, core_there = ids[2:3], 1 - ids[2:3]
    first_half, second_half = jnp.zeros(1, jnp.int32), jnp.ones(1, jnp.int32)

    def inward(values):
        lead = values.shape[:-1]
        cut = values.reshape(lead + (z_size, y_size, c_size, shard))
        count = len(lead)
        order = tuple(range(count)) + (count + 2, count + 1, count, count + 3)
        return cut.transpose(order).reshape(lead + (width,))

    def outward(values):
        lead = values.shape[:-1]
        cut = values.reshape(lead + (c_size, y_size, z_size, shard))
        count = len(lead)
        order = tuple(range(count)) + (count + 2, count + 1, count, count + 3)
        return cut.transpose(order).reshape(lead + (width,))

    pairs = y_size == 2
    row_axes = ("c", "y", "z")
    positions, allowed = tree_tables(seg_lengths[0], parents[0], group_rows)
    allowed = allowed.astype(jnp.int32)
    cosine, sine = rope_tables(positions, HD)
    attn_gain, attn_post_gain = inward(attn_gain), inward(attn_post_gain)
    ffn_gain, ffn_post_gain = inward(ffn_gain), inward(ffn_post_gain)
    state_in = inward(tokens).astype(F32)
    out_cotan = inward(out_grad).astype(F32)

    qkv_here = jnp.concatenate(
        [
            weight[:, g * (weight.shape[1] // kv_here) : (g + 1) * (weight.shape[1] // kv_here)]
            for g in range(kv_here)
            for weight in (w_query, w_key, w_value)
        ],
        axis=1,
    )
    inverse_one = lax.rsqrt(jnp.mean(state_in * state_in, axis=-1, keepdims=True) + NORM_EPS)
    unit_one = state_in * inverse_one
    normed_here = (unit_one * attn_gain).astype(BF)

    qkv_weight = lax.all_gather(qkv_here, row_axes, axis=0, tiled=True)
    out_weight = lax.all_gather(w_out.T, row_axes, axis=0, tiled=True)

    live = {"up": line_cuts(w_up), "down": line_cuts(w_down.T)}
    live["gate"] = line_swaps(line_cuts(w_gate))
    live["normed_one"] = [normed_here, swap(normed_here, "x", 1)]
    live = close(live)

    live["normed_one"] = pair_gather(*live["normed_one"])
    live["gate"] = cut_first(line_place(live["gate"]))
    live["up"] = line_swaps(live["up"])
    live = close(live)

    live["gate"] |= cut_over_x(live["gate"]) | cut_over_y(live["gate"])
    live["up"] = cut_first(line_place(live["up"]))
    live["down"] = line_swaps(live["down"])
    live["qkv"] = qkv_weight
    live = close(live)
    down_weight = gather_cut(line_place(live.pop("down")))

    live["up"] |= cut_over_x(live["up"]) | cut_over_y(live["up"])
    gate_half = cut_half(live["gate"])
    live["gate"] = [gate_half, swap(gate_half, "c", 1)]
    normed_one, qkv_weight = live["normed_one"], live["qkv"]
    query, key, value, attended = attention_call(
        normed_one, qkv_weight, cosine, sine, allowed, kv_here
    )
    live["attended"] = attended
    live = close(live)

    attended = live["attended"]
    live["branch"] = branch_call(ids, attended, out_weight)
    live = close(live)
    sent, kept = live["branch"]
    live["branch"] = [kept, swap(sent, "x", 1)]
    up_half = cut_half(live["up"])
    live["up"] = [up_half, swap(up_half, "c", 1)]
    live = close(live)
    branch = live["branch"][0] + live["branch"][1].astype(F32)
    inverse_two = lax.rsqrt(jnp.mean(branch * branch, axis=-1, keepdims=True) + NORM_EPS)
    unit_two = branch * inverse_two
    hidden = state_in + unit_two * attn_post_gain
    inverse_three = lax.rsqrt(jnp.mean(hidden * hidden, axis=-1, keepdims=True) + NORM_EPS)
    unit_three = hidden * inverse_three


    live["normed_two"] = line_gather((unit_three * ffn_gain).astype(BF))
    live = close(live)
    weights = [Weight(*live["gate"]), Weight(*live["up"]), Weight(down_weight)]
    normed_two = live["normed_two"]

    live["act"], gate_proj, up_proj, *sums = ffn_call(
        forward_kernel, ids, normed_two, weights, (), (BF, F32, F32), 384
    )
    live["sums"] = line_swaps(sums)
    live = close(live)
    ffn_out = line_total(live["sums"])
    inverse_four = lax.rsqrt(jnp.mean(ffn_out * ffn_out, axis=-1, keepdims=True) + NORM_EPS)
    unit_four = ffn_out * inverse_four
    mixed = (hidden + unit_four * ffn_post_gain).astype(BF)
    gain_four = jnp.sum(out_cotan * unit_four, axis=0)
    d_ffn = norm_back(out_cotan * ffn_post_gain, unit_four, inverse_four).astype(BF)
    live["d_ffn"] = line_gather(d_ffn)
    live = close(live)
    d_ffn, act, normed_two = live["d_ffn"], live["act"], live["normed_two"]
    grad_down = sum_cut(outer_halves(d_ffn, act))
    d_gate, d_up, *sums = ffn_call(
        backward_kernel, ids, d_ffn, weights, (gate_proj, up_proj), (BF, BF), 384
    )
    live = close({"d_gate": d_gate, "d_up": d_up, "sums": sums})

    live["sums"] = line_swaps(live["sums"])
    if pairs:
        gate = fold_parts(outer_low(normed_two, live["d_gate"], core_here, core_there))
        live["gate_got"] = fold_first(gate.pop("across"))
        live["gate"] = gate
    else:
        live["gate"] = outer_halves(normed_two, live["d_gate"])
    live["up"] = outer_halves(normed_two, live["d_up"])
    live = close({k: live[k] for k in ("sums", "up", "gate", "gate_got") if k in live})
    grad_up = sum_cut(live.pop("up"))

    d_normed_two = line_total(live["sums"])
    gain_three = jnp.sum(d_normed_two * unit_three, axis=0)
    d_hidden = out_cotan + norm_back(d_normed_two * ffn_gain, unit_three, inverse_three)
    gain_two = jnp.sum(d_hidden * unit_two, axis=0)
    d_branch = norm_back(d_hidden * attn_post_gain, unit_two, inverse_two).astype(BF)
    live["d_branch"] = [d_branch, swap(d_branch, "x", 1)]
    if pairs:
        own = live["gate"]["own"]
        over_x, over_y = fold_join(live["gate"], live.pop("gate_got"))
        live["gate"] = {"own": own, "x": over_x, "y": swap(over_y, "y", 1)}
    else:
        live["gate"] = {"own": sum_cut(live["gate"])}
    live = close({k: live[k] for k in ("d_branch", "gate")})
    d_branch = pair_gather(*live["d_branch"])

    if pairs:
        live["gate"]["x"] = swap(live["gate"]["x"], "x", 1)
    live["down"] = line_swaps(line_chunks(grad_down))
    grad_out = outer_low(d_branch, attended, core_here, core_there)
    if pairs:
        out_mine, out_far = pair_halves(grad_out, "y")
        live["out"] = [out_mine, swap(out_far, "y", 1)]
    else:
        live["out"] = [rows_sum(grad_out, "y")]
    d_qkv, sent, kept = attention_back_call(
        ids, d_branch, out_weight, qkv_weight, query, key, value, cosine, sine, allowed, kv_here
    )
    live["d_normed_one"] = [kept, sent]
    live["d_qkv"] = d_qkv
    live = close(live)

    grad_down = line_columns(live["down"])
    kept, sent = live["d_normed_one"]
    live["d_normed_one"] = [kept, swap(sent, "x", 1)]
    live["qkv"] = outer_low(normed_one, live["d_qkv"], core_here, core_there)
    live["out"] = add_low(*live["out"]) if pairs else live["out"][0]
    grad_gate = line_total(list(live["gate"].values())).astype(BF)
    live["gate"] = line_swaps(line_chunks(grad_gate))
    live = close({k: live[k] for k in ("d_normed_one", "qkv", "out", "gate")})
    grad_gate = line_columns(live["gate"])
    d_normed_one = live["d_normed_one"][0] + live["d_normed_one"][1].astype(F32)
    gain_one = jnp.sum(d_normed_one * unit_one, axis=0)
    grad_tokens = d_hidden + norm_back(d_normed_one * attn_gain, unit_one, inverse_one)

    parts = y_chunks(live["qkv"]) if pairs else line_chunks(rows_sum(live["qkv"], "y"))
    live = {"parts": parts, "out": line_swaps(line_chunks(live["out"]))}
    live["gains"] = jnp.stack([gain_one, gain_two, gain_three, gain_four], axis=0)
    if pairs:
        live["far"] = [swap(parts[k][1], "y", 1) for k in (2, 3)]
    live = close(live)
    parts, grad_out = live["parts"], line_total(live.pop("out"))

    if pairs:
        far = [add_low(parts[k][0], q) for k, q in zip((2, 3), live["far"])]
        live["near"] = [swap(parts[k][1], "y", 1) for k in (0, 1)]
    else:
        far = parts[2:]
    live["far"] = [swap(piece, "z", k) for k, piece in zip((2, 3), far)]
    gains = gain_sum(live.pop("gains"))
    live = close(live)

    if pairs:
        near = [add_low(live["parts"][k][0], q) for k, q in zip((0, 1), live["near"])]
    else:
        near = live["parts"][:2]
    grad_qkv = line_total([near[0], swap(near[1], "z", 1), *live["far"]])
    grad_up = line_columns(line_swaps(line_chunks(grad_up)))
    cols = grad_qkv.shape[1] // kv_here
    cuts = (0, cols - 2 * HD, cols - HD, cols)
    grad_query, grad_key, grad_value = (
        jnp.concatenate(
            [grad_qkv[:, g * cols + cuts[i] : g * cols + cuts[i + 1]] for g in range(kv_here)],
            axis=1,
        )
        for i in range(3)
    )
    return (
        outward(mixed),
        outward(grad_tokens),
        gains[0],
        grad_query,
        grad_key,
        grad_value,
        grad_out.T,
        gains[1],
        gains[2],
        grad_gate,
        grad_up,
        grad_down.T,
        gains[3],
    )


def solution(mesh):
    count, pair = mesh.devices.shape
    grid = Mesh(mesh.devices.reshape(4, count // 8, 2, pair), ("z", "y", "c", "x"))
    rows = ("z", "y", "c")
    return jax.shard_map(
        on_device,
        mesh=grid,
        in_specs=(
            P(rows + ("x",), None),
            P(rows, None),
            P(rows, None),
            P(),
            P(rows, "x"),
            P(rows, "x"),
            P(rows, "x"),
            P("x", rows),
            P(),
            P(),
            P(rows, "x"),
            P(rows, "x"),
            P("x", rows),
            P(),
            P(rows + ("x",), None),
        ),
        out_specs=(
            P(rows + ("x",), None),
            P(rows + ("x",), None),
            P(rows),
            P(rows, "x"),
            P(rows, "x"),
            P(rows, "x"),
            P("x", rows),
            P(rows),
            P(rows),
            P(rows, "x"),
            P(rows, "x"),
            P("x", rows),
            P(rows),
        ),
        check_vma=False,
    )
```

```python
import functools

import jax
import jax.numpy as jnp
from jax import lax
from jax.experimental import pallas as pl
from jax.experimental.pallas import tpu as pltpu
from jax.sharding import Mesh
from jax.sharding import PartitionSpec as P

HD = 256
NORM_EPS = 1e-06
SOFT_CAP = 50.0
ROPE_BASE = 10000.0
MASK_FILL = -1e30
BF = jnp.bfloat16
F32 = jnp.float32


def tree_tables(lengths_row, parents_row, row_total):
    seg_count = lengths_row.shape[0]
    seg_index = jnp.arange(seg_count, dtype=jnp.int32)
    ancestor = (seg_index[:, None] == seg_index[None, :]) | (
        parents_row[:, None] == seg_index[None, :]
    )
    for repeat in range(seg_count.bit_length()):
        ancestor = jnp.any(ancestor[:, :, None] & ancestor[None, :, :], axis=1)
    seg_ends = jnp.cumsum(lengths_row)
    seg_starts = seg_ends - lengths_row
    token_index = jnp.arange(row_total, dtype=jnp.int32)
    segment = jnp.sum((token_index[:, None] >= seg_ends[None, :]).astype(jnp.int32), axis=1)
    strict = ancestor & (seg_index[:, None] != seg_index[None, :])
    offsets = jnp.sum(jnp.where(strict, lengths_row[None, :], 0), axis=1)
    one_hot = segment[:, None] == seg_index[None, :]
    positions = (
        jnp.sum(jnp.where(one_hot, (offsets - seg_starts)[None, :], 0), axis=1) + token_index
    )
    reached = jnp.any(one_hot[:, :, None] & ancestor[None, :, :], axis=1)
    allowed = jnp.any(reached[:, None, :] & one_hot[None, :, :], axis=2) & (
        token_index[None, :] <= token_index[:, None]
    )
    return (positions, allowed)


def rope_tables(positions, width):
    half_width = width // 2
    frequency = ROPE_BASE ** (-2.0 * jnp.arange(half_width, dtype=F32) / width)
    angles = positions.astype(F32)[:, None] * frequency[None, :]
    return (jnp.cos(angles), jnp.sin(angles))


def norm_back(grad_unit, unit, inverse):
    return inverse * (grad_unit - unit * jnp.mean(grad_unit * unit, axis=-1, keepdims=True))


def gelu_parts(values):
    scale = (2.0 / jnp.pi) ** 0.5
    square = values * values
    bent = jnp.tanh(scale * (values + 0.044715 * values * square))
    half = 0.5 * (1.0 + bent)
    slope = half + 0.5 * values * (1.0 - bent * bent) * scale * (1.0 + 3 * 0.044715 * square)
    return values * half, slope


def tile_dot(left, right):
    return jnp.dot(left, right, preferred_element_type=F32)


def tile_dot_cols(left, right):
    return lax.dot_general(left, right, (((1,), (1,)), ((), ())), preferred_element_type=F32)


def spill(ids, total, outs):
    rows = total.shape[0] // 4
    if len(outs) == 1:
        for k in range(4):
            at = pl.multiple_of((ids[0] ^ k) * rows, rows)
            outs[0][pl.ds(at, rows), :] = total[k * rows : (k + 1) * rows, :].astype(BF)
        return
    for k, out in enumerate(outs):
        out[...] = total[k * rows : (k + 1) * rows, :].astype(out.dtype)


class Weight:
    def __init__(self, *arrays):
        self.arrays, self.whole = arrays, len(arrays) == 1
        self.rows = arrays[0].shape[-2]

    def specs(self, tile):
        if not self.whole:
            return [pl.BlockSpec((self.rows, tile), lambda i, ids: (0, i))] * 2
        count = self.arrays[0].shape[-1] // tile
        return [
            pl.BlockSpec(
                (None, None, self.rows, tile), lambda i, ids, c=c: (i // count, c, 0, i % count)
            )
            for c in range(2)
        ]

    def operands(self):
        return self.arrays * 2 if self.whole else self.arrays

    def columns(self, ids):
        first, second = (0, self.rows) if self.whole else (ids[2] * self.rows, (1 - ids[2]) * self.rows)
        if not self.whole:
            first, second = (pl.multiple_of(at, 128) for at in (first, second))
        return pl.ds(first, self.rows), pl.ds(second, self.rows)


def inner(values, refs, columns):
    return sum(tile_dot(values[:, at], ref[...]) for ref, at in zip(refs, columns))


def outer_add(total, tile, refs, columns, fresh):
    for ref, at in zip(refs, columns):
        part = tile_dot_cols(tile, ref[...])
        total[:, at] = jnp.where(fresh, part, total[:, at] + part)


def forward_kernel(columns, ids, x, *refs):
    gate_w, up_w, down_w, (act, gate, up), outs, total = (
        refs[:2], refs[2:4], refs[4:6], refs[6:9], refs[9:13], refs[13]
    )
    gate_at, up_at, down_at = (find(ids) for find in columns)
    gate_tile, up_tile = inner(x, gate_w, gate_at), inner(x, up_w, up_at)
    gate[...], up[...] = gate_tile, up_tile
    act_tile = (gelu_parts(gate_tile)[0] * up_tile).astype(BF)
    act[...] = act_tile
    outer_add(total, act_tile, down_w, down_at, pl.program_id(0) == 0)

    @pl.when(pl.program_id(0) == pl.num_programs(0) - 1)
    def _():
        spill(ids, total, outs)


def backward_kernel(columns, ids, d, *refs):
    gate_w, up_w, down_w, (gate, up), (d_gate, d_up), outs, total = (
        refs[:2], refs[2:4], refs[4:6], refs[6:8], refs[8:10], refs[10:-1], refs[-1]
    )
    gate_at, up_at, down_at = (find(ids) for find in columns)
    d_act = inner(d, down_w, down_at)
    bent, slope = gelu_parts(gate[...])
    gate_tile = (d_act * up[...] * slope).astype(BF)
    up_tile = (d_act * bent).astype(BF)
    d_gate[...], d_up[...] = gate_tile, up_tile
    outer_add(total, gate_tile, gate_w, gate_at, pl.program_id(0) == 0)
    outer_add(total, up_tile, up_w, up_at, False)

    @pl.when(pl.program_id(0) == pl.num_programs(0) - 1)
    def _():
        spill(ids, total, outs)


def ffn_call(kernel, ids, values, weights, kept, made, tile, natural):
    tokens, width = values.shape
    hidden = 2 * weights[-1].arrays[0].shape[-1] if weights[-1].whole else weights[-1].arrays[0].shape[-1]
    slot = tokens // 4
    across = pl.BlockSpec((tokens, tile), lambda i, ids: (0, i))
    parts = [(tokens, BF)] if natural else [(slot, F32)] + [(slot, BF)] * 3
    whole = [pl.BlockSpec((rows, width), lambda i, ids: (0, 0)) for rows, _ in parts]
    return pl.pallas_call(
        functools.partial(kernel, [weight.columns for weight in weights]),
        grid_spec=pltpu.PrefetchScalarGridSpec(
            num_scalar_prefetch=1,
            grid=(hidden // tile,),
            in_specs=[pl.BlockSpec((tokens, width), lambda i, ids: (0, 0))]
            + [spec for weight in weights for spec in weight.specs(tile)]
            + [across] * len(kept),
            out_specs=[across] * len(made) + whole,
            scratch_shapes=[pltpu.VMEM((tokens, width), F32)],
        ),
        out_shape=[jax.ShapeDtypeStruct((tokens, hidden), kind) for kind in made]
        + [jax.ShapeDtypeStruct((rows, width), kind) for rows, kind in parts],
        compiler_params=pltpu.CompilerParams(
            dimension_semantics=("arbitrary",), vmem_limit_bytes=58 * 2**20
        ),
        cost_estimate=pl.CostEstimate(flops=0, bytes_accessed=0, transcendentals=0),
    )(ids, values, *[array for weight in weights for array in weight.operands()], *kept)


def swap(values, axis, mask):
    size = lax.axis_size(axis)
    return lax.ppermute(values, axis, [(i, i ^ mask) for i in range(size)])


def rows_dot(left, right):
    return lax.dot_general(left, right, (((1,), (0,)), ((), ())), preferred_element_type=F32)


def cols_dot(left, right):
    return lax.dot_general(left, right, (((1,), (1,)), ((), ())), preferred_element_type=F32)


def outer_dot(left, right):
    return lax.dot_general(left, right, (((0,), (0,)), ((), ())), preferred_element_type=F32)


def close(live):
    return lax.optimization_barrier(live)


def pair_gather(values, other):
    mine = lax.axis_index("x")
    first = jnp.where(mine == 0, values, other)
    second = jnp.where(mine == 0, other, values)
    return jnp.concatenate([first, second], axis=0)


def pair_parts(partial):
    rows = partial.shape[0] // 2
    mine = lax.axis_index("x")
    sent = lax.dynamic_slice_in_dim(partial, (1 - mine) * rows, rows, 0).astype(BF)
    return sent, lax.dynamic_slice_in_dim(partial, mine * rows, rows, 0)


def pair_sum(partial):
    sent, kept = pair_parts(partial)
    return kept + swap(sent, "x", 1).astype(F32)


def rows_sum(values, axis):
    size = lax.axis_size(axis)
    if size != 2:
        return lax.psum_scatter(values, axis, scatter_dimension=0, tiled=True)
    rows, mine = values.shape[0] // 2, lax.axis_index(axis)
    sent = lax.dynamic_slice_in_dim(values, (1 - mine) * rows, rows, 0)
    return add_low(lax.dynamic_slice_in_dim(values, mine * rows, rows, 0), swap(sent, axis, 1))


def placed(rows, *pieces):
    held = jnp.zeros((rows,) + pieces[0][1].shape[1:], pieces[0][1].dtype)
    for offset, piece in pieces:
        held = lax.dynamic_update_slice_in_dim(held, piece, offset, 0)
    return held


def add_low(left, right):
    return (left.astype(F32) + right.astype(F32)).astype(BF)


def line_gather(values):
    near, far = swap(values, "z", 1), swap(values, "z", 2)
    return jnp.concatenate([values, near, far, swap(far, "z", 1)], axis=0)


def line_sum_first(parts):
    return [*parts[:3], swap(parts[3], "z", 1)]


def line_sum_second(parts):
    return [parts[0], swap(parts[1], "z", 1), swap(add_low(parts[2], parts[3]), "z", 2)]


def line_place(pieces):
    here, (rows, cols) = lax.axis_index("z"), pieces[0].shape
    if rows % 16 == 0:
        return assemble(
            (len(pieces) * rows, cols), (rows, cols), [(here ^ k, 0, p) for k, p in enumerate(pieces)]
        )
    return placed(len(pieces) * rows, *[((here ^ k) * rows, p) for k, p in enumerate(pieces)])


def line_cuts(weight):
    here, cut = lax.axis_index("z"), weight.shape[1] // 4
    return [lax.dynamic_slice_in_dim(weight, (here ^ k) * cut, cut, 1) for k in range(4)]


def line_swaps(cuts):
    return [cuts[0]] + [swap(cuts[k], "z", k) for k in (1, 2, 3)]


def line_chunks(grad):
    rows, here = grad.shape[0] // 4, lax.axis_index("z")
    return [lax.dynamic_slice_in_dim(grad, (here ^ k) * rows, rows, 0) for k in range(4)]


def line_columns(pieces):
    here, (rows, cols) = lax.axis_index("z"), pieces[0].shape
    spots = [(0, here ^ k, piece) for k, piece in enumerate(pieces)]
    return assemble((rows, 4 * cols), (rows, cols), spots, F32)


def line_total(pieces):
    total = pieces[0].astype(F32)
    for piece in pieces[1:]:
        total = total + piece.astype(F32)
    return total


def y_chunks(grad):
    rows, y, z = grad.shape[0] // 8, lax.axis_index("y"), lax.axis_index("z")
    return [
        tuple(
            lax.dynamic_slice_in_dim(grad, (4 * side + (z ^ k)) * rows, rows, 0)
            for side in (y, 1 - y)
        )
        for k in range(4)
    ]


def pair_rows(mine, other, axis):
    rows, here = mine.shape[0], lax.axis_index(axis)
    return placed(2 * rows, (here * rows, mine), ((1 - here) * rows, other))


def pair_halves(values, axis):
    rows, here = values.shape[0] // 2, lax.axis_index(axis)
    return (
        lax.dynamic_slice_in_dim(values, here * rows, rows, 0),
        lax.dynamic_slice_in_dim(values, (1 - here) * rows, rows, 0),
    )


def cut_first(own):
    got = {"own": own, "x": swap(own, "x", 1)}
    if lax.axis_size("y") == 2:
        got["y"] = swap(own, "y", 1)
    return got


def cut_over_x(got):
    rows = got["own"].shape[0] // 2
    return {"over_x": swap(got["y"][:rows], "x", 1)} if "y" in got else {}


def cut_over_y(got):
    rows = got["own"].shape[0] // 2
    return {"over_y": swap(got["x"][rows:], "y", 1)} if "y" in got else {}


def cut_half(got):
    own = got["own"]
    rows, cols = own.shape
    if "y" not in got:
        both = jnp.where(
            lax.axis_index("x") == 0,
            jnp.concatenate([own, got["x"]], axis=1),
            jnp.concatenate([got["x"], own], axis=1),
        )
        return lax.all_gather(both, "y", axis=0, tiled=True)
    here, half = lax.axis_index("y"), lax.axis_index("x")
    mine, far = 2 * here, 2 * (1 - here)
    spots = [
        (mine, half, own),
        (far, half, got["y"]),
        (mine, 1 - half, got["x"]),
        (far, 1 - half, got["over_x"]),
        (far + 1, 1 - half, got["over_y"]),
    ]
    return assemble((2 * rows, 2 * cols), (rows // 2, cols), spots)


def fold_parts(both):
    cols, here = both.shape[1] // 2, lax.axis_index("x")
    mine = lax.dynamic_slice_in_dim(both, here * cols, cols, 1)
    other = lax.dynamic_slice_in_dim(both, (1 - here) * cols, cols, 1)
    (own, over_y), (over_x, across) = pair_halves(mine, "y"), pair_halves(other, "y")
    return {"own": own, "x": over_x, "y": over_y, "across": across}


def fold_first(across):
    rows = across.shape[0] // 2
    return [swap(across[:rows], "x", 1), swap(across[rows:], "y", 1)]


def fold_join(parts, got):
    rows = got[0].shape[0]
    over_y = add_low(parts["y"][:rows], got[0])
    over_x = add_low(parts["x"][rows:], got[1])
    return (
        jnp.concatenate([parts["x"][:rows], over_x]),
        jnp.concatenate([over_y, parts["y"][rows:]]),
    )


def spread_ids():
    return jnp.stack([lax.axis_index(axis) for axis in ("z", "y", "c", "x")]).astype(jnp.int32)


LIGHT = pl.CostEstimate(flops=0, bytes_accessed=0, transcendentals=0)


def kernel_params(megabytes=50):
    return pltpu.CompilerParams(
        dimension_semantics=("arbitrary",), vmem_limit_bytes=megabytes * 2**20
    )


def turned(values, cosine, sine):
    half = values.shape[1] // 2
    front, back = values[:, :half], values[:, half:]
    return jnp.concatenate([front * cosine - back * sine, back * cosine + front * sine], axis=1)


def head_probs(query, key, allowed):
    scores = tile_dot_cols(query, key)
    bent = jnp.tanh(scores * (HD**-0.5 / SOFT_CAP))
    masked = jnp.where(allowed != 0, SOFT_CAP * bent, MASK_FILL)
    weights = jnp.exp(masked - jnp.max(masked, axis=1, keepdims=True))
    return bent, weights / jnp.sum(weights, axis=1, keepdims=True)


def attention_kernel(x, weight, cosine, sine, allowed, query, key, value, attended):
    heads = query.shape[1] // HD
    proj = tile_dot(x[...], weight[...])
    key_here = turned(proj[:, heads * HD : (heads + 1) * HD], cosine[...], sine[...]).astype(BF)
    value_here = proj[:, (heads + 1) * HD :].astype(BF)
    key[...], value[...] = key_here, value_here
    for head in range(heads):
        at = slice(head * HD, (head + 1) * HD)
        query_here = turned(proj[:, at], cosine[...], sine[...]).astype(BF)
        query[:, at] = query_here
        probs = head_probs(query_here, key_here, allowed[...])[1].astype(BF)
        attended[:, at] = tile_dot(probs, value_here).astype(BF)


def attention_call(x, weight, cosine, sine, allowed, groups):
    tokens, width = x.shape
    cols = weight.shape[1] // groups
    heads = cols // HD - 2

    def here(cut):
        return pl.BlockSpec((tokens, cut), lambda g: (0, g))

    def whole(values):
        return pl.BlockSpec(values.shape, lambda g: (0, 0))

    cuts = [heads * HD, HD, HD, heads * HD]
    return pl.pallas_call(
        attention_kernel,
        grid=(groups,),
        in_specs=[
            whole(x),
            pl.BlockSpec((width, cols), lambda g: (0, g)),
            whole(cosine),
            whole(sine),
            whole(allowed),
        ],
        out_specs=[here(cut) for cut in cuts],
        out_shape=[jax.ShapeDtypeStruct((tokens, groups * cut), BF) for cut in cuts],
        compiler_params=kernel_params(),
        cost_estimate=LIGHT,
    )(x, weight, cosine, sine, allowed)


def share(ids, total, sent, kept):
    rows = sent.shape[0]
    here = ids[3]
    sent[...] = total[pl.ds(pl.multiple_of((1 - here) * rows, rows), rows), :].astype(BF)
    kept[...] = total[pl.ds(pl.multiple_of(here * rows, rows), rows), :]


def branch_kernel(ids, attended, weight, sent, kept, total):
    part = tile_dot_cols(attended[...], weight[...])
    total[...] = jnp.where(pl.program_id(0) == 0, part, total[...] + part)

    @pl.when(pl.program_id(0) == pl.num_programs(0) - 1)
    def _():
        share(ids, total, sent, kept)


def branch_call(ids, attended, weight):
    tokens, cols = attended.shape
    width = weight.shape[0]
    tile = 512
    half = pl.BlockSpec((tokens // 2, width), lambda g, ids: (0, 0))
    return pl.pallas_call(
        branch_kernel,
        grid_spec=pltpu.PrefetchScalarGridSpec(
            num_scalar_prefetch=1,
            grid=(cols // tile,),
            in_specs=[
                pl.BlockSpec((tokens, tile), lambda g, ids: (0, g)),
                pl.BlockSpec((width, tile), lambda g, ids: (0, g)),
            ],
            out_specs=[half, half],
            scratch_shapes=[pltpu.VMEM((tokens, width), F32)],
        ),
        out_shape=[jax.ShapeDtypeStruct((tokens // 2, width), kind) for kind in (BF, F32)],
        compiler_params=kernel_params(),
        cost_estimate=LIGHT,
    )(ids, attended, weight)


def attention_back_kernel(
    ids, d, out, weight, query, key, value, cosine, sine, allowed, d_qkv, sent, kept, total
):
    heads = query.shape[1] // HD
    key_here, value_here = key[...], value[...]
    d_attended = tile_dot(d[...], out[...]).astype(BF)
    d_key = d_value = 0.0
    pieces = []
    for head in range(heads):
        at = slice(head * HD, (head + 1) * HD)
        query_here, d_here = query[:, at], d_attended[:, at]
        bent, probs = head_probs(query_here, key_here, allowed[...])
        d_probs = tile_dot_cols(d_here, value_here)
        inner = jnp.sum(probs * d_probs, axis=1, keepdims=True)
        d_scores = probs * (d_probs - inner) * (HD**-0.5) * (1.0 - bent * bent)
        d_scores = d_scores.astype(BF)
        d_query = tile_dot(d_scores, key_here)
        pieces.append(turned(d_query, cosine[...], -sine[...]).astype(BF))
        d_key = d_key + outer_dot(d_scores, query_here)
        d_value = d_value + outer_dot(probs.astype(BF), d_here)
    pieces.append(turned(d_key, cosine[...], -sine[...]).astype(BF))
    pieces.append(d_value.astype(BF))
    made = jnp.concatenate(pieces, axis=1)
    d_qkv[...] = made
    part = tile_dot_cols(made, weight[...])
    total[...] = jnp.where(pl.program_id(0) == 0, part, total[...] + part)

    @pl.when(pl.program_id(0) == pl.num_programs(0) - 1)
    def _():
        share(ids, total, sent, kept)


def attention_back_call(ids, d, out, weight, query, key, value, cosine, sine, allowed, groups):
    tokens, width = d.shape
    cols = weight.shape[1] // groups
    heads = cols // HD - 2

    def here(rows, cut):
        return pl.BlockSpec((rows, cut), lambda g, ids: (0, g))

    def whole(values):
        return pl.BlockSpec(values.shape, lambda g, ids: (0, 0))

    half = pl.BlockSpec((tokens // 2, width), lambda g, ids: (0, 0))
    return pl.pallas_call(
        attention_back_kernel,
        grid_spec=pltpu.PrefetchScalarGridSpec(
            num_scalar_prefetch=1,
            grid=(groups,),
            in_specs=[
                whole(d),
                here(width, heads * HD),
                here(width, cols),
                here(tokens, heads * HD),
                here(tokens, HD),
                here(tokens, HD),
                whole(cosine),
                whole(sine),
                whole(allowed),
            ],
            out_specs=[here(tokens, cols), half, half],
            scratch_shapes=[pltpu.VMEM((tokens, width), F32)],
        ),
        out_shape=[
            jax.ShapeDtypeStruct((tokens, groups * cols), BF),
            jax.ShapeDtypeStruct((tokens // 2, width), BF),
            jax.ShapeDtypeStruct((tokens // 2, width), F32),
        ],
        compiler_params=kernel_params(),
        cost_estimate=LIGHT,
    )(ids, d, out, weight, query, key, value, cosine, sine, allowed)


def outer_kernel(which, left, right, *rest):
    got, (made, flipped) = rest[:-2], rest[-2:]

    @pl.when(pl.program_id(0) == 0)
    def _():
        flipped[...] = left[...].T

    total = tile_dot(flipped[...], right[...])
    for piece in got:
        total = total + piece[...].astype(F32)
    made[...] = total.astype(BF)


def outer_call(left, right, which, *got):
    tokens, cut, cols = left.shape[0], left.shape[1] // 2, right.shape[1]
    tile = cols // 2
    across = pl.BlockSpec((cut, tile), lambda i, which: (0, i))
    return pl.pallas_call(
        outer_kernel,
        grid_spec=pltpu.PrefetchScalarGridSpec(
            num_scalar_prefetch=1,
            grid=(cols // tile,),
            in_specs=[
                pl.BlockSpec((tokens, cut), lambda i, which: (0, which[0])),
                pl.BlockSpec((tokens, tile), lambda i, which: (0, i)),
            ]
            + [across] * len(got),
            out_specs=across,
            scratch_shapes=[pltpu.VMEM((cut, tokens), BF)],
        ),
        out_shape=jax.ShapeDtypeStruct((cut, cols), BF),
        compiler_params=kernel_params(),
        cost_estimate=LIGHT,
    )(which, left, right, *got)


def outer_halves_kernel(number, which, left, *refs):
    rights, got, (made, flipped) = refs[:number], refs[number:-2], refs[-2:]
    step = pl.program_id(0)

    @pl.when(step == 0)
    def _():
        flipped[...] = left[...].T

    for k, right in enumerate(rights):

        @pl.when(step % number == k)
        def _(right=right):
            total = tile_dot(flipped[...], right[...])
            for piece in got:
                total = total + piece[...].astype(F32)
            made[...] = total.astype(BF)


def outer_halves(which, left, rights, *got):
    tokens, cut = left.shape[0], left.shape[1] // 2
    cols, number = rights[0].shape[1] // 2, len(rights)
    across = pl.BlockSpec((None, cut, cols), lambda i, which: (i // number, 0, i % number))
    return pl.pallas_call(
        functools.partial(outer_halves_kernel, number),
        grid_spec=pltpu.PrefetchScalarGridSpec(
            num_scalar_prefetch=1,
            grid=(2 * number,),
            in_specs=[pl.BlockSpec((tokens, cut), lambda i, which: (0, which[0]))]
            + [pl.BlockSpec((tokens, cols), lambda i, which: (0, i // number))] * number
            + [across] * len(got),
            out_specs=across,
            scratch_shapes=[pltpu.VMEM((cut, tokens), BF)],
        ),
        out_shape=jax.ShapeDtypeStruct((2, cut, number * cols), BF),
        compiler_params=kernel_params(),
        cost_estimate=LIGHT,
    )(which, left, *rights, *got)


def sum_cut(grad):
    half, cols = grad.shape[1:]
    blocks = 2 * lax.axis_size("y")
    grad = grad.reshape(blocks, 2 * half // blocks, cols)
    return lax.psum_scatter(grad, ("x", "y"), scatter_dimension=0, tiled=True)[0]


def gather_cut(own):
    whole = lax.all_gather(own, ("x", "c", "y"), axis=0, tiled=True)
    return whole.reshape(2, 2, -1, own.shape[1])


def outer_low(left, right, mine, theirs):
    sent = outer_call(left, right, theirs)
    return outer_call(left, right, mine, swap(sent, "c", 1))


def outer_quarters_kernel(ids, which, left, right, *refs):
    (plain, flipped), refs = refs[-2:], refs[:-2]
    got, outs = (refs[:4], refs[4:]) if len(refs) > 1 else ((), refs)
    step, rows = pl.program_id(0), flipped.shape[0] // 2

    @pl.when(step == 0)
    def _():
        plain[...] = left[...].T
        for k, side in enumerate((ids[1], 1 - ids[1])):
            at = pl.multiple_of(side * rows, rows)
            flipped[k * rows : (k + 1) * rows, :] = plain[pl.ds(at, rows), :]

    for half in range(2):

        @pl.when(step == half)
        def _(half=half):
            for side in range(2):
                k = half + 2 * side
                total = tile_dot(flipped[side * rows : (side + 1) * rows, :], right[...])
                if got:
                    outs[k][...] = (total + got[k][...].astype(F32)).astype(BF)
                else:
                    outs[0][side] = total.astype(BF)


def outer_quarters(ids, which, left, right, *got):
    tokens, cut, cols = left.shape[0], left.shape[1] // 2, right.shape[1] // 2
    rows = cut // 2
    quarter = pl.BlockSpec((rows, cols), lambda i, ids, which: (0, 0))
    taken = [
        pl.BlockSpec((None, rows, cols), lambda i, ids, which, k=k: (k // 2, 0, k % 2))
        for k in range(4)
    ]
    shape = jax.ShapeDtypeStruct((rows, cols), BF)
    return pl.pallas_call(
        outer_quarters_kernel,
        grid_spec=pltpu.PrefetchScalarGridSpec(
            num_scalar_prefetch=2,
            grid=(2,),
            in_specs=[
                pl.BlockSpec((tokens, cut), lambda i, ids, which: (0, which[0])),
                pl.BlockSpec((tokens, cols), lambda i, ids, which: (0, ids[3] ^ i)),
            ]
            + (taken if got else []),
            out_specs=[quarter] * 4
            if got
            else pl.BlockSpec((2, rows, cols), lambda i, ids, which: (0, 0, i)),
            scratch_shapes=[pltpu.VMEM((cut, tokens), BF)] * 2,
        ),
        out_shape=[shape] * 4 if got else jax.ShapeDtypeStruct((2, rows, 2 * cols), BF),
        compiler_params=kernel_params(),
        cost_estimate=LIGHT,
    )(ids, which, left, right, *got * 4)


def outer_rows_kernel(ids, which, left_a, left_b, right_a, right_b, *refs):
    (plain, flipped), refs = refs[-2:], refs[:-2]
    got, outs = (refs[:4], refs[4:]) if len(refs) > 1 else ((), refs)
    step, last = pl.program_id(0), pl.num_programs(0) - 1
    rows = flipped.shape[0] // 8
    z, y = ids[0], ids[1]
    order = [4 * side + (z ^ k) for side in (1 - y, y) for k in (1, 3, 0, 2)]
    for left, when in ((left_a, 0), (left_b, last)):

        @pl.when(step == when)
        def _(left=left):
            plain[...] = left[...].T
            for k, block in enumerate(order):
                at = pl.multiple_of(block * rows, rows)
                flipped[k * rows : (k + 1) * rows, :] = plain[pl.ds(at, rows), :]

    def give(right):
        total = tile_dot(flipped[...], right[...])
        if not got:
            outs[0][...] = total.astype(BF)
        for k, piece in enumerate(got):
            part = total[2 * k * rows : (2 * k + 2) * rows, :]
            outs[k][...] = (part + piece[...].astype(F32)).astype(BF)

    @pl.when(step < last)
    def _():
        give(right_a)

    @pl.when(step == last)
    def _():
        give(right_b)


def outer_rows(ids, which, left_a, right_a, left_b, right_b, *got):
    tokens, cut = left_a.shape[0], left_a.shape[1] // 2
    tile = right_b.shape[1]
    cols = right_a.shape[1] + tile
    rows = cut // 4
    count = cols // tile
    half = pl.BlockSpec((tokens, cut), lambda i, ids, which: (0, which[0]))
    across = pl.BlockSpec((rows, tile), lambda i, ids, which: (0, i))
    taken = [pl.BlockSpec((rows, tile), lambda i, ids, which, k=k: (k, i)) for k in range(4)]
    return pl.pallas_call(
        outer_rows_kernel,
        grid_spec=pltpu.PrefetchScalarGridSpec(
            num_scalar_prefetch=2,
            grid=(count,),
            in_specs=[
                half,
                half,
                pl.BlockSpec((tokens, tile), lambda i, ids, which: (0, jnp.minimum(i, count - 2))),
                pl.BlockSpec((tokens, tile), lambda i, ids, which: (0, 0)),
            ]
            + (taken if got else []),
            out_specs=[across] * 4
            if got
            else pl.BlockSpec((cut, tile), lambda i, ids, which: (0, i)),
            scratch_shapes=[pltpu.VMEM((cut, tokens), BF)] * 2,
        ),
        out_shape=[jax.ShapeDtypeStruct((rows, cols), BF)] * 4
        if got
        else jax.ShapeDtypeStruct((cut, cols), BF),
        compiler_params=kernel_params(),
        cost_estimate=LIGHT,
    )(ids, which, left_a, left_b, right_a, right_b, *got * 4)


def assemble_kernel(counts, rows, cols, *refs):
    pieces, made = refs[:-1], refs[-1]
    step, first = pl.program_id(0), 0
    for piece, count in zip(pieces, counts):

        @pl.when((step >= first) & (step < first + count))
        def _(piece=piece):
            made[...] = piece[...].astype(made.dtype)

        first += count


def assemble(shape, block, placed, kind=BF):
    counts = [array.shape[0] // block[0] for _, _, array in placed]
    steps = [(row + k, col) for (row, col, _), n in zip(placed, counts) for k in range(n)]
    rows, cols = (jnp.stack([jnp.asarray(s[i], jnp.int32) for s in steps]) for i in range(2))
    specs, first = [], 0
    for count in counts:

        def at(step, rows, cols, first=first, count=count):
            return (jnp.clip(step - first, 0, count - 1), 0)

        specs.append(pl.BlockSpec(block, at))
        first += count
    return pl.pallas_call(
        functools.partial(assemble_kernel, counts),
        grid_spec=pltpu.PrefetchScalarGridSpec(
            num_scalar_prefetch=2,
            grid=(len(steps),),
            in_specs=specs,
            out_specs=pl.BlockSpec(block, lambda step, rows, cols: (rows[step], cols[step])),
        ),
        out_shape=jax.ShapeDtypeStruct(shape, kind),
        compiler_params=kernel_params(),
        cost_estimate=LIGHT,
    )(rows, cols, *[array for _, _, array in placed])


def gain_sum(parts):
    count, width = parts.shape
    c_size, y_size, z_size = (lax.axis_size(axis) for axis in ("c", "y", "z"))
    parts = parts + swap(parts, "x", 1)
    parts = parts.reshape(count, c_size, y_size, z_size, -1).transpose(3, 1, 2, 0, 4)
    here = lax.axis_index("z")
    total = lax.dynamic_index_in_dim(parts, here, 0, keepdims=False)
    for k in (1, 2, 3):
        piece = lax.dynamic_index_in_dim(parts, here ^ k, 0, keepdims=False)
        total = total + swap(piece, "z", k)
    here = lax.axis_index("c")
    sent = lax.dynamic_index_in_dim(total, 1 - here, 0, keepdims=False)
    return lax.dynamic_index_in_dim(total, here, 0, keepdims=False) + swap(sent, "c", 1)


def sum_over_y(parts):
    if lax.axis_size("y") != 2:
        return lax.psum_scatter(parts, "y", scatter_dimension=0, tiled=True)[0]
    here = lax.axis_index("y")
    sent = lax.dynamic_index_in_dim(parts, 1 - here, 0, keepdims=False)
    return lax.dynamic_index_in_dim(parts, here, 0, keepdims=False) + swap(sent, "y", 1)


def on_device(
    tokens,
    seg_lengths,
    parents,
    attn_gain,
    w_query,
    w_key,
    w_value,
    w_out,
    attn_post_gain,
    ffn_gain,
    w_gate,
    w_up,
    w_down,
    ffn_post_gain,
    out_grad,
):
    local_rows, width = tokens.shape
    z_size, y_size, c_size = lax.axis_size("z"), lax.axis_size("y"), lax.axis_size("c")
    shard = width // (z_size * y_size * c_size)
    group_rows = local_rows * lax.axis_size("x")
    head_cols = w_query.shape[1]
    kv_cols = w_key.shape[1]
    kv_here = kv_cols // HD
    ids = spread_ids()
    core_here, core_there = ids[2:3], 1 - ids[2:3]
    first_half, second_half = jnp.zeros(1, jnp.int32), jnp.ones(1, jnp.int32)

    def inward(values):
        lead = values.shape[:-1]
        cut = values.reshape(lead + (z_size, y_size, c_size, shard))
        count = len(lead)
        order = tuple(range(count)) + (count + 2, count + 1, count, count + 3)
        return cut.transpose(order).reshape(lead + (width,))

    def outward(values):
        lead = values.shape[:-1]
        cut = values.reshape(lead + (c_size, y_size, z_size, shard))
        count = len(lead)
        order = tuple(range(count)) + (count + 2, count + 1, count, count + 3)
        return cut.transpose(order).reshape(lead + (width,))

    pairs = y_size == 2
    row_axes = ("c", "y", "z")
    positions, allowed = tree_tables(seg_lengths[0], parents[0], group_rows)
    allowed = allowed.astype(jnp.int32)
    cosine, sine = rope_tables(positions, HD)
    attn_gain, attn_post_gain = inward(attn_gain), inward(attn_post_gain)
    ffn_gain, ffn_post_gain = inward(ffn_gain), inward(ffn_post_gain)
    state_in = inward(tokens).astype(F32)
    out_cotan = inward(out_grad).astype(F32)

    qkv_here = jnp.concatenate(
        [
            weight[:, g * (weight.shape[1] // kv_here) : (g + 1) * (weight.shape[1] // kv_here)]
            for g in range(kv_here)
            for weight in (w_query, w_key, w_value)
        ],
        axis=1,
    )
    inverse_one = lax.rsqrt(jnp.mean(state_in * state_in, axis=-1, keepdims=True) + NORM_EPS)
    unit_one = state_in * inverse_one
    normed_here = (unit_one * attn_gain).astype(BF)

    qkv_weight = lax.all_gather(qkv_here, row_axes, axis=0, tiled=True)
    out_weight = lax.all_gather(w_out.T, row_axes, axis=0, tiled=True)

    live = {"up": line_cuts(w_up), "down": line_cuts(w_down.T)}
    live["gate"] = line_swaps(line_cuts(w_gate))
    live["normed_one"] = [normed_here, swap(normed_here, "x", 1)]
    live = close(live)

    live["normed_one"] = pair_gather(*live["normed_one"])
    live["gate"] = cut_first(line_place(live["gate"]))
    live["up"] = line_swaps(live["up"])
    live = close(live)

    live["gate"] |= cut_over_x(live["gate"]) | cut_over_y(live["gate"])
    live["up"] = cut_first(line_place(live["up"]))
    live["down"] = line_swaps(live["down"])
    live["qkv"] = qkv_weight
    live = close(live)
    down_weight = gather_cut(line_place(live.pop("down")))

    live["up"] |= cut_over_x(live["up"]) | cut_over_y(live["up"])
    gate_half = cut_half(live["gate"])
    live["gate"] = [gate_half, swap(gate_half, "c", 1)]
    normed_one, qkv_weight = live["normed_one"], live["qkv"]
    query, key, value, attended = attention_call(
        normed_one, qkv_weight, cosine, sine, allowed, kv_here
    )
    live["attended"] = attended
    live = close(live)

    attended = live["attended"]
    live["branch"] = branch_call(ids, attended, out_weight)
    live = close(live)
    sent, kept = live["branch"]
    live["branch"] = [kept, swap(sent, "x", 1)]
    up_half = cut_half(live["up"])
    live["up"] = [up_half, swap(up_half, "c", 1)]
    live = close(live)
    branch = live["branch"][0] + live["branch"][1].astype(F32)
    inverse_two = lax.rsqrt(jnp.mean(branch * branch, axis=-1, keepdims=True) + NORM_EPS)
    unit_two = branch * inverse_two
    hidden = state_in + unit_two * attn_post_gain
    inverse_three = lax.rsqrt(jnp.mean(hidden * hidden, axis=-1, keepdims=True) + NORM_EPS)
    unit_three = hidden * inverse_three


    live["normed_two"] = line_gather((unit_three * ffn_gain).astype(BF))
    live = close(live)
    weights = [Weight(*live["gate"]), Weight(*live["up"]), Weight(down_weight)]
    normed_two = live["normed_two"]

    live["act"], gate_proj, up_proj, *sums = ffn_call(
        forward_kernel, ids, normed_two, weights, (), (BF, F32, F32), 384, False
    )
    live["sums"] = line_sum_second(line_sum_first(sums))
    live = close(live)
    ffn_out = line_total(live["sums"])
    inverse_four = lax.rsqrt(jnp.mean(ffn_out * ffn_out, axis=-1, keepdims=True) + NORM_EPS)
    unit_four = ffn_out * inverse_four
    mixed = (hidden + unit_four * ffn_post_gain).astype(BF)
    gain_four = jnp.sum(out_cotan * unit_four, axis=0)
    d_ffn = norm_back(out_cotan * ffn_post_gain, unit_four, inverse_four).astype(BF)
    live["d_ffn"] = line_gather(d_ffn)
    live = close(live)
    d_ffn, act, normed_two = live["d_ffn"], live["act"], live["normed_two"]
    def product(left, right, *got):
        which = core_here if got else core_there
        if pairs:
            return outer_quarters(ids, which, left, right, *got)
        made = outer_halves(which, left, (right,), *got)
        return [made] if got else made

    live = {"down": swap(product(d_ffn, act), "c", 1), "d_ffn": d_ffn, "act": act}
    d_gate, d_up, *sums = ffn_call(
        backward_kernel, ids, d_ffn, weights, (gate_proj, up_proj), (BF, BF), 384, False
    )
    live = close(live | {"d_gate": d_gate, "d_up": d_up, "sums": sums})

    live["sums"] = line_sum_first(live["sums"])
    live["down"] = product(live["d_ffn"], live["act"], live["down"])
    d_gate, d_up = live["d_gate"], live["d_up"]
    live |= {"up": product(normed_two, d_up), "gate": product(normed_two, d_gate)}
    live = close({k: live[k] for k in ("sums", "down", "up", "gate", "d_gate", "d_up")})
    live["sums"] = line_sum_second(live["sums"])
    if pairs:
        *quarters, across = live["down"]
        live["down"] = [*quarters, *fold_first(across)]
    live["up"] = product(normed_two, live["d_up"], swap(live["up"], "c", 1))
    live = close({k: live[k] for k in ("sums", "down", "up", "gate", "d_gate")})

    d_normed_two = line_total(live["sums"])
    gain_three = jnp.sum(d_normed_two * unit_three, axis=0)
    d_hidden = out_cotan + norm_back(d_normed_two * ffn_gain, unit_three, inverse_three)
    gain_two = jnp.sum(d_hidden * unit_two, axis=0)
    d_branch = norm_back(d_hidden * attn_post_gain, unit_two, inverse_two).astype(BF)
    live["d_branch"] = [d_branch, swap(d_branch, "x", 1)]
    live["gate"] = product(normed_two, live["d_gate"], swap(live["gate"], "c", 1))
    if pairs:
        own, over_x, over_y, *got = live["down"]
        over_x, over_y = fold_join({"x": over_x, "y": over_y}, got)
        live["down"] = [own, over_x, swap(over_y, "y", 1)]
    else:
        live |= {name: [sum_cut(*live[name])] for name in ("down", "up", "gate")}
    live = close({k: live[k] for k in ("d_branch", "up", "down", "gate")})
    d_branch = pair_gather(*live["d_branch"])

    if pairs:
        own, over_x, got = live["down"]
        live["down"] = [own, got, swap(over_x, "x", 1)]
        own, over_x, over_y, across = live["up"]
        live["up"] = [own, over_x, over_y, swap(across, "y", 1)]
    live = {k: live[k] for k in ("up", "down", "gate")}
    d_qkv, d_sent, d_kept = attention_back_call(
        ids, d_branch, out_weight, qkv_weight, query, key, value, cosine, sine, allowed, kv_here
    )
    live["d_normed_one"] = [d_kept, d_sent]
    if pairs:
        live["rows"] = outer_rows(ids, core_there, normed_one, d_qkv, d_branch, attended)
    else:
        rows = [outer_dot(normed_one, d_qkv), outer_dot(d_branch, attended)]
        live["rows"] = jnp.concatenate(rows, axis=1).astype(BF)
    live = close(live | {"d_qkv": d_qkv})

    if pairs:
        products = (normed_one, live["d_qkv"], d_branch, attended)
        live["rows"] = outer_rows(ids, core_here, *products, swap(live["rows"], "c", 1))
        own, over_x, over_y, got = live["up"]
        live["up"] = [own, swap(add_low(over_x, got), "x", 1), swap(over_y, "y", 1)]
    live["down"] = line_swaps(line_chunks(line_total(live["down"]).astype(BF)))
    live = close({k: live[k] for k in ("rows", "up", "down", "gate", "d_normed_one")})
    grad_down = line_columns(live.pop("down"))

    live["up"] = line_swaps(line_chunks(line_total(live["up"]).astype(BF)))
    if pairs:
        own, over_x, over_y, across = live["gate"]
        live["gate"] = [own, over_x, over_y, swap(across, "x", 1)]
        far_sent, near_sent, far, near = live["rows"]
        live["rows"] = [near_sent, add_low(far, swap(far_sent, "y", 1)), near]
    live = close(live)
    grad_up = line_columns(live.pop("up"))
    d_kept, d_sent = live["d_normed_one"]
    live["d_normed_one"] = [d_kept, swap(d_sent, "x", 1)]
    if pairs:
        near_sent, far, near = live["rows"]
        live["rows"] = [near, swap(near_sent, "y", 1), swap(far, "z", 1)]
        own, over_x, over_y, got = live["gate"]
        live["gate"] = [own, swap(over_x, "x", 1), over_y, got]
    live = close(live)

    d_normed_one = live["d_normed_one"][0] + live["d_normed_one"][1].astype(F32)
    gain_one = jnp.sum(d_normed_one * unit_one, axis=0)
    grad_tokens = d_hidden + norm_back(d_normed_one * attn_gain, unit_one, inverse_one)
    gains = jnp.stack([gain_one, gain_two, gain_three, gain_four], axis=0)
    rows = live["rows"]
    if pairs:
        far = line_total([part[shard:] for part in rows]).astype(BF)
        own, got_x, over_y, got = live["gate"]
        gate = [own, got_x, swap(add_low(over_y, got), "y", 1)]
        rows = [part[:shard] for part in rows] + [swap(far, "z", 2)]
    else:
        gate = live["gate"]
    live = close({"rows": rows, "gate": gate, "gains": sum_over_y(gain_sum(gains))})
    gains = live["gains"]

    grad_gate = line_total(live["gate"]).astype(BF)
    grad_gate = line_columns(line_swaps(line_chunks(grad_gate)))
    if pairs:
        grad_rows = line_total(live["rows"])
    else:
        grad_rows = lax.psum_scatter(live["rows"], row_axes, scatter_dimension=0, tiled=True)
        grad_rows = grad_rows.astype(F32)
    out_from = grad_rows.shape[1] - attended.shape[1]
    grad_qkv, grad_out = grad_rows[:, :out_from], grad_rows[:, out_from:]
    cols = grad_qkv.shape[1] // kv_here
    cuts = (0, cols - 2 * HD, cols - HD, cols)
    grad_query, grad_key, grad_value = (
        jnp.concatenate(
            [grad_qkv[:, g * cols + cuts[i] : g * cols + cuts[i + 1]] for g in range(kv_here)],
            axis=1,
        )
        for i in range(3)
    )
    return (
        outward(mixed),
        outward(grad_tokens),
        gains[0],
        grad_query,
        grad_key,
        grad_value,
        grad_out.T,
        gains[1],
        gains[2],
        grad_gate,
        grad_up,
        grad_down.T,
        gains[3],
    )


def solution(mesh):
    count, pair = mesh.devices.shape
    grid = Mesh(mesh.devices.reshape(4, count // 8, 2, pair), ("z", "y", "c", "x"))
    rows = ("z", "y", "c")
    return jax.shard_map(
        on_device,
        mesh=grid,
        in_specs=(
            P(rows + ("x",), None),
            P(rows, None),
            P(rows, None),
            P(),
            P(rows, "x"),
            P(rows, "x"),
            P(rows, "x"),
            P("x", rows),
            P(),
            P(),
            P(rows, "x"),
            P(rows, "x"),
            P("x", rows),
            P(),
            P(rows + ("x",), None),
        ),
        out_specs=(
            P(rows + ("x",), None),
            P(rows + ("x",), None),
            P(rows),
            P(rows, "x"),
            P(rows, "x"),
            P(rows, "x"),
            P("x", rows),
            P(rows),
            P(rows),
            P(rows, "x"),
            P(rows, "x"),
            P("x", rows),
            P(rows),
        ),
        check_vma=False,
    )
```

```python
import functools

import jax
import jax.numpy as jnp
from jax import lax
from jax.experimental import pallas as pl
from jax.experimental.pallas import tpu as pltpu
from jax.sharding import Mesh
from jax.sharding import PartitionSpec as P

HD = 256
NORM_EPS = 1e-06
SOFT_CAP = 50.0
ROPE_BASE = 10000.0
MASK_FILL = -1e30
BF = jnp.bfloat16
F32 = jnp.float32


def tree_tables(lengths_row, parents_row, row_total):
    seg_count = lengths_row.shape[0]
    seg_index = jnp.arange(seg_count, dtype=jnp.int32)
    ancestor = (seg_index[:, None] == seg_index[None, :]) | (
        parents_row[:, None] == seg_index[None, :]
    )
    for repeat in range(seg_count.bit_length()):
        ancestor = jnp.any(ancestor[:, :, None] & ancestor[None, :, :], axis=1)
    seg_ends = jnp.cumsum(lengths_row)
    seg_starts = seg_ends - lengths_row
    token_index = jnp.arange(row_total, dtype=jnp.int32)
    segment = jnp.sum((token_index[:, None] >= seg_ends[None, :]).astype(jnp.int32), axis=1)
    strict = ancestor & (seg_index[:, None] != seg_index[None, :])
    offsets = jnp.sum(jnp.where(strict, lengths_row[None, :], 0), axis=1)
    one_hot = segment[:, None] == seg_index[None, :]
    positions = (
        jnp.sum(jnp.where(one_hot, (offsets - seg_starts)[None, :], 0), axis=1) + token_index
    )
    reached = jnp.any(one_hot[:, :, None] & ancestor[None, :, :], axis=1)
    allowed = jnp.any(reached[:, None, :] & one_hot[None, :, :], axis=2) & (
        token_index[None, :] <= token_index[:, None]
    )
    return (positions, allowed)


def rope_tables(positions, width):
    half_width = width // 2
    frequency = ROPE_BASE ** (-2.0 * jnp.arange(half_width, dtype=F32) / width)
    angles = positions.astype(F32)[:, None] * frequency[None, :]
    return (jnp.cos(angles), jnp.sin(angles))


def norm_back(grad_unit, unit, inverse):
    return inverse * (grad_unit - unit * jnp.mean(grad_unit * unit, axis=-1, keepdims=True))


def gelu_parts(values):
    scale = (2.0 / jnp.pi) ** 0.5
    square = values * values
    bent = jnp.tanh(scale * (values + 0.044715 * values * square))
    half = 0.5 * (1.0 + bent)
    slope = half + 0.5 * values * (1.0 - bent * bent) * scale * (1.0 + 3 * 0.044715 * square)
    return values * half, slope


def tile_dot(left, right):
    return jnp.dot(left, right, preferred_element_type=F32)


def tile_dot_cols(left, right):
    return lax.dot_general(left, right, (((1,), (1,)), ((), ())), preferred_element_type=F32)


def spill(ids, total, outs):
    rows = outs[0].shape[0]
    for k, out in enumerate(outs):
        out[...] = total[k * rows : (k + 1) * rows, :].astype(out.dtype)


class Weight:
    def __init__(self, *arrays):
        self.arrays, self.whole = arrays, len(arrays) == 1
        self.rows = arrays[0].shape[-2]

    def specs(self, tile):
        if not self.whole:
            return [pl.BlockSpec((self.rows, tile), lambda i, ids: (0, i))] * 2
        count = self.arrays[0].shape[-1] // tile
        return [pl.BlockSpec((None, self.rows, tile), lambda i, ids: (i // count, 0, i % count))]

    def columns(self, ids):
        if self.whole:
            return (pl.ds(0, self.rows),)
        starts = (pl.multiple_of(core * self.rows, 128) for core in (ids[2], 1 - ids[2]))
        return tuple(pl.ds(start, self.rows) for start in starts)


def inner(values, refs, columns):
    return sum(tile_dot(values[:, at], ref[...]) for ref, at in zip(refs, columns))


def outer_add(total, tile, refs, columns, fresh):
    for ref, at in zip(refs, columns):
        part = tile_dot_cols(tile, ref[...])
        total[:, at] = jnp.where(fresh, part, total[:, at] + part)


def up_kernel(columns, ids, x, *refs):
    gate_w, up_w, (act, gate, up) = refs[:2], refs[2:4], refs[4:]
    gate_at, up_at = (find(ids) for find in columns)
    gate_tile, up_tile = inner(x, gate_w, gate_at), inner(x, up_w, up_at)
    gate[...], up[...] = gate_tile, up_tile
    act[...] = (gelu_parts(gate_tile)[0] * up_tile).astype(BF)


def down_kernel(columns, ids, act, *refs):
    down_w, outs, total = refs[:1], refs[1:-1], refs[-1]
    outer_add(total, act[...], down_w, columns[0](ids), pl.program_id(0) == 0)

    @pl.when(pl.program_id(0) == pl.num_programs(0) - 1)
    def _():
        spill(ids, total, outs)


def backward_kernel(columns, ids, d, *refs):
    gate_w, up_w, down_w, (gate, up), (d_gate, d_up), outs, total = (
        refs[:2], refs[2:4], refs[4:5], refs[5:7], refs[7:9], refs[9:-1], refs[-1]
    )
    gate_at, up_at, down_at = (find(ids) for find in columns)
    d_act = inner(d, down_w, down_at)
    bent, slope = gelu_parts(gate[...])
    gate_tile = (d_act * up[...] * slope).astype(BF)
    up_tile = (d_act * bent).astype(BF)
    d_gate[...], d_up[...] = gate_tile, up_tile
    outer_add(total, gate_tile, gate_w, gate_at, pl.program_id(0) == 0)
    outer_add(total, up_tile, up_w, up_at, False)

    @pl.when(pl.program_id(0) == pl.num_programs(0) - 1)
    def _():
        spill(ids, total, outs)


def ffn_call(kernel, ids, values, weights, kept, made, tile, width):
    tokens = (values or kept)[0].shape[0]
    cols = weights[-1].arrays[0].shape[-1]
    hidden = 2 * cols if weights[-1].whole else cols
    across = pl.BlockSpec((tokens, tile), lambda i, ids: (0, i))
    parts = [F32, BF, BF, BF] if width else []
    return pl.pallas_call(
        functools.partial(kernel, [weight.columns for weight in weights]),
        grid_spec=pltpu.PrefetchScalarGridSpec(
            num_scalar_prefetch=1,
            grid=(hidden // tile,),
            in_specs=[pl.BlockSpec(array.shape, lambda i, ids: (0, 0)) for array in values]
            + ([] if values else [across] * len(kept))
            + [spec for weight in weights for spec in weight.specs(tile)]
            + ([across] * len(kept) if values else []),
            out_specs=[across] * len(made)
            + [pl.BlockSpec((tokens // 4, width), lambda i, ids: (0, 0)) for _ in parts],
            scratch_shapes=[pltpu.VMEM((tokens, width), F32)] if width else [],
        ),
        out_shape=[jax.ShapeDtypeStruct((tokens, hidden), kind) for kind in made]
        + [jax.ShapeDtypeStruct((tokens // 4, width), kind) for kind in parts],
        compiler_params=pltpu.CompilerParams(
            dimension_semantics=("arbitrary",), vmem_limit_bytes=58 * 2**20
        ),
        cost_estimate=pl.CostEstimate(flops=0, bytes_accessed=0, transcendentals=0),
    )(
        ids,
        *values,
        *([] if values else kept),
        *[array for weight in weights for array in weight.arrays],
        *(kept if values else []),
    )


def swap(values, axis, mask):
    size = lax.axis_size(axis)
    return lax.ppermute(values, axis, [(i, i ^ mask) for i in range(size)])


def rows_dot(left, right):
    return lax.dot_general(left, right, (((1,), (0,)), ((), ())), preferred_element_type=F32)


def cols_dot(left, right):
    return lax.dot_general(left, right, (((1,), (1,)), ((), ())), preferred_element_type=F32)


def outer_dot(left, right):
    return lax.dot_general(left, right, (((0,), (0,)), ((), ())), preferred_element_type=F32)


def close(live):
    return lax.optimization_barrier(live)


def pair_gather(values, other):
    mine = lax.axis_index("x")
    first = jnp.where(mine == 0, values, other)
    second = jnp.where(mine == 0, other, values)
    return jnp.concatenate([first, second], axis=0)


def pair_parts(partial):
    rows = partial.shape[0] // 2
    mine = lax.axis_index("x")
    sent = lax.dynamic_slice_in_dim(partial, (1 - mine) * rows, rows, 0).astype(BF)
    return sent, lax.dynamic_slice_in_dim(partial, mine * rows, rows, 0)


def pair_sum(partial):
    sent, kept = pair_parts(partial)
    return kept + swap(sent, "x", 1).astype(F32)


def rows_sum(values, axis):
    size = lax.axis_size(axis)
    if size != 2:
        return lax.psum_scatter(values, axis, scatter_dimension=0, tiled=True)
    rows, mine = values.shape[0] // 2, lax.axis_index(axis)
    sent = lax.dynamic_slice_in_dim(values, (1 - mine) * rows, rows, 0)
    return add_low(lax.dynamic_slice_in_dim(values, mine * rows, rows, 0), swap(sent, axis, 1))


def placed(rows, *pieces):
    held = jnp.zeros((rows,) + pieces[0][1].shape[1:], pieces[0][1].dtype)
    for offset, piece in pieces:
        held = lax.dynamic_update_slice_in_dim(held, piece, offset, 0)
    return held


def add_low(left, right):
    return (left.astype(F32) + right.astype(F32)).astype(BF)


def line_gather(values):
    near, far = swap(values, "z", 1), swap(values, "z", 2)
    return jnp.concatenate([values, near, far, swap(far, "z", 1)], axis=0)


def line_sum_first(parts):
    return [*parts[:3], swap(parts[3], "z", 1)]


def line_sum_second(parts):
    return [parts[0], swap(parts[1], "z", 1), swap(add_low(parts[2], parts[3]), "z", 2)]


def line_place(pieces):
    here, (rows, cols) = lax.axis_index("z"), pieces[0].shape
    if rows % 16 == 0:
        return assemble(
            (len(pieces) * rows, cols), (rows, cols), [(here ^ k, 0, p) for k, p in enumerate(pieces)]
        )
    return placed(len(pieces) * rows, *[((here ^ k) * rows, p) for k, p in enumerate(pieces)])


def line_cuts(weight):
    here, cut = lax.axis_index("z"), weight.shape[1] // 4
    return [lax.dynamic_slice_in_dim(weight, (here ^ k) * cut, cut, 1) for k in range(4)]


def line_swaps(cuts):
    return [cuts[0]] + [swap(cuts[k], "z", k) for k in (1, 2, 3)]


def line_chunks(grad):
    rows, here = grad.shape[0] // 4, lax.axis_index("z")
    return [lax.dynamic_slice_in_dim(grad, (here ^ k) * rows, rows, 0) for k in range(4)]


def line_columns(pieces):
    here, (rows, cols) = lax.axis_index("z"), pieces[0].shape
    spots = [(0, here ^ k, piece) for k, piece in enumerate(pieces)]
    return assemble((rows, 4 * cols), (rows, cols), spots, F32)


def line_total(pieces):
    total = pieces[0].astype(F32)
    for piece in pieces[1:]:
        total = total + piece.astype(F32)
    return total


def y_chunks(grad):
    rows, y, z = grad.shape[0] // 8, lax.axis_index("y"), lax.axis_index("z")
    return [
        tuple(
            lax.dynamic_slice_in_dim(grad, (4 * side + (z ^ k)) * rows, rows, 0)
            for side in (y, 1 - y)
        )
        for k in range(4)
    ]


def pair_rows(mine, other, axis):
    rows, here = mine.shape[0], lax.axis_index(axis)
    return placed(2 * rows, (here * rows, mine), ((1 - here) * rows, other))


def pair_halves(values, axis):
    rows, here = values.shape[0] // 2, lax.axis_index(axis)
    return (
        lax.dynamic_slice_in_dim(values, here * rows, rows, 0),
        lax.dynamic_slice_in_dim(values, (1 - here) * rows, rows, 0),
    )


def cut_first(own):
    got = {"own": own, "x": swap(own, "x", 1)}
    if lax.axis_size("y") == 2:
        got["y"] = swap(own, "y", 1)
    return got


def cut_over_x(got):
    rows = got["own"].shape[0] // 2
    return {"over_x": swap(got["y"][:rows], "x", 1)} if "y" in got else {}


def cut_over_y(got):
    rows = got["own"].shape[0] // 2
    return {"over_y": swap(got["x"][rows:], "y", 1)} if "y" in got else {}


def cut_half(got):
    own = got["own"]
    rows, cols = own.shape
    if "y" not in got:
        both = jnp.where(
            lax.axis_index("x") == 0,
            jnp.concatenate([own, got["x"]], axis=1),
            jnp.concatenate([got["x"], own], axis=1),
        )
        return lax.all_gather(both, "y", axis=0, tiled=True)
    here, half = lax.axis_index("y"), lax.axis_index("x")
    mine, far = 2 * here, 2 * (1 - here)
    spots = [
        (mine, half, own),
        (far, half, got["y"]),
        (mine, 1 - half, got["x"]),
        (far, 1 - half, got["over_x"]),
        (far + 1, 1 - half, got["over_y"]),
    ]
    return assemble((2 * rows, 2 * cols), (rows // 2, cols), spots)


def fold_parts(both):
    cols, here = both.shape[1] // 2, lax.axis_index("x")
    mine = lax.dynamic_slice_in_dim(both, here * cols, cols, 1)
    other = lax.dynamic_slice_in_dim(both, (1 - here) * cols, cols, 1)
    (own, over_y), (over_x, across) = pair_halves(mine, "y"), pair_halves(other, "y")
    return {"own": own, "x": over_x, "y": over_y, "across": across}


def fold_first(across, rows):
    return [swap(across[:rows], "x", 1), swap(across[rows:], "y", 1)]


def fold_join(parts, got):
    rows = got[0].shape[0]
    over_y = add_low(parts["y"][:rows], got[0])
    over_x = add_low(parts["x"][rows:], got[1])
    return (
        jnp.concatenate([parts["x"][:rows], over_x]),
        jnp.concatenate([over_y, parts["y"][rows:]]),
    )


def spread_ids():
    return jnp.stack([lax.axis_index(axis) for axis in ("z", "y", "c", "x")]).astype(jnp.int32)


LIGHT = pl.CostEstimate(flops=0, bytes_accessed=0, transcendentals=0)


def kernel_params(megabytes=50):
    return pltpu.CompilerParams(
        dimension_semantics=("arbitrary",), vmem_limit_bytes=megabytes * 2**20
    )


def turned(values, cosine, sine):
    half = values.shape[1] // 2
    front, back = values[:, :half], values[:, half:]
    return jnp.concatenate([front * cosine - back * sine, back * cosine + front * sine], axis=1)


def head_probs(query, key, allowed):
    scores = tile_dot_cols(query, key)
    bent = jnp.tanh(scores * (HD**-0.5 / SOFT_CAP))
    masked = jnp.where(allowed != 0, SOFT_CAP * bent, MASK_FILL)
    weights = jnp.exp(masked - jnp.max(masked, axis=1, keepdims=True))
    return bent, weights / jnp.sum(weights, axis=1, keepdims=True)


def attention_kernel(x, weight, cosine, sine, allowed, query, key, value, attended):
    heads = query.shape[1] // HD
    proj = tile_dot(x[...], weight[...])
    key_here = turned(proj[:, heads * HD : (heads + 1) * HD], cosine[...], sine[...]).astype(BF)
    value_here = proj[:, (heads + 1) * HD :].astype(BF)
    key[...], value[...] = key_here, value_here
    for head in range(heads):
        at = slice(head * HD, (head + 1) * HD)
        query_here = turned(proj[:, at], cosine[...], sine[...]).astype(BF)
        query[:, at] = query_here
        probs = head_probs(query_here, key_here, allowed[...])[1].astype(BF)
        attended[:, at] = tile_dot(probs, value_here).astype(BF)


def attention_call(x, weight, cosine, sine, allowed, groups):
    tokens, width = x.shape
    cols = weight.shape[1] // groups
    heads = cols // HD - 2

    def here(cut):
        return pl.BlockSpec((tokens, cut), lambda g: (0, g))

    def whole(values):
        return pl.BlockSpec(values.shape, lambda g: (0, 0))

    cuts = [heads * HD, HD, HD, heads * HD]
    return pl.pallas_call(
        attention_kernel,
        grid=(groups,),
        in_specs=[
            whole(x),
            pl.BlockSpec((width, cols), lambda g: (0, g)),
            whole(cosine),
            whole(sine),
            whole(allowed),
        ],
        out_specs=[here(cut) for cut in cuts],
        out_shape=[jax.ShapeDtypeStruct((tokens, groups * cut), BF) for cut in cuts],
        compiler_params=kernel_params(),
        cost_estimate=LIGHT,
    )(x, weight, cosine, sine, allowed)


def share(ids, total, sent, kept):
    rows = sent.shape[0]
    here = ids[3]
    sent[...] = total[pl.ds(pl.multiple_of((1 - here) * rows, rows), rows), :].astype(BF)
    kept[...] = total[pl.ds(pl.multiple_of(here * rows, rows), rows), :]


def branch_kernel(ids, attended, weight, sent, kept, total):
    part = tile_dot_cols(attended[...], weight[...])
    total[...] = jnp.where(pl.program_id(0) == 0, part, total[...] + part)

    @pl.when(pl.program_id(0) == pl.num_programs(0) - 1)
    def _():
        share(ids, total, sent, kept)


def branch_call(ids, attended, weight):
    tokens, cols = attended.shape
    width = weight.shape[0]
    tile = 512
    half = pl.BlockSpec((tokens // 2, width), lambda g, ids: (0, 0))
    return pl.pallas_call(
        branch_kernel,
        grid_spec=pltpu.PrefetchScalarGridSpec(
            num_scalar_prefetch=1,
            grid=(cols // tile,),
            in_specs=[
                pl.BlockSpec((tokens, tile), lambda g, ids: (0, g)),
                pl.BlockSpec((width, tile), lambda g, ids: (0, g)),
            ],
            out_specs=[half, half],
            scratch_shapes=[pltpu.VMEM((tokens, width), F32)],
        ),
        out_shape=[jax.ShapeDtypeStruct((tokens // 2, width), kind) for kind in (BF, F32)],
        compiler_params=kernel_params(),
        cost_estimate=LIGHT,
    )(ids, attended, weight)


def attention_back_kernel(
    ids, d, out, weight, query, key, value, cosine, sine, allowed, d_qkv, sent, kept, total
):
    heads = query.shape[1] // HD
    key_here, value_here = key[...], value[...]
    d_attended = tile_dot(d[...], out[...]).astype(BF)
    d_key = d_value = 0.0
    pieces = []
    for head in range(heads):
        at = slice(head * HD, (head + 1) * HD)
        query_here, d_here = query[:, at], d_attended[:, at]
        bent, probs = head_probs(query_here, key_here, allowed[...])
        d_probs = tile_dot_cols(d_here, value_here)
        inner = jnp.sum(probs * d_probs, axis=1, keepdims=True)
        d_scores = probs * (d_probs - inner) * (HD**-0.5) * (1.0 - bent * bent)
        d_scores = d_scores.astype(BF)
        d_query = tile_dot(d_scores, key_here)
        pieces.append(turned(d_query, cosine[...], -sine[...]).astype(BF))
        d_key = d_key + outer_dot(d_scores, query_here)
        d_value = d_value + outer_dot(probs.astype(BF), d_here)
    pieces.append(turned(d_key, cosine[...], -sine[...]).astype(BF))
    pieces.append(d_value.astype(BF))
    made = jnp.concatenate(pieces, axis=1)
    d_qkv[...] = made
    part = tile_dot_cols(made, weight[...])
    total[...] = jnp.where(pl.program_id(0) == 0, part, total[...] + part)

    @pl.when(pl.program_id(0) == pl.num_programs(0) - 1)
    def _():
        share(ids, total, sent, kept)


def attention_back_call(ids, d, out, weight, query, key, value, cosine, sine, allowed, groups):
    tokens, width = d.shape
    cols = weight.shape[1] // groups
    heads = cols // HD - 2

    def here(rows, cut):
        return pl.BlockSpec((rows, cut), lambda g, ids: (0, g))

    def whole(values):
        return pl.BlockSpec(values.shape, lambda g, ids: (0, 0))

    half = pl.BlockSpec((tokens // 2, width), lambda g, ids: (0, 0))
    return pl.pallas_call(
        attention_back_kernel,
        grid_spec=pltpu.PrefetchScalarGridSpec(
            num_scalar_prefetch=1,
            grid=(groups,),
            in_specs=[
                whole(d),
                here(width, heads * HD),
                here(width, cols),
                here(tokens, heads * HD),
                here(tokens, HD),
                here(tokens, HD),
                whole(cosine),
                whole(sine),
                whole(allowed),
            ],
            out_specs=[here(tokens, cols), half, half],
            scratch_shapes=[pltpu.VMEM((tokens, width), F32)],
        ),
        out_shape=[
            jax.ShapeDtypeStruct((tokens, groups * cols), BF),
            jax.ShapeDtypeStruct((tokens // 2, width), BF),
            jax.ShapeDtypeStruct((tokens // 2, width), F32),
        ],
        compiler_params=kernel_params(),
        cost_estimate=LIGHT,
    )(ids, d, out, weight, query, key, value, cosine, sine, allowed)


def outer_kernel(which, left, right, *rest):
    got, (made, flipped) = rest[:-2], rest[-2:]

    @pl.when(pl.program_id(0) == 0)
    def _():
        flipped[...] = left[...].T

    total = tile_dot(flipped[...], right[...])
    for piece in got:
        total = total + piece[...].astype(F32)
    made[...] = total.astype(BF)


def outer_call(left, right, which, *got):
    tokens, cut, cols = left.shape[0], left.shape[1] // 2, right.shape[1]
    tile = cols // 2
    across = pl.BlockSpec((cut, tile), lambda i, which: (0, i))
    return pl.pallas_call(
        outer_kernel,
        grid_spec=pltpu.PrefetchScalarGridSpec(
            num_scalar_prefetch=1,
            grid=(cols // tile,),
            in_specs=[
                pl.BlockSpec((tokens, cut), lambda i, which: (0, which[0])),
                pl.BlockSpec((tokens, tile), lambda i, which: (0, i)),
            ]
            + [across] * len(got),
            out_specs=across,
            scratch_shapes=[pltpu.VMEM((cut, tokens), BF)],
        ),
        out_shape=jax.ShapeDtypeStruct((cut, cols), BF),
        compiler_params=kernel_params(),
        cost_estimate=LIGHT,
    )(which, left, right, *got)


def outer_halves_kernel(number, which, left, *refs):
    rights, got, (made, flipped) = refs[:number], refs[number:-2], refs[-2:]
    step = pl.program_id(0)

    @pl.when(step == 0)
    def _():
        flipped[...] = left[...].T

    for k, right in enumerate(rights):

        @pl.when(step % number == k)
        def _(right=right):
            total = tile_dot(flipped[...], right[...])
            for piece in got:
                total = total + piece[...].astype(F32)
            made[...] = total.astype(BF)


def outer_halves(which, left, rights, *got):
    tokens, cut = left.shape[0], left.shape[1] // 2
    cols, number = rights[0].shape[1] // 2, len(rights)
    across = pl.BlockSpec((None, cut, cols), lambda i, which: (i // number, 0, i % number))
    return pl.pallas_call(
        functools.partial(outer_halves_kernel, number),
        grid_spec=pltpu.PrefetchScalarGridSpec(
            num_scalar_prefetch=1,
            grid=(2 * number,),
            in_specs=[pl.BlockSpec((tokens, cut), lambda i, which: (0, which[0]))]
            + [pl.BlockSpec((tokens, cols), lambda i, which: (0, i // number))] * number
            + [across] * len(got),
            out_specs=across,
            scratch_shapes=[pltpu.VMEM((cut, tokens), BF)],
        ),
        out_shape=jax.ShapeDtypeStruct((2, cut, number * cols), BF),
        compiler_params=kernel_params(),
        cost_estimate=LIGHT,
    )(which, left, *rights, *got)


def sum_cut(grad):
    half, cols = grad.shape[1:]
    blocks = 2 * lax.axis_size("y")
    grad = grad.reshape(blocks, 2 * half // blocks, cols)
    return lax.psum_scatter(grad, ("x", "y"), scatter_dimension=0, tiled=True)[0]


def gather_cut(own):
    whole = lax.all_gather(own, ("x", "c", "y"), axis=0, tiled=True)
    return whole.reshape(2, -1, own.shape[1])


def outer_low(left, right, mine, theirs):
    sent = outer_call(left, right, theirs)
    return outer_call(left, right, mine, swap(sent, "c", 1))


def outer_quarters_kernel(ids, which, left, right, *refs):
    (plain, flipped), refs = refs[-2:], refs[:-2]
    got, outs = (refs[:4], refs[4:]) if len(refs) > 1 else ((), refs)
    step, rows = pl.program_id(0), flipped.shape[0] // 2

    @pl.when(step == 0)
    def _():
        plain[...] = left[...].T
        for k, side in enumerate((ids[1], 1 - ids[1])):
            at = pl.multiple_of(side * rows, rows)
            flipped[k * rows : (k + 1) * rows, :] = plain[pl.ds(at, rows), :]

    for half in range(2):

        @pl.when(step % 2 == half)
        def _(half=half):
            for side in range(2):
                k = half + 2 * side
                total = tile_dot(flipped[side * rows : (side + 1) * rows, :], right[...])
                if got:
                    outs[k][...] = (total + got[k][...].astype(F32)).astype(BF)
                else:
                    outs[0][side] = total.astype(BF)


def outer_quarters(ids, which, left, right, *got, place=0):
    tokens, cut, cols = left.shape[0], left.shape[1] // 2, right.shape[1] // 2
    rows = cut // 2
    quarter = pl.BlockSpec((rows, cols), lambda i, ids, which: (0, 0))
    taken = [
        pl.BlockSpec((None, rows, cols), lambda i, ids, which, k=k: (2 * place + k // 2, 0, k % 2))
        for k in range(4)
    ]
    shape = jax.ShapeDtypeStruct((rows, cols), BF)
    return pl.pallas_call(
        outer_quarters_kernel,
        grid_spec=pltpu.PrefetchScalarGridSpec(
            num_scalar_prefetch=2,
            grid=(2,),
            in_specs=[
                pl.BlockSpec((tokens, cut), lambda i, ids, which: (0, which[0])),
                pl.BlockSpec((tokens, cols), lambda i, ids, which: (0, ids[3] ^ i)),
            ]
            + (taken if got else []),
            out_specs=[quarter] * 4
            if got
            else pl.BlockSpec((2, rows, cols), lambda i, ids, which: (0, 0, i)),
            scratch_shapes=[pltpu.VMEM((cut, tokens), BF)] * 2,
        ),
        out_shape=[shape] * 4 if got else jax.ShapeDtypeStruct((2, rows, 2 * cols), BF),
        compiler_params=kernel_params(),
        cost_estimate=LIGHT,
    )(ids, which, left, right, *got * 4)


def outer_pair_kernel(ids, which, left, right_a, right_b, made, plain, flipped):
    step, rows = pl.program_id(0), flipped.shape[0] // 2

    @pl.when(step == 0)
    def _():
        plain[...] = left[...].T
        for k, side in enumerate((ids[1], 1 - ids[1])):
            at = pl.multiple_of(side * rows, rows)
            flipped[k * rows : (k + 1) * rows, :] = plain[pl.ds(at, rows), :]

    for k, right in enumerate((right_a, right_b)):

        @pl.when(step // 2 == k)
        def _(right=right):
            for side in range(2):
                at = slice(side * rows, (side + 1) * rows)
                made[side] = tile_dot(flipped[at, :], right[...]).astype(BF)


def outer_pair(ids, which, left, right_a, right_b):
    tokens, cut, cols = left.shape[0], left.shape[1] // 2, right_a.shape[1] // 2
    rows = cut // 2
    return pl.pallas_call(
        outer_pair_kernel,
        grid_spec=pltpu.PrefetchScalarGridSpec(
            num_scalar_prefetch=2,
            grid=(4,),
            in_specs=[
                pl.BlockSpec((tokens, cut), lambda i, ids, which: (0, which[0])),
                pl.BlockSpec((tokens, cols), lambda i, ids, which: (0, ids[3] ^ jnp.minimum(i, 1))),
                pl.BlockSpec(
                    (tokens, cols), lambda i, ids, which: (0, ids[3] ^ jnp.maximum(i - 2, 0))
                ),
            ],
            out_specs=pl.BlockSpec((2, rows, cols), lambda i, ids, which: (i // 2, 0, i % 2)),
            scratch_shapes=[pltpu.VMEM((cut, tokens), BF)] * 2,
        ),
        out_shape=jax.ShapeDtypeStruct((4, rows, 2 * cols), BF),
        compiler_params=kernel_params(),
        cost_estimate=LIGHT,
    )(ids, which, left, right_a, right_b)


def outer_rows_kernel(ids, which, left_a, left_b, right_a, right_b, *refs):
    (plain, flipped), refs = refs[-2:], refs[:-2]
    got, outs = (refs[:4], refs[4:]) if len(refs) > 1 else ((), refs)
    step, last = pl.program_id(0), pl.num_programs(0) - 1
    rows = flipped.shape[0] // 8
    z, y = ids[0], ids[1]
    order = [4 * side + (z ^ k) for side in (1 - y, y) for k in (1, 3, 0, 2)]
    for left, when in ((left_a, 0), (left_b, last)):

        @pl.when(step == when)
        def _(left=left):
            plain[...] = left[...].T
            for k, block in enumerate(order):
                at = pl.multiple_of(block * rows, rows)
                flipped[k * rows : (k + 1) * rows, :] = plain[pl.ds(at, rows), :]

    def give(right):
        total = tile_dot(flipped[...], right[...])
        if not got:
            outs[0][...] = total.astype(BF)
        for k, piece in enumerate(got):
            part = total[2 * k * rows : (2 * k + 2) * rows, :]
            outs[k][...] = (part + piece[...].astype(F32)).astype(BF)

    @pl.when(step < last)
    def _():
        give(right_a)

    @pl.when(step == last)
    def _():
        give(right_b)


def outer_rows(ids, which, left_a, right_a, left_b, right_b, *got):
    tokens, cut = left_a.shape[0], left_a.shape[1] // 2
    tile = right_b.shape[1]
    cols = right_a.shape[1] + tile
    rows = cut // 4
    count = cols // tile
    half = pl.BlockSpec((tokens, cut), lambda i, ids, which: (0, which[0]))
    across = pl.BlockSpec((rows, tile), lambda i, ids, which: (0, i))
    taken = [pl.BlockSpec((rows, tile), lambda i, ids, which, k=k: (k, i)) for k in range(4)]
    return pl.pallas_call(
        outer_rows_kernel,
        grid_spec=pltpu.PrefetchScalarGridSpec(
            num_scalar_prefetch=2,
            grid=(count,),
            in_specs=[
                half,
                half,
                pl.BlockSpec((tokens, tile), lambda i, ids, which: (0, jnp.minimum(i, count - 2))),
                pl.BlockSpec((tokens, tile), lambda i, ids, which: (0, 0)),
            ]
            + (taken if got else []),
            out_specs=[across] * 4
            if got
            else pl.BlockSpec((cut, tile), lambda i, ids, which: (0, i)),
            scratch_shapes=[pltpu.VMEM((cut, tokens), BF)] * 2,
        ),
        out_shape=[jax.ShapeDtypeStruct((rows, cols), BF)] * 4
        if got
        else jax.ShapeDtypeStruct((cut, cols), BF),
        compiler_params=kernel_params(),
        cost_estimate=LIGHT,
    )(ids, which, left_a, left_b, right_a, right_b, *got * 4)


def assemble_kernel(counts, rows, cols, *refs):
    pieces, made = refs[:-1], refs[-1]
    step, first = pl.program_id(0), 0
    for piece, count in zip(pieces, counts):

        @pl.when((step >= first) & (step < first + count))
        def _(piece=piece):
            made[...] = piece[...].astype(made.dtype)

        first += count


def assemble(shape, block, placed, kind=BF):
    counts = [array.shape[0] // block[0] for _, _, array in placed]
    steps = [(row + k, col) for (row, col, _), n in zip(placed, counts) for k in range(n)]
    rows, cols = (jnp.stack([jnp.asarray(s[i], jnp.int32) for s in steps]) for i in range(2))
    specs, first = [], 0
    for count in counts:

        def at(step, rows, cols, first=first, count=count):
            return (jnp.clip(step - first, 0, count - 1), 0)

        specs.append(pl.BlockSpec(block, at))
        first += count
    return pl.pallas_call(
        functools.partial(assemble_kernel, counts),
        grid_spec=pltpu.PrefetchScalarGridSpec(
            num_scalar_prefetch=2,
            grid=(len(steps),),
            in_specs=specs,
            out_specs=pl.BlockSpec(block, lambda step, rows, cols: (rows[step], cols[step])),
        ),
        out_shape=jax.ShapeDtypeStruct(shape, kind),
        compiler_params=kernel_params(),
        cost_estimate=LIGHT,
    )(rows, cols, *[array for _, _, array in placed])


def gain_sum(parts):
    count = parts.shape[0]
    c_size, y_size, z_size = (lax.axis_size(axis) for axis in ("c", "y", "z"))
    parts = parts + swap(parts, "x", 1)
    parts = parts.reshape(count, c_size, y_size, z_size, -1).transpose(1, 2, 3, 0, 4)
    here = lax.axis_index("c")
    sent = lax.dynamic_index_in_dim(parts, 1 - here, 0, keepdims=False)
    return lax.dynamic_index_in_dim(parts, here, 0, keepdims=False) + swap(sent, "c", 1)


def gain_sum_last(parts):
    if lax.axis_size("y") == 2:
        here = lax.axis_index("y")
        sent = lax.dynamic_index_in_dim(parts, 1 - here, 0, keepdims=False)
        parts = lax.dynamic_index_in_dim(parts, here, 0, keepdims=False) + swap(sent, "y", 1)
    else:
        parts = lax.psum_scatter(parts, "y", scatter_dimension=0, tiled=True)[0]
    here = lax.axis_index("z")
    total = lax.dynamic_index_in_dim(parts, here, 0, keepdims=False)
    for k in (1, 2, 3):
        piece = lax.dynamic_index_in_dim(parts, here ^ k, 0, keepdims=False)
        total = total + swap(piece, "z", k)
    return total


def on_device(
    tokens,
    seg_lengths,
    parents,
    attn_gain,
    w_query,
    w_key,
    w_value,
    w_out,
    attn_post_gain,
    ffn_gain,
    w_gate,
    w_up,
    w_down,
    ffn_post_gain,
    out_grad,
):
    local_rows, width = tokens.shape
    z_size, y_size, c_size = lax.axis_size("z"), lax.axis_size("y"), lax.axis_size("c")
    shard = width // (z_size * y_size * c_size)
    group_rows = local_rows * lax.axis_size("x")
    head_cols = w_query.shape[1]
    kv_cols = w_key.shape[1]
    kv_here = kv_cols // HD
    ids = spread_ids()
    core_here, core_there = ids[2:3], 1 - ids[2:3]
    first_half, second_half = jnp.zeros(1, jnp.int32), jnp.ones(1, jnp.int32)

    def inward(values):
        lead = values.shape[:-1]
        cut = values.reshape(lead + (z_size, y_size, c_size, shard))
        count = len(lead)
        order = tuple(range(count)) + (count + 2, count + 1, count, count + 3)
        return cut.transpose(order).reshape(lead + (width,))

    def outward(values):
        lead = values.shape[:-1]
        cut = values.reshape(lead + (c_size, y_size, z_size, shard))
        count = len(lead)
        order = tuple(range(count)) + (count + 2, count + 1, count, count + 3)
        return cut.transpose(order).reshape(lead + (width,))

    pairs = y_size == 2
    row_axes = ("c", "y", "z")
    positions, allowed = tree_tables(seg_lengths[0], parents[0], group_rows)
    allowed = allowed.astype(jnp.int32)
    cosine, sine = rope_tables(positions, HD)
    attn_gain, attn_post_gain = inward(attn_gain), inward(attn_post_gain)
    ffn_gain, ffn_post_gain = inward(ffn_gain), inward(ffn_post_gain)
    state_in = inward(tokens).astype(F32)
    out_cotan = inward(out_grad).astype(F32)

    qkv_here = jnp.concatenate(
        [
            weight[:, g * (weight.shape[1] // kv_here) : (g + 1) * (weight.shape[1] // kv_here)]
            for g in range(kv_here)
            for weight in (w_query, w_key, w_value)
        ],
        axis=1,
    )
    inverse_one = lax.rsqrt(jnp.mean(state_in * state_in, axis=-1, keepdims=True) + NORM_EPS)
    unit_one = state_in * inverse_one
    normed_here = (unit_one * attn_gain).astype(BF)

    qkv_weight = lax.all_gather(qkv_here, row_axes, axis=0, tiled=True)
    out_weight = lax.all_gather(w_out.T, row_axes, axis=0, tiled=True)

    live = {"up": line_cuts(w_up), "down": line_cuts(w_down.T)}
    live["gate"] = line_swaps(line_cuts(w_gate))
    live["normed_one"] = [normed_here, swap(normed_here, "x", 1)]
    live = close(live)

    live["normed_one"] = pair_gather(*live["normed_one"])
    live["gate"] = cut_first(line_place(live["gate"]))
    live["up"] = line_swaps(live["up"])
    live = close(live)

    live["gate"] |= cut_over_x(live["gate"]) | cut_over_y(live["gate"])
    live["up"] = cut_first(line_place(live["up"]))
    live["down"] = line_swaps(live["down"])
    live["qkv"] = qkv_weight
    live = close(live)
    live["down"] = line_place(live["down"])

    live["up"] |= cut_over_x(live["up"]) | cut_over_y(live["up"])
    gate_half = cut_half(live["gate"])
    live["gate"] = [gate_half, swap(gate_half, "c", 1)]
    normed_one, qkv_weight = live["normed_one"], live["qkv"]
    query, key, value, attended = attention_call(
        normed_one, qkv_weight, cosine, sine, allowed, kv_here
    )
    live["attended"] = attended
    live = close(live)

    attended = live["attended"]
    live["branch"] = branch_call(ids, attended, out_weight)
    live = close(live)
    sent, kept = live["branch"]
    live["branch"] = [kept, swap(sent, "x", 1)]
    live["up"] = cut_half(live["up"])
    live = close(live)
    down_weight = gather_cut(live.pop("down"))
    branch = live["branch"][0] + live["branch"][1].astype(F32)
    inverse_two = lax.rsqrt(jnp.mean(branch * branch, axis=-1, keepdims=True) + NORM_EPS)
    unit_two = branch * inverse_two
    hidden = state_in + unit_two * attn_post_gain
    inverse_three = lax.rsqrt(jnp.mean(hidden * hidden, axis=-1, keepdims=True) + NORM_EPS)
    unit_three = hidden * inverse_three


    live["normed_two"] = line_gather((unit_three * ffn_gain).astype(BF))
    live["up"] = [live["up"], swap(live["up"], "c", 1)]
    live = close(live)
    gate_weight, up_weight = Weight(*live["gate"]), Weight(*live["up"])
    down_weight, normed_two = Weight(down_weight), live["normed_two"]

    act, gate_proj, up_proj = ffn_call(
        up_kernel, ids, [normed_two], [gate_weight, up_weight], [], (BF, F32, F32), 256, 0
    )
    sums = ffn_call(down_kernel, ids, [], [down_weight], [act], (), 1152, width)
    live = {"act": act, "sums": line_sum_second(line_sum_first(sums))}
    live = close(live)
    ffn_out = line_total(live["sums"])
    inverse_four = lax.rsqrt(jnp.mean(ffn_out * ffn_out, axis=-1, keepdims=True) + NORM_EPS)
    unit_four = ffn_out * inverse_four
    mixed = (hidden + unit_four * ffn_post_gain).astype(BF)
    gain_four = jnp.sum(out_cotan * unit_four, axis=0)
    d_ffn = norm_back(out_cotan * ffn_post_gain, unit_four, inverse_four).astype(BF)
    live["d_ffn"] = line_gather(d_ffn)
    live = close(live)
    d_ffn, act = live["d_ffn"], live["act"]
    def product(left, right, *got, place=0):
        which = core_here if got else core_there
        if pairs:
            return outer_quarters(ids, which, left, right, *got, place=place)
        made = outer_halves(which, left, (right,), *got)
        return [made] if got else made

    def first_sums(quarters, rows):
        if not pairs:
            return quarters
        *quarters, across = quarters
        return [*quarters, *fold_first(across, rows)]

    def second_sums(quarters):
        if not pairs:
            return [sum_cut(*quarters)]
        own, over_x, over_y, *got = quarters
        over_x, over_y = fold_join({"x": over_x, "y": over_y}, got)
        return [own, swap(over_x, "x", 1), swap(over_y, "y", 1)]

    def over_line(terms):
        return line_swaps(line_chunks(line_total(terms).astype(BF)))

    live = {"down": product(d_ffn, act, swap(product(d_ffn, act), "c", 1))}
    weights = [gate_weight, up_weight, down_weight]
    d_gate, d_up, *sums = ffn_call(
        backward_kernel, ids, [d_ffn], weights, [gate_proj, up_proj], (BF, BF), 384, width
    )
    live = close(live | {"d_gate": d_gate, "d_up": d_up, "sums": sums})

    d_gate, d_up = live["d_gate"], live["d_up"]
    live["sums"] = line_sum_first(live["sums"])
    live["down"] = first_sums(live["down"], 2 * shard)
    if pairs:
        live["sent"] = [outer_pair(ids, core_there, normed_two, d_up, d_gate)]
    else:
        live["sent"] = [product(normed_two, d_up), product(normed_two, d_gate)]
    live = close(live)
    live["sums"] = line_sum_second(live["sums"])
    live["down"] = second_sums(live["down"])
    got = [swap(part, "c", 1) for part in live["sent"]]
    live["up"] = product(normed_two, live["d_up"], got[0], place=0)
    live["gate"] = product(normed_two, live["d_gate"], got[-1], place=1)
    live = close({k: live[k] for k in ("sums", "down", "up", "gate")})

    d_normed_two = line_total(live["sums"])
    gain_three = jnp.sum(d_normed_two * unit_three, axis=0)
    d_hidden = out_cotan + norm_back(d_normed_two * ffn_gain, unit_three, inverse_three)
    gain_two = jnp.sum(d_hidden * unit_two, axis=0)
    d_branch = norm_back(d_hidden * attn_post_gain, unit_two, inverse_two).astype(BF)
    live["d_branch"] = [d_branch, swap(d_branch, "x", 1)]
    live["up"] = first_sums(live["up"], 2 * shard)
    live["gate"] = first_sums(live["gate"], shard)
    live = close({k: live[k] for k in ("d_branch", "down", "up", "gate")})
    d_branch = pair_gather(*live["d_branch"])

    live = {k: live[k] for k in ("down", "up", "gate")}
    live["down"], live["up"] = over_line(live["down"]), second_sums(live["up"])
    d_qkv, d_sent, d_kept = attention_back_call(
        ids, d_branch, out_weight, qkv_weight, query, key, value, cosine, sine, allowed, kv_here
    )
    if pairs:
        live["rows"] = outer_rows(ids, core_there, normed_one, d_qkv, d_branch, attended)
    else:
        rows = [outer_dot(normed_one, d_qkv), outer_dot(d_branch, attended)]
        live["rows"] = jnp.concatenate(rows, axis=1).astype(BF)
    live = close(live | {"d_qkv": d_qkv, "d_normed_one": [d_kept, d_sent]})
    grad_down = line_columns(live["down"])

    live["up"], live["gate"] = over_line(live["up"]), second_sums(live["gate"])
    if pairs:
        products = (normed_one, live["d_qkv"], d_branch, attended)
        live["rows"] = outer_rows(ids, core_here, *products, swap(live["rows"], "c", 1))
    live = close({k: live[k] for k in ("up", "gate", "rows", "d_normed_one")})
    grad_up = line_columns(live["up"])

    d_kept, d_sent = live["d_normed_one"]
    live = {"gate": over_line(live["gate"]), "rows": live["rows"]}
    live["d_normed_one"] = [d_kept, swap(d_sent, "x", 1)]
    if pairs:
        far_sent, near_sent, far, near = live["rows"]
        live["rows"] = [near_sent, add_low(far, swap(far_sent, "y", 1)), near]
    live = close(live)
    grad_gate = line_columns(live["gate"])
    d_normed_one = live["d_normed_one"][0] + live["d_normed_one"][1].astype(F32)
    gain_one = jnp.sum(d_normed_one * unit_one, axis=0)
    grad_tokens = d_hidden + norm_back(d_normed_one * attn_gain, unit_one, inverse_one)
    gains = jnp.stack([gain_one, gain_two, gain_three, gain_four], axis=0)

    live = {"rows": live["rows"], "gains": gain_sum(gains)}
    if pairs:
        near_sent, far, near = live["rows"]
        live["rows"] = [near, swap(near_sent, "y", 1), swap(far, "z", 1)]
    live = close(live)

    gains = gain_sum_last(live["gains"])
    rows = live["rows"]
    if pairs:
        far = line_total([part[shard:] for part in rows]).astype(BF)
        grad_rows = line_total([part[:shard] for part in rows] + [swap(far, "z", 2)])
    else:
        grad_rows = lax.psum_scatter(rows, row_axes, scatter_dimension=0, tiled=True)
        grad_rows = grad_rows.astype(F32)
    out_from = grad_rows.shape[1] - attended.shape[1]
    grad_qkv, grad_out = grad_rows[:, :out_from], grad_rows[:, out_from:]
    cols = grad_qkv.shape[1] // kv_here
    cuts = (0, cols - 2 * HD, cols - HD, cols)
    grad_query, grad_key, grad_value = (
        jnp.concatenate(
            [grad_qkv[:, g * cols + cuts[i] : g * cols + cuts[i + 1]] for g in range(kv_here)],
            axis=1,
        )
        for i in range(3)
    )
    return (
        outward(mixed),
        outward(grad_tokens),
        gains[0],
        grad_query,
        grad_key,
        grad_value,
        grad_out.T,
        gains[1],
        gains[2],
        grad_gate,
        grad_up,
        grad_down.T,
        gains[3],
    )


def solution(mesh):
    count, pair = mesh.devices.shape
    grid = Mesh(mesh.devices.reshape(4, count // 8, 2, pair), ("z", "y", "c", "x"))
    rows = ("z", "y", "c")
    return jax.shard_map(
        on_device,
        mesh=grid,
        in_specs=(
            P(rows + ("x",), None),
            P(rows, None),
            P(rows, None),
            P(),
            P(rows, "x"),
            P(rows, "x"),
            P(rows, "x"),
            P("x", rows),
            P(),
            P(),
            P(rows, "x"),
            P(rows, "x"),
            P("x", rows),
            P(),
            P(rows + ("x",), None),
        ),
        out_specs=(
            P(rows + ("x",), None),
            P(rows + ("x",), None),
            P(rows),
            P(rows, "x"),
            P(rows, "x"),
            P(rows, "x"),
            P("x", rows),
            P(rows),
            P(rows),
            P(rows, "x"),
            P(rows, "x"),
            P("x", rows),
            P(rows),
        ),
        check_vma=False,
    )
```

```python
import functools

import jax
import jax.numpy as jnp
from jax import lax
from jax.experimental import pallas as pl
from jax.experimental.pallas import tpu as pltpu
from jax.sharding import Mesh
from jax.sharding import PartitionSpec as P

HD = 256
NORM_EPS = 1e-06
SOFT_CAP = 50.0
ROPE_BASE = 10000.0
MASK_FILL = -1e30
BF = jnp.bfloat16
F32 = jnp.float32


def tree_tables(lengths_row, parents_row, row_total):
    seg_count = lengths_row.shape[0]
    seg_index = jnp.arange(seg_count, dtype=jnp.int32)
    ancestor = (seg_index[:, None] == seg_index[None, :]) | (
        parents_row[:, None] == seg_index[None, :]
    )
    for repeat in range(seg_count.bit_length()):
        ancestor = jnp.any(ancestor[:, :, None] & ancestor[None, :, :], axis=1)
    seg_ends = jnp.cumsum(lengths_row)
    seg_starts = seg_ends - lengths_row
    token_index = jnp.arange(row_total, dtype=jnp.int32)
    segment = jnp.sum((token_index[:, None] >= seg_ends[None, :]).astype(jnp.int32), axis=1)
    strict = ancestor & (seg_index[:, None] != seg_index[None, :])
    offsets = jnp.sum(jnp.where(strict, lengths_row[None, :], 0), axis=1)
    one_hot = segment[:, None] == seg_index[None, :]
    positions = (
        jnp.sum(jnp.where(one_hot, (offsets - seg_starts)[None, :], 0), axis=1) + token_index
    )
    reached = jnp.any(one_hot[:, :, None] & ancestor[None, :, :], axis=1)
    allowed = jnp.any(reached[:, None, :] & one_hot[None, :, :], axis=2) & (
        token_index[None, :] <= token_index[:, None]
    )
    return (positions, allowed)


def rope_tables(positions, width):
    half_width = width // 2
    frequency = ROPE_BASE ** (-2.0 * jnp.arange(half_width, dtype=F32) / width)
    angles = positions.astype(F32)[:, None] * frequency[None, :]
    return (jnp.cos(angles), jnp.sin(angles))


def norm_back(grad_unit, unit, inverse):
    return inverse * (grad_unit - unit * jnp.mean(grad_unit * unit, axis=-1, keepdims=True))


def gelu_parts(values):
    scale = (2.0 / jnp.pi) ** 0.5
    square = values * values
    bent = jnp.tanh(scale * (values + 0.044715 * values * square))
    half = 0.5 * (1.0 + bent)
    slope = half + 0.5 * values * (1.0 - bent * bent) * scale * (1.0 + 3 * 0.044715 * square)
    return values * half, slope


def tile_dot(left, right):
    return jnp.dot(left, right, preferred_element_type=F32)


def tile_dot_cols(left, right):
    return lax.dot_general(left, right, (((1,), (1,)), ((), ())), preferred_element_type=F32)


def spill(ids, total, outs):
    rows = outs[0].shape[0]
    for k, out in enumerate(outs):
        out[...] = total[k * rows : (k + 1) * rows, :].astype(out.dtype)


class Weight:
    def __init__(self, *arrays):
        self.arrays, self.whole = arrays, len(arrays) == 1
        self.rows = arrays[0].shape[-2]

    def specs(self, tile):
        if not self.whole:
            return [pl.BlockSpec((self.rows, tile), lambda i, ids: (0, i))] * 2
        count = self.arrays[0].shape[-1] // tile
        return [pl.BlockSpec((None, self.rows, tile), lambda i, ids: (i // count, 0, i % count))]

    def columns(self, ids):
        if self.whole:
            return (pl.ds(0, self.rows),)
        starts = (pl.multiple_of(core * self.rows, 128) for core in (ids[2], 1 - ids[2]))
        return tuple(pl.ds(start, self.rows) for start in starts)


def inner(values, refs, columns):
    return sum(tile_dot(values[:, at], ref[...]) for ref, at in zip(refs, columns))


def outer_add(total, tile, refs, columns, fresh):
    for ref, at in zip(refs, columns):
        part = tile_dot_cols(tile, ref[...])
        total[:, at] = jnp.where(fresh, part, total[:, at] + part)


def up_kernel(columns, ids, x, *refs):
    gate_w, up_w, (act, gate, up) = refs[:2], refs[2:4], refs[4:]
    gate_at, up_at = (find(ids) for find in columns)
    gate_tile, up_tile = inner(x, gate_w, gate_at), inner(x, up_w, up_at)
    gate[...], up[...] = gate_tile, up_tile
    act[...] = (gelu_parts(gate_tile)[0] * up_tile).astype(BF)


def down_kernel(columns, ids, act, *refs):
    down_w, outs, total = refs[:1], refs[1:-1], refs[-1]
    outer_add(total, act[...], down_w, columns[0](ids), pl.program_id(0) == 0)

    @pl.when(pl.program_id(0) == pl.num_programs(0) - 1)
    def _():
        spill(ids, total, outs)


def backward_kernel(columns, ids, d, *refs):
    gate_w, up_w, down_w, (gate, up), (d_gate, d_up), outs, total = (
        refs[:2], refs[2:4], refs[4:5], refs[5:7], refs[7:9], refs[9:-1], refs[-1]
    )
    gate_at, up_at, down_at = (find(ids) for find in columns)
    d_act = inner(d, down_w, down_at)
    bent, slope = gelu_parts(gate[...])
    gate_tile = (d_act * up[...] * slope).astype(BF)
    up_tile = (d_act * bent).astype(BF)
    d_gate[...], d_up[...] = gate_tile, up_tile
    outer_add(total, gate_tile, gate_w, gate_at, pl.program_id(0) == 0)
    outer_add(total, up_tile, up_w, up_at, False)

    @pl.when(pl.program_id(0) == pl.num_programs(0) - 1)
    def _():
        spill(ids, total, outs)


def ffn_call(kernel, ids, values, weights, kept, made, tile, width):
    tokens = (values or kept)[0].shape[0]
    cols = weights[-1].arrays[0].shape[-1]
    hidden = 2 * cols if weights[-1].whole else cols
    across = pl.BlockSpec((tokens, tile), lambda i, ids: (0, i))
    parts = [F32, BF, BF, BF] if width else []
    return pl.pallas_call(
        functools.partial(kernel, [weight.columns for weight in weights]),
        grid_spec=pltpu.PrefetchScalarGridSpec(
            num_scalar_prefetch=1,
            grid=(hidden // tile,),
            in_specs=[pl.BlockSpec(array.shape, lambda i, ids: (0, 0)) for array in values]
            + ([] if values else [across] * len(kept))
            + [spec for weight in weights for spec in weight.specs(tile)]
            + ([across] * len(kept) if values else []),
            out_specs=[across] * len(made)
            + [pl.BlockSpec((tokens // 4, width), lambda i, ids: (0, 0)) for _ in parts],
            scratch_shapes=[pltpu.VMEM((tokens, width), F32)] if width else [],
        ),
        out_shape=[jax.ShapeDtypeStruct((tokens, hidden), kind) for kind in made]
        + [jax.ShapeDtypeStruct((tokens // 4, width), kind) for kind in parts],
        compiler_params=pltpu.CompilerParams(
            dimension_semantics=("arbitrary",), vmem_limit_bytes=58 * 2**20
        ),
        cost_estimate=pl.CostEstimate(flops=0, bytes_accessed=0, transcendentals=0),
    )(
        ids,
        *values,
        *([] if values else kept),
        *[array for weight in weights for array in weight.arrays],
        *(kept if values else []),
    )


def swap(values, axis, mask):
    size = lax.axis_size(axis)
    return lax.ppermute(values, axis, [(i, i ^ mask) for i in range(size)])


def rows_dot(left, right):
    return lax.dot_general(left, right, (((1,), (0,)), ((), ())), preferred_element_type=F32)


def cols_dot(left, right):
    return lax.dot_general(left, right, (((1,), (1,)), ((), ())), preferred_element_type=F32)


def outer_dot(left, right):
    return lax.dot_general(left, right, (((0,), (0,)), ((), ())), preferred_element_type=F32)


def close(live):
    return lax.optimization_barrier(live)


def pair_gather(values, other):
    mine = lax.axis_index("x")
    first = jnp.where(mine == 0, values, other)
    second = jnp.where(mine == 0, other, values)
    return jnp.concatenate([first, second], axis=0)


def pair_parts(partial):
    rows = partial.shape[0] // 2
    mine = lax.axis_index("x")
    sent = lax.dynamic_slice_in_dim(partial, (1 - mine) * rows, rows, 0).astype(BF)
    return sent, lax.dynamic_slice_in_dim(partial, mine * rows, rows, 0)


def pair_sum(partial):
    sent, kept = pair_parts(partial)
    return kept + swap(sent, "x", 1).astype(F32)


def rows_sum(values, axis):
    size = lax.axis_size(axis)
    if size != 2:
        return lax.psum_scatter(values, axis, scatter_dimension=0, tiled=True)
    rows, mine = values.shape[0] // 2, lax.axis_index(axis)
    sent = lax.dynamic_slice_in_dim(values, (1 - mine) * rows, rows, 0)
    return add_low(lax.dynamic_slice_in_dim(values, mine * rows, rows, 0), swap(sent, axis, 1))


def placed(rows, *pieces):
    held = jnp.zeros((rows,) + pieces[0][1].shape[1:], pieces[0][1].dtype)
    for offset, piece in pieces:
        held = lax.dynamic_update_slice_in_dim(held, piece, offset, 0)
    return held


def add_low(left, right):
    return (left.astype(F32) + right.astype(F32)).astype(BF)


def line_gather(values):
    near, far = swap(values, "z", 1), swap(values, "z", 2)
    return jnp.concatenate([values, near, far, swap(far, "z", 1)], axis=0)


def line_sum_first(parts):
    return [*parts[:3], swap(parts[3], "z", 1)]


def line_sum_second(parts):
    return [parts[0], swap(parts[1], "z", 1), swap(add_low(parts[2], parts[3]), "z", 2)]


def line_place(pieces):
    here, (rows, cols) = lax.axis_index("z"), pieces[0].shape
    if rows % 16 == 0:
        return assemble(
            (len(pieces) * rows, cols), (rows, cols), [(here ^ k, 0, p) for k, p in enumerate(pieces)]
        )
    return placed(len(pieces) * rows, *[((here ^ k) * rows, p) for k, p in enumerate(pieces)])


def line_cuts(weight):
    here, cut = lax.axis_index("z"), weight.shape[1] // 4
    return [lax.dynamic_slice_in_dim(weight, (here ^ k) * cut, cut, 1) for k in range(4)]


def line_swaps(cuts):
    return [cuts[0]] + [swap(cuts[k], "z", k) for k in (1, 2, 3)]


def line_chunks(grad):
    rows, here = grad.shape[0] // 4, lax.axis_index("z")
    return [lax.dynamic_slice_in_dim(grad, (here ^ k) * rows, rows, 0) for k in range(4)]


def line_columns(pieces):
    here, (rows, cols) = lax.axis_index("z"), pieces[0].shape
    spots = [(0, here ^ k, piece) for k, piece in enumerate(pieces)]
    return assemble((rows, 4 * cols), (rows, cols), spots, F32)


def line_total(pieces):
    total = pieces[0].astype(F32)
    for piece in pieces[1:]:
        total = total + piece.astype(F32)
    return total


def y_chunks(grad):
    rows, y, z = grad.shape[0] // 8, lax.axis_index("y"), lax.axis_index("z")
    return [
        tuple(
            lax.dynamic_slice_in_dim(grad, (4 * side + (z ^ k)) * rows, rows, 0)
            for side in (y, 1 - y)
        )
        for k in range(4)
    ]


def pair_rows(mine, other, axis):
    rows, here = mine.shape[0], lax.axis_index(axis)
    return placed(2 * rows, (here * rows, mine), ((1 - here) * rows, other))


def pair_halves(values, axis):
    rows, here = values.shape[0] // 2, lax.axis_index(axis)
    return (
        lax.dynamic_slice_in_dim(values, here * rows, rows, 0),
        lax.dynamic_slice_in_dim(values, (1 - here) * rows, rows, 0),
    )


def cut_first(own):
    got = {"own": own, "x": swap(own, "x", 1)}
    if lax.axis_size("y") == 2:
        got["y"] = swap(own, "y", 1)
    return got


def cut_over_x(got):
    rows = got["own"].shape[0] // 2
    return {"over_x": swap(got["y"][:rows], "x", 1)} if "y" in got else {}


def cut_over_y(got):
    rows = got["own"].shape[0] // 2
    return {"over_y": swap(got["x"][rows:], "y", 1)} if "y" in got else {}


def cut_half(got):
    own = got["own"]
    rows, cols = own.shape
    if "y" not in got:
        both = jnp.where(
            lax.axis_index("x") == 0,
            jnp.concatenate([own, got["x"]], axis=1),
            jnp.concatenate([got["x"], own], axis=1),
        )
        return lax.all_gather(both, "y", axis=0, tiled=True)
    here, half = lax.axis_index("y"), lax.axis_index("x")
    mine, far = 2 * here, 2 * (1 - here)
    spots = [
        (mine, half, own),
        (far, half, got["y"]),
        (mine, 1 - half, got["x"]),
        (far, 1 - half, got["over_x"]),
        (far + 1, 1 - half, got["over_y"]),
    ]
    return assemble((2 * rows, 2 * cols), (rows // 2, cols), spots)


def fold_parts(both):
    cols, here = both.shape[1] // 2, lax.axis_index("x")
    mine = lax.dynamic_slice_in_dim(both, here * cols, cols, 1)
    other = lax.dynamic_slice_in_dim(both, (1 - here) * cols, cols, 1)
    (own, over_y), (over_x, across) = pair_halves(mine, "y"), pair_halves(other, "y")
    return {"own": own, "x": over_x, "y": over_y, "across": across}


def fold_first(across, rows):
    return [swap(across[:rows], "x", 1), swap(across[rows:], "y", 1)]


def fold_join(parts, got):
    rows = got[0].shape[0]
    over_y = add_low(parts["y"][:rows], got[0])
    over_x = add_low(parts["x"][rows:], got[1])
    return (
        jnp.concatenate([parts["x"][:rows], over_x]),
        jnp.concatenate([over_y, parts["y"][rows:]]),
    )


def spread_ids():
    return jnp.stack([lax.axis_index(axis) for axis in ("z", "y", "c", "x")]).astype(jnp.int32)


LIGHT = pl.CostEstimate(flops=0, bytes_accessed=0, transcendentals=0)


def kernel_params(megabytes=50):
    return pltpu.CompilerParams(
        dimension_semantics=("arbitrary",), vmem_limit_bytes=megabytes * 2**20
    )


def turned(values, cosine, sine):
    half = values.shape[1] // 2
    front, back = values[:, :half], values[:, half:]
    return jnp.concatenate([front * cosine - back * sine, back * cosine + front * sine], axis=1)


def head_probs(query, key, allowed):
    scores = tile_dot_cols(query, key)
    bent = jnp.tanh(scores * (HD**-0.5 / SOFT_CAP))
    masked = jnp.where(allowed != 0, SOFT_CAP * bent, MASK_FILL)
    weights = jnp.exp(masked - jnp.max(masked, axis=1, keepdims=True))
    return bent, weights / jnp.sum(weights, axis=1, keepdims=True)


def share(ids, total, sent, kept):
    rows = sent.shape[0]
    here = ids[3]
    sent[...] = total[pl.ds(pl.multiple_of((1 - here) * rows, rows), rows), :].astype(BF)
    kept[...] = total[pl.ds(pl.multiple_of(here * rows, rows), rows), :]


def attention_kernel(
    ids, x, weight, cosine, sine, allowed, query, key, value, attended, sent, kept, total
):
    heads = query.shape[1] // HD
    keys = heads * HD
    proj = tile_dot(x[...], weight[:, : keys + 2 * HD])
    key_here = turned(proj[:, keys : keys + HD], cosine[...], sine[...]).astype(BF)
    value_here = proj[:, keys + HD :].astype(BF)
    key[...], value[...] = key_here, value_here
    for head in range(heads):
        at = slice(head * HD, (head + 1) * HD)
        query_here = turned(proj[:, at], cosine[...], sine[...]).astype(BF)
        query[:, at] = query_here
        probs = head_probs(query_here, key_here, allowed[...])[1].astype(BF)
        attended[:, at] = tile_dot(probs, value_here).astype(BF)
    part = tile_dot_cols(attended[...], weight[:, keys + 2 * HD :])
    total[...] = jnp.where(pl.program_id(0) == 0, part, total[...] + part)

    @pl.when(pl.program_id(0) == pl.num_programs(0) - 1)
    def _():
        share(ids, total, sent, kept)


def attention_specs(tokens, width, cols, heads):
    def here(rows, cut):
        return pl.BlockSpec((rows, cut), lambda g, ids: (0, g))

    def whole(rows, cut):
        return pl.BlockSpec((rows, cut), lambda g, ids: (0, 0))

    first = [whole(tokens, width), here(width, cols)]
    tables = [whole(tokens, HD // 2), whole(tokens, HD // 2), whole(tokens, tokens)]
    held = [here(tokens, cut) for cut in (heads * HD, HD, HD)]
    halves = [whole(tokens // 2, width)] * 2
    return first, tables, held, halves, here


def attention_call(ids, x, weight, cosine, sine, allowed, groups):
    tokens, width = x.shape
    cols = weight.shape[1] // groups
    heads = (cols // HD - 2) // 2
    first, tables, held, halves, here = attention_specs(tokens, width, cols, heads)
    shapes = [groups * cut for cut in (heads * HD, HD, HD, heads * HD)]
    return pl.pallas_call(
        attention_kernel,
        grid_spec=pltpu.PrefetchScalarGridSpec(
            num_scalar_prefetch=1,
            grid=(groups,),
            in_specs=first + tables,
            out_specs=held + [here(tokens, heads * HD)] + halves,
            scratch_shapes=[pltpu.VMEM((tokens, width), F32)],
        ),
        out_shape=[jax.ShapeDtypeStruct((tokens, cut), BF) for cut in shapes]
        + [jax.ShapeDtypeStruct((tokens // 2, width), kind) for kind in (BF, F32)],
        compiler_params=kernel_params(),
        cost_estimate=LIGHT,
    )(ids, x, weight, cosine, sine, allowed)


def attention_back_kernel(
    ids, d, weight, cosine, sine, allowed, query, key, value, d_qkv, sent, kept, total
):
    heads = query.shape[1] // HD
    cut = (heads + 2) * HD
    key_here, value_here = key[...], value[...]
    d_attended = tile_dot(d[...], weight[:, cut:]).astype(BF)
    d_key = d_value = 0.0
    pieces = []
    for head in range(heads):
        at = slice(head * HD, (head + 1) * HD)
        query_here, d_here = query[:, at], d_attended[:, at]
        bent, probs = head_probs(query_here, key_here, allowed[...])
        d_probs = tile_dot_cols(d_here, value_here)
        inner = jnp.sum(probs * d_probs, axis=1, keepdims=True)
        d_scores = probs * (d_probs - inner) * (HD**-0.5) * (1.0 - bent * bent)
        d_scores = d_scores.astype(BF)
        d_query = tile_dot(d_scores, key_here)
        pieces.append(turned(d_query, cosine[...], -sine[...]).astype(BF))
        d_key = d_key + outer_dot(d_scores, query_here)
        d_value = d_value + outer_dot(probs.astype(BF), d_here)
    pieces.append(turned(d_key, cosine[...], -sine[...]).astype(BF))
    pieces.append(d_value.astype(BF))
    made = jnp.concatenate(pieces, axis=1)
    d_qkv[...] = made
    part = tile_dot_cols(made, weight[:, :cut])
    total[...] = jnp.where(pl.program_id(0) == 0, part, total[...] + part)

    @pl.when(pl.program_id(0) == pl.num_programs(0) - 1)
    def _():
        share(ids, total, sent, kept)


def attention_back_call(ids, d, weight, cosine, sine, allowed, query, key, value, groups):
    tokens, width = d.shape
    cols = weight.shape[1] // groups
    heads = (cols // HD - 2) // 2
    first, tables, held, halves, here = attention_specs(tokens, width, cols, heads)
    cut = (heads + 2) * HD
    return pl.pallas_call(
        attention_back_kernel,
        grid_spec=pltpu.PrefetchScalarGridSpec(
            num_scalar_prefetch=1,
            grid=(groups,),
            in_specs=first + tables + held,
            out_specs=[here(tokens, cut)] + halves,
            scratch_shapes=[pltpu.VMEM((tokens, width), F32)],
        ),
        out_shape=[
            jax.ShapeDtypeStruct((tokens, groups * cut), BF),
            jax.ShapeDtypeStruct((tokens // 2, width), BF),
            jax.ShapeDtypeStruct((tokens // 2, width), F32),
        ],
        compiler_params=kernel_params(),
        cost_estimate=LIGHT,
    )(ids, d, weight, cosine, sine, allowed, query, key, value)


def outer_kernel(which, left, right, *rest):
    got, (made, flipped) = rest[:-2], rest[-2:]

    @pl.when(pl.program_id(0) == 0)
    def _():
        flipped[...] = left[...].T

    total = tile_dot(flipped[...], right[...])
    for piece in got:
        total = total + piece[...].astype(F32)
    made[...] = total.astype(BF)


def outer_call(left, right, which, *got):
    tokens, cut, cols = left.shape[0], left.shape[1] // 2, right.shape[1]
    tile = cols // 2
    across = pl.BlockSpec((cut, tile), lambda i, which: (0, i))
    return pl.pallas_call(
        outer_kernel,
        grid_spec=pltpu.PrefetchScalarGridSpec(
            num_scalar_prefetch=1,
            grid=(cols // tile,),
            in_specs=[
                pl.BlockSpec((tokens, cut), lambda i, which: (0, which[0])),
                pl.BlockSpec((tokens, tile), lambda i, which: (0, i)),
            ]
            + [across] * len(got),
            out_specs=across,
            scratch_shapes=[pltpu.VMEM((cut, tokens), BF)],
        ),
        out_shape=jax.ShapeDtypeStruct((cut, cols), BF),
        compiler_params=kernel_params(),
        cost_estimate=LIGHT,
    )(which, left, right, *got)


def outer_halves_kernel(number, which, left, *refs):
    rights, got, (made, flipped) = refs[:number], refs[number:-2], refs[-2:]
    step = pl.program_id(0)

    @pl.when(step == 0)
    def _():
        flipped[...] = left[...].T

    for k, right in enumerate(rights):

        @pl.when(step % number == k)
        def _(right=right):
            total = tile_dot(flipped[...], right[...])
            for piece in got:
                total = total + piece[...].astype(F32)
            made[...] = total.astype(BF)


def outer_halves(which, left, rights, *got):
    tokens, cut = left.shape[0], left.shape[1] // 2
    cols, number = rights[0].shape[1] // 2, len(rights)
    across = pl.BlockSpec((None, cut, cols), lambda i, which: (i // number, 0, i % number))
    return pl.pallas_call(
        functools.partial(outer_halves_kernel, number),
        grid_spec=pltpu.PrefetchScalarGridSpec(
            num_scalar_prefetch=1,
            grid=(2 * number,),
            in_specs=[pl.BlockSpec((tokens, cut), lambda i, which: (0, which[0]))]
            + [pl.BlockSpec((tokens, cols), lambda i, which: (0, i // number))] * number
            + [across] * len(got),
            out_specs=across,
            scratch_shapes=[pltpu.VMEM((cut, tokens), BF)],
        ),
        out_shape=jax.ShapeDtypeStruct((2, cut, number * cols), BF),
        compiler_params=kernel_params(),
        cost_estimate=LIGHT,
    )(which, left, *rights, *got)


def sum_cut(grad):
    half, cols = grad.shape[1:]
    blocks = 2 * lax.axis_size("y")
    grad = grad.reshape(blocks, 2 * half // blocks, cols)
    return lax.psum_scatter(grad, ("x", "y"), scatter_dimension=0, tiled=True)[0]


def gather_cut(own):
    whole = lax.all_gather(own, ("x", "c", "y"), axis=0, tiled=True)
    return whole.reshape(2, -1, own.shape[1])


def outer_low(left, right, mine, theirs):
    sent = outer_call(left, right, theirs)
    return outer_call(left, right, mine, swap(sent, "c", 1))


def outer_quarters_kernel(ids, which, left, right, *refs):
    (plain, flipped), refs = refs[-2:], refs[:-2]
    got, outs = (refs[:4], refs[4:]) if len(refs) > 1 else ((), refs)
    step, rows = pl.program_id(0), flipped.shape[0] // 2

    @pl.when(step == 0)
    def _():
        plain[...] = left[...].T
        for k, side in enumerate((ids[1], 1 - ids[1])):
            at = pl.multiple_of(side * rows, rows)
            flipped[k * rows : (k + 1) * rows, :] = plain[pl.ds(at, rows), :]

    for half in range(2):

        @pl.when(step % 2 == half)
        def _(half=half):
            for side in range(2):
                k = half + 2 * side
                total = tile_dot(flipped[side * rows : (side + 1) * rows, :], right[...])
                if got:
                    outs[k][...] = (total + got[k][...].astype(F32)).astype(BF)
                else:
                    outs[0][side] = total.astype(BF)


def outer_quarters(ids, which, left, right, *got, place=0):
    tokens, cut, cols = left.shape[0], left.shape[1] // 2, right.shape[1] // 2
    rows = cut // 2
    quarter = pl.BlockSpec((rows, cols), lambda i, ids, which: (0, 0))
    taken = [
        pl.BlockSpec((None, rows, cols), lambda i, ids, which, k=k: (2 * place + k // 2, 0, k % 2))
        for k in range(4)
    ]
    shape = jax.ShapeDtypeStruct((rows, cols), BF)
    return pl.pallas_call(
        outer_quarters_kernel,
        grid_spec=pltpu.PrefetchScalarGridSpec(
            num_scalar_prefetch=2,
            grid=(2,),
            in_specs=[
                pl.BlockSpec((tokens, cut), lambda i, ids, which: (0, which[0])),
                pl.BlockSpec((tokens, cols), lambda i, ids, which: (0, ids[3] ^ i)),
            ]
            + (taken if got else []),
            out_specs=[quarter] * 4
            if got
            else pl.BlockSpec((2, rows, cols), lambda i, ids, which: (0, 0, i)),
            scratch_shapes=[pltpu.VMEM((cut, tokens), BF)] * 2,
        ),
        out_shape=[shape] * 4 if got else jax.ShapeDtypeStruct((2, rows, 2 * cols), BF),
        compiler_params=kernel_params(),
        cost_estimate=LIGHT,
    )(ids, which, left, right, *got * 4)


def outer_pair_kernel(ids, which, left, right_a, right_b, made, plain, flipped):
    step, rows = pl.program_id(0), flipped.shape[0] // 2

    @pl.when(step == 0)
    def _():
        plain[...] = left[...].T
        for k, side in enumerate((ids[1], 1 - ids[1])):
            at = pl.multiple_of(side * rows, rows)
            flipped[k * rows : (k + 1) * rows, :] = plain[pl.ds(at, rows), :]

    for k, right in enumerate((right_a, right_b)):

        @pl.when(step // 2 == k)
        def _(right=right):
            for side in range(2):
                at = slice(side * rows, (side + 1) * rows)
                made[side] = tile_dot(flipped[at, :], right[...]).astype(BF)


def outer_pair(ids, which, left, right_a, right_b):
    tokens, cut, cols = left.shape[0], left.shape[1] // 2, right_a.shape[1] // 2
    rows = cut // 2
    return pl.pallas_call(
        outer_pair_kernel,
        grid_spec=pltpu.PrefetchScalarGridSpec(
            num_scalar_prefetch=2,
            grid=(4,),
            in_specs=[
                pl.BlockSpec((tokens, cut), lambda i, ids, which: (0, which[0])),
                pl.BlockSpec((tokens, cols), lambda i, ids, which: (0, ids[3] ^ jnp.minimum(i, 1))),
                pl.BlockSpec(
                    (tokens, cols), lambda i, ids, which: (0, ids[3] ^ jnp.maximum(i - 2, 0))
                ),
            ],
            out_specs=pl.BlockSpec((2, rows, cols), lambda i, ids, which: (i // 2, 0, i % 2)),
            scratch_shapes=[pltpu.VMEM((cut, tokens), BF)] * 2,
        ),
        out_shape=jax.ShapeDtypeStruct((4, rows, 2 * cols), BF),
        compiler_params=kernel_params(),
        cost_estimate=LIGHT,
    )(ids, which, left, right_a, right_b)


def outer_rows_kernel(ids, which, left_a, left_b, right_a, right_b, *refs):
    (plain, flipped), refs = refs[-2:], refs[:-2]
    got, outs = (refs[:4], refs[4:]) if len(refs) > 1 else ((), refs)
    step, last = pl.program_id(0), pl.num_programs(0) - 1
    rows = flipped.shape[0] // 8
    z, y = ids[0], ids[1]
    order = [4 * side + (z ^ k) for side in (1 - y, y) for k in (1, 3, 0, 2)]
    for left, when in ((left_a, 0), (left_b, last)):

        @pl.when(step == when)
        def _(left=left):
            plain[...] = left[...].T
            for k, block in enumerate(order):
                at = pl.multiple_of(block * rows, rows)
                flipped[k * rows : (k + 1) * rows, :] = plain[pl.ds(at, rows), :]

    def give(right):
        total = tile_dot(flipped[...], right[...])
        if not got:
            outs[0][...] = total.astype(BF)
        for k, piece in enumerate(got):
            part = total[2 * k * rows : (2 * k + 2) * rows, :]
            outs[k][...] = (part + piece[...].astype(F32)).astype(BF)

    @pl.when(step < last)
    def _():
        give(right_a)

    @pl.when(step == last)
    def _():
        give(right_b)


def outer_rows(ids, which, left_a, right_a, left_b, right_b, *got):
    tokens, cut = left_a.shape[0], left_a.shape[1] // 2
    tile = right_b.shape[1]
    cols = right_a.shape[1] + tile
    rows = cut // 4
    count = cols // tile
    half = pl.BlockSpec((tokens, cut), lambda i, ids, which: (0, which[0]))
    across = pl.BlockSpec((rows, tile), lambda i, ids, which: (0, i))
    taken = [pl.BlockSpec((rows, tile), lambda i, ids, which, k=k: (k, i)) for k in range(4)]
    return pl.pallas_call(
        outer_rows_kernel,
        grid_spec=pltpu.PrefetchScalarGridSpec(
            num_scalar_prefetch=2,
            grid=(count,),
            in_specs=[
                half,
                half,
                pl.BlockSpec((tokens, tile), lambda i, ids, which: (0, jnp.minimum(i, count - 2))),
                pl.BlockSpec((tokens, tile), lambda i, ids, which: (0, 0)),
            ]
            + (taken if got else []),
            out_specs=[across] * 4
            if got
            else pl.BlockSpec((cut, tile), lambda i, ids, which: (0, i)),
            scratch_shapes=[pltpu.VMEM((cut, tokens), BF)] * 2,
        ),
        out_shape=[jax.ShapeDtypeStruct((rows, cols), BF)] * 4
        if got
        else jax.ShapeDtypeStruct((cut, cols), BF),
        compiler_params=kernel_params(),
        cost_estimate=LIGHT,
    )(ids, which, left_a, left_b, right_a, right_b, *got * 4)


def assemble_kernel(counts, rows, cols, *refs):
    pieces, made = refs[:-1], refs[-1]
    step, first = pl.program_id(0), 0
    for piece, count in zip(pieces, counts):

        @pl.when((step >= first) & (step < first + count))
        def _(piece=piece):
            made[...] = piece[...].astype(made.dtype)

        first += count


def assemble(shape, block, placed, kind=BF):
    counts = [array.shape[0] // block[0] for _, _, array in placed]
    steps = [(row + k, col) for (row, col, _), n in zip(placed, counts) for k in range(n)]
    rows, cols = (jnp.stack([jnp.asarray(s[i], jnp.int32) for s in steps]) for i in range(2))
    specs, first = [], 0
    for count in counts:

        def at(step, rows, cols, first=first, count=count):
            return (jnp.clip(step - first, 0, count - 1), 0)

        specs.append(pl.BlockSpec(block, at))
        first += count
    return pl.pallas_call(
        functools.partial(assemble_kernel, counts),
        grid_spec=pltpu.PrefetchScalarGridSpec(
            num_scalar_prefetch=2,
            grid=(len(steps),),
            in_specs=specs,
            out_specs=pl.BlockSpec(block, lambda step, rows, cols: (rows[step], cols[step])),
        ),
        out_shape=jax.ShapeDtypeStruct(shape, kind),
        compiler_params=kernel_params(),
        cost_estimate=LIGHT,
    )(rows, cols, *[array for _, _, array in placed])


def gain_sum(parts):
    count = parts.shape[0]
    c_size, y_size, z_size = (lax.axis_size(axis) for axis in ("c", "y", "z"))
    parts = parts + swap(parts, "x", 1)
    parts = parts.reshape(count, c_size, y_size, z_size, -1).transpose(1, 2, 3, 0, 4)
    here = lax.axis_index("c")
    sent = lax.dynamic_index_in_dim(parts, 1 - here, 0, keepdims=False)
    return lax.dynamic_index_in_dim(parts, here, 0, keepdims=False) + swap(sent, "c", 1)


def gain_sum_last(parts):
    if lax.axis_size("y") == 2:
        here = lax.axis_index("y")
        sent = lax.dynamic_index_in_dim(parts, 1 - here, 0, keepdims=False)
        parts = lax.dynamic_index_in_dim(parts, here, 0, keepdims=False) + swap(sent, "y", 1)
    else:
        parts = lax.psum_scatter(parts, "y", scatter_dimension=0, tiled=True)[0]
    here = lax.axis_index("z")
    total = lax.dynamic_index_in_dim(parts, here, 0, keepdims=False)
    for k in (1, 2, 3):
        piece = lax.dynamic_index_in_dim(parts, here ^ k, 0, keepdims=False)
        total = total + swap(piece, "z", k)
    return total


def on_device(
    tokens,
    seg_lengths,
    parents,
    attn_gain,
    w_query,
    w_key,
    w_value,
    w_out,
    attn_post_gain,
    ffn_gain,
    w_gate,
    w_up,
    w_down,
    ffn_post_gain,
    out_grad,
):
    local_rows, width = tokens.shape
    z_size, y_size, c_size = lax.axis_size("z"), lax.axis_size("y"), lax.axis_size("c")
    shard = width // (z_size * y_size * c_size)
    group_rows = local_rows * lax.axis_size("x")
    head_cols = w_query.shape[1]
    kv_cols = w_key.shape[1]
    kv_here = kv_cols // HD
    ids = spread_ids()
    core_here, core_there = ids[2:3], 1 - ids[2:3]
    first_half, second_half = jnp.zeros(1, jnp.int32), jnp.ones(1, jnp.int32)

    def inward(values):
        lead = values.shape[:-1]
        cut = values.reshape(lead + (z_size, y_size, c_size, shard))
        count = len(lead)
        order = tuple(range(count)) + (count + 2, count + 1, count, count + 3)
        return cut.transpose(order).reshape(lead + (width,))

    def outward(values):
        lead = values.shape[:-1]
        cut = values.reshape(lead + (c_size, y_size, z_size, shard))
        count = len(lead)
        order = tuple(range(count)) + (count + 2, count + 1, count, count + 3)
        return cut.transpose(order).reshape(lead + (width,))

    pairs = y_size == 2
    row_axes = ("c", "y", "z")
    positions, allowed = tree_tables(seg_lengths[0], parents[0], group_rows)
    allowed = allowed.astype(jnp.int32)
    cosine, sine = rope_tables(positions, HD)
    attn_gain, attn_post_gain = inward(attn_gain), inward(attn_post_gain)
    ffn_gain, ffn_post_gain = inward(ffn_gain), inward(ffn_post_gain)
    state_in = inward(tokens).astype(F32)
    out_cotan = inward(out_grad).astype(F32)

    qkvo_here = jnp.concatenate(
        [
            weight[:, g * (weight.shape[1] // kv_here) : (g + 1) * (weight.shape[1] // kv_here)]
            for g in range(kv_here)
            for weight in (w_query, w_key, w_value, w_out.T)
        ],
        axis=1,
    )
    inverse_one = lax.rsqrt(jnp.mean(state_in * state_in, axis=-1, keepdims=True) + NORM_EPS)
    unit_one = state_in * inverse_one
    normed_here = (unit_one * attn_gain).astype(BF)

    qkvo_weight = lax.all_gather(qkvo_here, row_axes, axis=0, tiled=True)

    live = {"up": line_cuts(w_up), "down": line_cuts(w_down.T)}
    live["gate"] = line_swaps(line_cuts(w_gate))
    live["normed_one"] = [normed_here, swap(normed_here, "x", 1)]
    live = close(live)

    live["normed_one"] = pair_gather(*live["normed_one"])
    live["gate"] = cut_first(line_place(live["gate"]))
    live["up"] = line_swaps(live["up"])
    live = close(live)

    live["gate"] |= cut_over_x(live["gate"]) | cut_over_y(live["gate"])
    live["up"] = cut_first(line_place(live["up"]))
    live["down"] = line_swaps(live["down"])
    live = close(live)
    live["down"] = line_place(live["down"])

    live["up"] |= cut_over_x(live["up"]) | cut_over_y(live["up"])
    normed_one = live["normed_one"]
    query, key, value, attended, *live["branch"] = attention_call(
        ids, normed_one, qkvo_weight, cosine, sine, allowed, kv_here
    )
    live = close(live)

    sent, kept = live["branch"]
    live["branch"] = [kept, swap(sent, "x", 1)]
    live["gate"], live["up"] = cut_half(live["gate"]), cut_half(live["up"])
    live = close(live)
    down_weight = gather_cut(live.pop("down"))
    branch = live["branch"][0] + live["branch"][1].astype(F32)
    inverse_two = lax.rsqrt(jnp.mean(branch * branch, axis=-1, keepdims=True) + NORM_EPS)
    unit_two = branch * inverse_two
    hidden = state_in + unit_two * attn_post_gain
    inverse_three = lax.rsqrt(jnp.mean(hidden * hidden, axis=-1, keepdims=True) + NORM_EPS)
    unit_three = hidden * inverse_three


    live["normed_two"] = line_gather((unit_three * ffn_gain).astype(BF))
    live |= {name: [live[name], swap(live[name], "c", 1)] for name in ("gate", "up")}
    live = close(live)
    gate_weight, up_weight = Weight(*live["gate"]), Weight(*live["up"])
    down_weight, normed_two = Weight(down_weight), live["normed_two"]

    act, gate_proj, up_proj = ffn_call(
        up_kernel, ids, [normed_two], [gate_weight, up_weight], [], (BF, F32, F32), 256, 0
    )
    sums = ffn_call(down_kernel, ids, [], [down_weight], [act], (), 1152, width)
    live = {"act": act, "sums": line_sum_second(line_sum_first(sums))}
    live = close(live)
    ffn_out = line_total(live["sums"])
    inverse_four = lax.rsqrt(jnp.mean(ffn_out * ffn_out, axis=-1, keepdims=True) + NORM_EPS)
    unit_four = ffn_out * inverse_four
    mixed = (hidden + unit_four * ffn_post_gain).astype(BF)
    gain_four = jnp.sum(out_cotan * unit_four, axis=0)
    d_ffn = norm_back(out_cotan * ffn_post_gain, unit_four, inverse_four).astype(BF)
    live["d_ffn"] = line_gather(d_ffn)
    live = close(live)
    d_ffn, act = live["d_ffn"], live["act"]
    def product(left, right, *got, place=0):
        which = core_here if got else core_there
        if pairs:
            return outer_quarters(ids, which, left, right, *got, place=place)
        made = outer_halves(which, left, (right,), *got)
        return [made] if got else made

    def first_sums(quarters, rows):
        if not pairs:
            return quarters
        *quarters, across = quarters
        return [*quarters, *fold_first(across, rows)]

    def second_sums(quarters):
        if not pairs:
            return [sum_cut(*quarters)]
        own, over_x, over_y, *got = quarters
        over_x, over_y = fold_join({"x": over_x, "y": over_y}, got)
        return [own, swap(over_x, "x", 1), swap(over_y, "y", 1)]

    def over_line(terms):
        return line_swaps(line_chunks(line_total(terms).astype(BF)))

    live = {"down": product(d_ffn, act, swap(product(d_ffn, act), "c", 1))}
    weights = [gate_weight, up_weight, down_weight]
    d_gate, d_up, *sums = ffn_call(
        backward_kernel, ids, [d_ffn], weights, [gate_proj, up_proj], (BF, BF), 384, width
    )
    live = close(live | {"d_gate": d_gate, "d_up": d_up, "sums": sums})

    d_gate, d_up = live["d_gate"], live["d_up"]
    live["sums"] = line_sum_first(live["sums"])
    live["down"] = first_sums(live["down"], 2 * shard)
    if pairs:
        live["sent"] = [outer_pair(ids, core_there, normed_two, d_up, d_gate)]
    else:
        live["sent"] = [product(normed_two, d_up), product(normed_two, d_gate)]
    live = close(live)
    live["sums"] = line_sum_second(live["sums"])
    live["down"] = second_sums(live["down"])
    got = [swap(part, "c", 1) for part in live["sent"]]
    live["up"] = product(normed_two, live["d_up"], got[0], place=0)
    live["gate"] = product(normed_two, live["d_gate"], got[-1], place=1)
    live = close({k: live[k] for k in ("sums", "down", "up", "gate")})

    d_normed_two = line_total(live["sums"])
    gain_three = jnp.sum(d_normed_two * unit_three, axis=0)
    d_hidden = out_cotan + norm_back(d_normed_two * ffn_gain, unit_three, inverse_three)
    gain_two = jnp.sum(d_hidden * unit_two, axis=0)
    d_branch = norm_back(d_hidden * attn_post_gain, unit_two, inverse_two).astype(BF)
    live["d_branch"] = [d_branch, swap(d_branch, "x", 1)]
    live["up"] = first_sums(live["up"], 2 * shard)
    live["gate"] = first_sums(live["gate"], shard)
    live = close({k: live[k] for k in ("d_branch", "down", "up", "gate")})
    d_branch = pair_gather(*live["d_branch"])

    live = {k: live[k] for k in ("down", "up", "gate")}
    live["down"], live["up"] = over_line(live["down"]), second_sums(live["up"])
    d_qkv, d_sent, d_kept = attention_back_call(
        ids, d_branch, qkvo_weight, cosine, sine, allowed, query, key, value, kv_here
    )
    if pairs:
        live["rows"] = outer_rows(ids, core_there, normed_one, d_qkv, d_branch, attended)
    else:
        rows = [outer_dot(normed_one, d_qkv), outer_dot(d_branch, attended)]
        live["rows"] = jnp.concatenate(rows, axis=1).astype(BF)
    live = close(live | {"d_qkv": d_qkv, "d_normed_one": [d_kept, d_sent]})
    grad_down = line_columns(live["down"])

    live["up"], live["gate"] = over_line(live["up"]), second_sums(live["gate"])
    if pairs:
        products = (normed_one, live["d_qkv"], d_branch, attended)
        live["rows"] = outer_rows(ids, core_here, *products, swap(live["rows"], "c", 1))
    live = close({k: live[k] for k in ("up", "gate", "rows", "d_normed_one")})
    grad_up = line_columns(live["up"])

    d_kept, d_sent = live["d_normed_one"]
    live = {"gate": over_line(live["gate"]), "rows": live["rows"]}
    live["d_normed_one"] = [d_kept, swap(d_sent, "x", 1)]
    if pairs:
        far_sent, near_sent, far, near = live["rows"]
        live["rows"] = [near_sent, add_low(far, swap(far_sent, "y", 1)), near]
    live = close(live)
    grad_gate = line_columns(live["gate"])
    d_normed_one = live["d_normed_one"][0] + live["d_normed_one"][1].astype(F32)
    gain_one = jnp.sum(d_normed_one * unit_one, axis=0)
    grad_tokens = d_hidden + norm_back(d_normed_one * attn_gain, unit_one, inverse_one)
    gains = jnp.stack([gain_one, gain_two, gain_three, gain_four], axis=0)

    live = {"rows": live["rows"], "gains": gain_sum(gains)}
    if pairs:
        near_sent, far, near = live["rows"]
        live["rows"] = [near, swap(near_sent, "y", 1), swap(far, "z", 1)]
    live = close(live)

    gains = gain_sum_last(live["gains"])
    rows = live["rows"]
    if pairs:
        far = line_total([part[shard:] for part in rows]).astype(BF)
        grad_rows = line_total([part[:shard] for part in rows] + [swap(far, "z", 2)])
    else:
        grad_rows = lax.psum_scatter(rows, row_axes, scatter_dimension=0, tiled=True)
        grad_rows = grad_rows.astype(F32)
    out_from = grad_rows.shape[1] - attended.shape[1]
    grad_qkv, grad_out = grad_rows[:, :out_from], grad_rows[:, out_from:]
    cols = grad_qkv.shape[1] // kv_here
    cuts = (0, cols - 2 * HD, cols - HD, cols)
    grad_query, grad_key, grad_value = (
        jnp.concatenate(
            [grad_qkv[:, g * cols + cuts[i] : g * cols + cuts[i + 1]] for g in range(kv_here)],
            axis=1,
        )
        for i in range(3)
    )
    return (
        outward(mixed),
        outward(grad_tokens),
        gains[0],
        grad_query,
        grad_key,
        grad_value,
        grad_out.T,
        gains[1],
        gains[2],
        grad_gate,
        grad_up,
        grad_down.T,
        gains[3],
    )


def solution(mesh):
    count, pair = mesh.devices.shape
    grid = Mesh(mesh.devices.reshape(4, count // 8, 2, pair), ("z", "y", "c", "x"))
    rows = ("z", "y", "c")
    return jax.shard_map(
        on_device,
        mesh=grid,
        in_specs=(
            P(rows + ("x",), None),
            P(rows, None),
            P(rows, None),
            P(),
            P(rows, "x"),
            P(rows, "x"),
            P(rows, "x"),
            P("x", rows),
            P(),
            P(),
            P(rows, "x"),
            P(rows, "x"),
            P("x", rows),
            P(),
            P(rows + ("x",), None),
        ),
        out_specs=(
            P(rows + ("x",), None),
            P(rows + ("x",), None),
            P(rows),
            P(rows, "x"),
            P(rows, "x"),
            P(rows, "x"),
            P("x", rows),
            P(rows),
            P(rows),
            P(rows, "x"),
            P(rows, "x"),
            P("x", rows),
            P(rows),
        ),
        check_vma=False,
    )
```

```python
import functools

import jax
import jax.numpy as jnp
from jax import lax
from jax.experimental import pallas as pl
from jax.experimental.pallas import tpu as pltpu
from jax.sharding import Mesh
from jax.sharding import PartitionSpec as P

HD = 256
NORM_EPS = 1e-06
SOFT_CAP = 50.0
ROPE_BASE = 10000.0
MASK_FILL = -1e30
BF = jnp.bfloat16
F32 = jnp.float32


def tree_tables(lengths_row, parents_row, row_total):
    seg_count = lengths_row.shape[0]
    seg_index = jnp.arange(seg_count, dtype=jnp.int32)
    ancestor = (seg_index[:, None] == seg_index[None, :]) | (
        parents_row[:, None] == seg_index[None, :]
    )
    for repeat in range(seg_count.bit_length()):
        ancestor = jnp.any(ancestor[:, :, None] & ancestor[None, :, :], axis=1)
    seg_ends = jnp.cumsum(lengths_row)
    seg_starts = seg_ends - lengths_row
    token_index = jnp.arange(row_total, dtype=jnp.int32)
    segment = jnp.sum((token_index[:, None] >= seg_ends[None, :]).astype(jnp.int32), axis=1)
    strict = ancestor & (seg_index[:, None] != seg_index[None, :])
    offsets = jnp.sum(jnp.where(strict, lengths_row[None, :], 0), axis=1)
    one_hot = segment[:, None] == seg_index[None, :]
    positions = (
        jnp.sum(jnp.where(one_hot, (offsets - seg_starts)[None, :], 0), axis=1) + token_index
    )
    reached = jnp.any(one_hot[:, :, None] & ancestor[None, :, :], axis=1)
    allowed = jnp.any(reached[:, None, :] & one_hot[None, :, :], axis=2) & (
        token_index[None, :] <= token_index[:, None]
    )
    return (positions, allowed)


def rope_tables(positions, width):
    half_width = width // 2
    frequency = ROPE_BASE ** (-2.0 * jnp.arange(half_width, dtype=F32) / width)
    angles = positions.astype(F32)[:, None] * frequency[None, :]
    return (jnp.cos(angles), jnp.sin(angles))


def norm_back(grad_unit, unit, inverse):
    return inverse * (grad_unit - unit * jnp.mean(grad_unit * unit, axis=-1, keepdims=True))


def gelu_parts(values):
    scale = (2.0 / jnp.pi) ** 0.5
    square = values * values
    bent = jnp.tanh(scale * (values + 0.044715 * values * square))
    half = 0.5 * (1.0 + bent)
    slope = half + 0.5 * values * (1.0 - bent * bent) * scale * (1.0 + 3 * 0.044715 * square)
    return values * half, slope


def tile_dot(left, right):
    return jnp.dot(left, right, preferred_element_type=F32)


def tile_dot_cols(left, right):
    return lax.dot_general(left, right, (((1,), (1,)), ((), ())), preferred_element_type=F32)


def spill(ids, total, outs):
    rows = outs[0].shape[0]
    for k, out in enumerate(outs):
        out[...] = total[k * rows : (k + 1) * rows, :].astype(out.dtype)


class Weight:
    def __init__(self, *arrays):
        self.arrays, self.whole = arrays, len(arrays) == 1
        self.rows = arrays[0].shape[-2]

    def specs(self, tile):
        if not self.whole:
            return [pl.BlockSpec((self.rows, tile), lambda i, ids: (0, i))] * 2
        count = self.arrays[0].shape[-1] // tile
        return [pl.BlockSpec((None, self.rows, tile), lambda i, ids: (i // count, 0, i % count))]

    def columns(self, ids):
        if self.whole:
            return (pl.ds(0, self.rows),)
        starts = (pl.multiple_of(core * self.rows, 128) for core in (ids[2], 1 - ids[2]))
        return tuple(pl.ds(start, self.rows) for start in starts)


def inner(values, refs, columns):
    return sum(tile_dot(values[:, at], ref[...]) for ref, at in zip(refs, columns))


def outer_add(total, tile, refs, columns, fresh):
    for ref, at in zip(refs, columns):
        part = tile_dot_cols(tile, ref[...])
        total[:, at] = jnp.where(fresh, part, total[:, at] + part)


def up_kernel(columns, ids, x, *refs):
    gate_w, up_w, (act, gate, up) = refs[:2], refs[2:4], refs[4:]
    gate_at, up_at = (find(ids) for find in columns)
    gate_tile, up_tile = inner(x, gate_w, gate_at), inner(x, up_w, up_at)
    gate[...], up[...] = gate_tile, up_tile
    act[...] = (gelu_parts(gate_tile)[0] * up_tile).astype(BF)


def down_kernel(columns, ids, act, *refs):
    down_w, outs, total = refs[:1], refs[1:-1], refs[-1]
    outer_add(total, act[...], down_w, columns[0](ids), pl.program_id(0) == 0)

    @pl.when(pl.program_id(0) == pl.num_programs(0) - 1)
    def _():
        spill(ids, total, outs)


def backward_kernel(columns, ids, d, *refs):
    gate_w, up_w, down_w, (gate, up), (d_gate, d_up), outs, total = (
        refs[:2], refs[2:4], refs[4:5], refs[5:7], refs[7:9], refs[9:-1], refs[-1]
    )
    gate_at, _, down_at = (find(ids) for find in columns)
    d_act = inner(d, down_w, down_at)
    bent, slope = gelu_parts(gate[...])
    gate_tile = (d_act * up[...] * slope).astype(BF)
    up_tile = (d_act * bent).astype(BF)
    d_gate[...], d_up[...] = gate_tile, up_tile
    fresh = pl.program_id(0) == 0
    for at, gate_ref, up_ref in zip(gate_at, gate_w, up_w):
        part = tile_dot_cols(gate_tile, gate_ref[...]) + tile_dot_cols(up_tile, up_ref[...])
        total[:, at] = jnp.where(fresh, part, total[:, at] + part)

    @pl.when(pl.program_id(0) == pl.num_programs(0) - 1)
    def _():
        spill(ids, total, outs)


def ffn_call(kernel, ids, values, weights, kept, made, tile, width):
    tokens = (values or kept)[0].shape[0]
    cols = weights[-1].arrays[0].shape[-1]
    hidden = 2 * cols if weights[-1].whole else cols
    across = pl.BlockSpec((tokens, tile), lambda i, ids: (0, i))
    parts = [F32, BF, BF, BF] if width else []
    return pl.pallas_call(
        functools.partial(kernel, [weight.columns for weight in weights]),
        grid_spec=pltpu.PrefetchScalarGridSpec(
            num_scalar_prefetch=1,
            grid=(hidden // tile,),
            in_specs=[pl.BlockSpec(array.shape, lambda i, ids: (0, 0)) for array in values]
            + ([] if values else [across] * len(kept))
            + [spec for weight in weights for spec in weight.specs(tile)]
            + ([across] * len(kept) if values else []),
            out_specs=[across] * len(made)
            + [pl.BlockSpec((tokens // 4, width), lambda i, ids: (0, 0)) for _ in parts],
            scratch_shapes=[pltpu.VMEM((tokens, width), F32)] if width else [],
        ),
        out_shape=[jax.ShapeDtypeStruct((tokens, hidden), kind) for kind in made]
        + [jax.ShapeDtypeStruct((tokens // 4, width), kind) for kind in parts],
        compiler_params=pltpu.CompilerParams(
            dimension_semantics=("arbitrary",), vmem_limit_bytes=58 * 2**20
        ),
        cost_estimate=pl.CostEstimate(flops=0, bytes_accessed=0, transcendentals=0),
    )(
        ids,
        *values,
        *([] if values else kept),
        *[array for weight in weights for array in weight.arrays],
        *(kept if values else []),
    )


def swap(values, axis, mask):
    size = lax.axis_size(axis)
    return lax.ppermute(values, axis, [(i, i ^ mask) for i in range(size)])


def rows_dot(left, right):
    return lax.dot_general(left, right, (((1,), (0,)), ((), ())), preferred_element_type=F32)


def cols_dot(left, right):
    return lax.dot_general(left, right, (((1,), (1,)), ((), ())), preferred_element_type=F32)


def outer_dot(left, right):
    return lax.dot_general(left, right, (((0,), (0,)), ((), ())), preferred_element_type=F32)


def close(live):
    return lax.optimization_barrier(live)


def pair_gather(values, other):
    mine = lax.axis_index("x")
    first = jnp.where(mine == 0, values, other)
    second = jnp.where(mine == 0, other, values)
    return jnp.concatenate([first, second], axis=0)


def pair_parts(partial):
    rows = partial.shape[0] // 2
    mine = lax.axis_index("x")
    sent = lax.dynamic_slice_in_dim(partial, (1 - mine) * rows, rows, 0).astype(BF)
    return sent, lax.dynamic_slice_in_dim(partial, mine * rows, rows, 0)


def pair_sum(partial):
    sent, kept = pair_parts(partial)
    return kept + swap(sent, "x", 1).astype(F32)


def rows_sum(values, axis):
    size = lax.axis_size(axis)
    if size != 2:
        return lax.psum_scatter(values, axis, scatter_dimension=0, tiled=True)
    rows, mine = values.shape[0] // 2, lax.axis_index(axis)
    sent = lax.dynamic_slice_in_dim(values, (1 - mine) * rows, rows, 0)
    return add_low(lax.dynamic_slice_in_dim(values, mine * rows, rows, 0), swap(sent, axis, 1))


def placed(rows, *pieces):
    held = jnp.zeros((rows,) + pieces[0][1].shape[1:], pieces[0][1].dtype)
    for offset, piece in pieces:
        held = lax.dynamic_update_slice_in_dim(held, piece, offset, 0)
    return held


def add_low(left, right):
    return (left.astype(F32) + right.astype(F32)).astype(BF)


def line_gather(values):
    near, far = swap(values, "z", 1), swap(values, "z", 2)
    return jnp.concatenate([values, near, far, swap(far, "z", 1)], axis=0)


def line_sum_first(parts):
    return [*parts[:3], swap(parts[3], "z", 1)]


def line_sum_second(parts):
    return [parts[0], swap(parts[1], "z", 1), swap(add_low(parts[2], parts[3]), "z", 2)]


def line_place(pieces):
    here, (rows, cols) = lax.axis_index("z"), pieces[0].shape
    if rows % 16 == 0:
        return assemble(
            (len(pieces) * rows, cols), (rows, cols), [(here ^ k, 0, p) for k, p in enumerate(pieces)]
        )
    return placed(len(pieces) * rows, *[((here ^ k) * rows, p) for k, p in enumerate(pieces)])


def line_cuts(weight):
    here, cut = lax.axis_index("z"), weight.shape[1] // 4
    return [lax.dynamic_slice_in_dim(weight, (here ^ k) * cut, cut, 1) for k in range(4)]


def line_swaps(cuts):
    return [cuts[0]] + [swap(cuts[k], "z", k) for k in (1, 2, 3)]


def line_chunks(grad):
    rows, here = grad.shape[0] // 4, lax.axis_index("z")
    return [lax.dynamic_slice_in_dim(grad, (here ^ k) * rows, rows, 0) for k in range(4)]


def line_columns(pieces):
    here, (rows, cols) = lax.axis_index("z"), pieces[0].shape
    spots = [(0, here ^ k, piece) for k, piece in enumerate(pieces)]
    return assemble((rows, 4 * cols), (rows, cols), spots, F32)


def line_total(pieces):
    total = pieces[0].astype(F32)
    for piece in pieces[1:]:
        total = total + piece.astype(F32)
    return total


def y_chunks(grad):
    rows, y, z = grad.shape[0] // 8, lax.axis_index("y"), lax.axis_index("z")
    return [
        tuple(
            lax.dynamic_slice_in_dim(grad, (4 * side + (z ^ k)) * rows, rows, 0)
            for side in (y, 1 - y)
        )
        for k in range(4)
    ]


def pair_rows(mine, other, axis):
    rows, here = mine.shape[0], lax.axis_index(axis)
    return placed(2 * rows, (here * rows, mine), ((1 - here) * rows, other))


def pair_halves(values, axis):
    rows, here = values.shape[0] // 2, lax.axis_index(axis)
    return (
        lax.dynamic_slice_in_dim(values, here * rows, rows, 0),
        lax.dynamic_slice_in_dim(values, (1 - here) * rows, rows, 0),
    )


def cut_first(own):
    got = {"own": own, "x": swap(own, "x", 1)}
    if lax.axis_size("y") == 2:
        got["y"] = swap(own, "y", 1)
    return got


def cut_over_x(got):
    rows = got["own"].shape[0] // 2
    return {"over_x": swap(got["y"][:rows], "x", 1)} if "y" in got else {}


def cut_over_y(got):
    rows = got["own"].shape[0] // 2
    return {"over_y": swap(got["x"][rows:], "y", 1)} if "y" in got else {}


def cut_half(got):
    own = got["own"]
    rows, cols = own.shape
    if "y" not in got:
        both = jnp.where(
            lax.axis_index("x") == 0,
            jnp.concatenate([own, got["x"]], axis=1),
            jnp.concatenate([got["x"], own], axis=1),
        )
        return lax.all_gather(both, "y", axis=0, tiled=True)
    here, half = lax.axis_index("y"), lax.axis_index("x")
    mine, far = 2 * here, 2 * (1 - here)
    spots = [
        (mine, half, own),
        (far, half, got["y"]),
        (mine, 1 - half, got["x"]),
        (far, 1 - half, got["over_x"]),
        (far + 1, 1 - half, got["over_y"]),
    ]
    return assemble((2 * rows, 2 * cols), (rows // 2, cols), spots)


def fold_parts(both):
    cols, here = both.shape[1] // 2, lax.axis_index("x")
    mine = lax.dynamic_slice_in_dim(both, here * cols, cols, 1)
    other = lax.dynamic_slice_in_dim(both, (1 - here) * cols, cols, 1)
    (own, over_y), (over_x, across) = pair_halves(mine, "y"), pair_halves(other, "y")
    return {"own": own, "x": over_x, "y": over_y, "across": across}


def fold_first(across, rows):
    return [swap(across[:rows], "x", 1), swap(across[rows:], "y", 1)]


def fold_join(parts, got):
    rows = got[0].shape[0]
    over_y = add_low(parts["y"][:rows], got[0])
    over_x = add_low(parts["x"][rows:], got[1])
    return (
        jnp.concatenate([parts["x"][:rows], over_x]),
        jnp.concatenate([over_y, parts["y"][rows:]]),
    )


def spread_ids():
    return jnp.stack([lax.axis_index(axis) for axis in ("z", "y", "c", "x")]).astype(jnp.int32)


LIGHT = pl.CostEstimate(flops=0, bytes_accessed=0, transcendentals=0)


def kernel_params(megabytes=50):
    return pltpu.CompilerParams(
        dimension_semantics=("arbitrary",), vmem_limit_bytes=megabytes * 2**20
    )


def turned(values, cosine, sine):
    half = values.shape[1] // 2
    front, back = values[:, :half], values[:, half:]
    return jnp.concatenate([front * cosine - back * sine, back * cosine + front * sine], axis=1)


def head_probs(query, key, allowed):
    scores = tile_dot_cols(query, key)
    bent = jnp.tanh(scores * (HD**-0.5 / SOFT_CAP))
    masked = jnp.where(allowed != 0, SOFT_CAP * bent, MASK_FILL)
    weights = jnp.exp(masked - jnp.max(masked, axis=1, keepdims=True))
    return bent, weights / jnp.sum(weights, axis=1, keepdims=True)


def share(ids, total, sent, kept):
    rows = sent.shape[0]
    here = ids[3]
    sent[...] = total[pl.ds(pl.multiple_of((1 - here) * rows, rows), rows), :].astype(BF)
    kept[...] = total[pl.ds(pl.multiple_of(here * rows, rows), rows), :]


def attention_kernel(
    ids, x, weight, cosine, sine, allowed, query, key, value, attended, sent, kept, total
):
    heads = query.shape[1] // HD
    keys = heads * HD
    proj = tile_dot(x[...], weight[:, : keys + 2 * HD])
    key_here = turned(proj[:, keys : keys + HD], cosine[...], sine[...]).astype(BF)
    value_here = proj[:, keys + HD :].astype(BF)
    key[...], value[...] = key_here, value_here
    for head in range(heads):
        at = slice(head * HD, (head + 1) * HD)
        query_here = turned(proj[:, at], cosine[...], sine[...]).astype(BF)
        query[:, at] = query_here
        probs = head_probs(query_here, key_here, allowed[...])[1].astype(BF)
        attended[:, at] = tile_dot(probs, value_here).astype(BF)
    part = tile_dot_cols(attended[...], weight[:, keys + 2 * HD :])
    total[...] = jnp.where(pl.program_id(0) == 0, part, total[...] + part)

    @pl.when(pl.program_id(0) == pl.num_programs(0) - 1)
    def _():
        share(ids, total, sent, kept)


def attention_specs(tokens, width, cols, heads):
    def here(rows, cut):
        return pl.BlockSpec((rows, cut), lambda g, ids: (0, g))

    def whole(rows, cut):
        return pl.BlockSpec((rows, cut), lambda g, ids: (0, 0))

    first = [whole(tokens, width), here(width, cols)]
    tables = [whole(tokens, HD // 2), whole(tokens, HD // 2), whole(tokens, tokens)]
    held = [here(tokens, cut) for cut in (heads * HD, HD, HD)]
    halves = [whole(tokens // 2, width)] * 2
    return first, tables, held, halves, here


def attention_call(ids, x, weight, cosine, sine, allowed, groups):
    tokens, width = x.shape
    cols = weight.shape[1] // groups
    heads = (cols // HD - 2) // 2
    first, tables, held, halves, here = attention_specs(tokens, width, cols, heads)
    shapes = [groups * cut for cut in (heads * HD, HD, HD, heads * HD)]
    return pl.pallas_call(
        attention_kernel,
        grid_spec=pltpu.PrefetchScalarGridSpec(
            num_scalar_prefetch=1,
            grid=(groups,),
            in_specs=first + tables,
            out_specs=held + [here(tokens, heads * HD)] + halves,
            scratch_shapes=[pltpu.VMEM((tokens, width), F32)],
        ),
        out_shape=[jax.ShapeDtypeStruct((tokens, cut), BF) for cut in shapes]
        + [jax.ShapeDtypeStruct((tokens // 2, width), kind) for kind in (BF, F32)],
        compiler_params=kernel_params(),
        cost_estimate=LIGHT,
    )(ids, x, weight, cosine, sine, allowed)


def attention_back_kernel(
    ids, d, weight, cosine, sine, allowed, query, key, value, d_qkv, sent, kept, total
):
    heads = query.shape[1] // HD
    cut = (heads + 2) * HD
    key_here, value_here = key[...], value[...]
    d_attended = tile_dot(d[...], weight[:, cut:]).astype(BF)
    d_key = d_value = 0.0
    pieces = []
    for head in range(heads):
        at = slice(head * HD, (head + 1) * HD)
        query_here, d_here = query[:, at], d_attended[:, at]
        bent, probs = head_probs(query_here, key_here, allowed[...])
        d_probs = tile_dot_cols(d_here, value_here)
        inner = jnp.sum(probs * d_probs, axis=1, keepdims=True)
        d_scores = probs * (d_probs - inner) * (HD**-0.5) * (1.0 - bent * bent)
        d_scores = d_scores.astype(BF)
        d_query = tile_dot(d_scores, key_here)
        pieces.append(turned(d_query, cosine[...], -sine[...]).astype(BF))
        d_key = d_key + outer_dot(d_scores, query_here)
        d_value = d_value + outer_dot(probs.astype(BF), d_here)
    pieces.append(turned(d_key, cosine[...], -sine[...]).astype(BF))
    pieces.append(d_value.astype(BF))
    made = jnp.concatenate(pieces, axis=1)
    d_qkv[...] = made
    part = tile_dot_cols(made, weight[:, :cut])
    total[...] = jnp.where(pl.program_id(0) == 0, part, total[...] + part)

    @pl.when(pl.program_id(0) == pl.num_programs(0) - 1)
    def _():
        share(ids, total, sent, kept)


def attention_back_call(ids, d, weight, cosine, sine, allowed, query, key, value, groups):
    tokens, width = d.shape
    cols = weight.shape[1] // groups
    heads = (cols // HD - 2) // 2
    first, tables, held, halves, here = attention_specs(tokens, width, cols, heads)
    cut = (heads + 2) * HD
    return pl.pallas_call(
        attention_back_kernel,
        grid_spec=pltpu.PrefetchScalarGridSpec(
            num_scalar_prefetch=1,
            grid=(groups,),
            in_specs=first + tables + held,
            out_specs=[here(tokens, cut)] + halves,
            scratch_shapes=[pltpu.VMEM((tokens, width), F32)],
        ),
        out_shape=[
            jax.ShapeDtypeStruct((tokens, groups * cut), BF),
            jax.ShapeDtypeStruct((tokens // 2, width), BF),
            jax.ShapeDtypeStruct((tokens // 2, width), F32),
        ],
        compiler_params=kernel_params(),
        cost_estimate=LIGHT,
    )(ids, d, weight, cosine, sine, allowed, query, key, value)


def outer_kernel(which, left, right, *rest):
    got, (made, flipped) = rest[:-2], rest[-2:]

    @pl.when(pl.program_id(0) == 0)
    def _():
        flipped[...] = left[...].T

    total = tile_dot(flipped[...], right[...])
    for piece in got:
        total = total + piece[...].astype(F32)
    made[...] = total.astype(BF)


def outer_call(left, right, which, *got):
    tokens, cut, cols = left.shape[0], left.shape[1] // 2, right.shape[1]
    tile = cols // 2
    across = pl.BlockSpec((cut, tile), lambda i, which: (0, i))
    return pl.pallas_call(
        outer_kernel,
        grid_spec=pltpu.PrefetchScalarGridSpec(
            num_scalar_prefetch=1,
            grid=(cols // tile,),
            in_specs=[
                pl.BlockSpec((tokens, cut), lambda i, which: (0, which[0])),
                pl.BlockSpec((tokens, tile), lambda i, which: (0, i)),
            ]
            + [across] * len(got),
            out_specs=across,
            scratch_shapes=[pltpu.VMEM((cut, tokens), BF)],
        ),
        out_shape=jax.ShapeDtypeStruct((cut, cols), BF),
        compiler_params=kernel_params(),
        cost_estimate=LIGHT,
    )(which, left, right, *got)


def outer_halves_kernel(number, which, left, *refs):
    rights, got, (made, flipped) = refs[:number], refs[number:-2], refs[-2:]
    step = pl.program_id(0)

    @pl.when(step == 0)
    def _():
        flipped[...] = left[...].T

    for k, right in enumerate(rights):

        @pl.when(step % number == k)
        def _(right=right):
            total = tile_dot(flipped[...], right[...])
            for piece in got:
                total = total + piece[...].astype(F32)
            made[...] = total.astype(BF)


def outer_halves(which, left, rights, *got):
    tokens, cut = left.shape[0], left.shape[1] // 2
    cols, number = rights[0].shape[1] // 2, len(rights)
    across = pl.BlockSpec((None, cut, cols), lambda i, which: (i // number, 0, i % number))
    return pl.pallas_call(
        functools.partial(outer_halves_kernel, number),
        grid_spec=pltpu.PrefetchScalarGridSpec(
            num_scalar_prefetch=1,
            grid=(2 * number,),
            in_specs=[pl.BlockSpec((tokens, cut), lambda i, which: (0, which[0]))]
            + [pl.BlockSpec((tokens, cols), lambda i, which: (0, i // number))] * number
            + [across] * len(got),
            out_specs=across,
            scratch_shapes=[pltpu.VMEM((cut, tokens), BF)],
        ),
        out_shape=jax.ShapeDtypeStruct((2, cut, number * cols), BF),
        compiler_params=kernel_params(),
        cost_estimate=LIGHT,
    )(which, left, *rights, *got)


def sum_cut(grad):
    half, cols = grad.shape[1:]
    blocks = 2 * lax.axis_size("y")
    grad = grad.reshape(blocks, 2 * half // blocks, cols)
    return lax.psum_scatter(grad, ("x", "y"), scatter_dimension=0, tiled=True)[0]


def gather_cut(own):
    whole = lax.all_gather(own, ("x", "c", "y"), axis=0, tiled=True)
    return whole.reshape(2, -1, own.shape[1])


def outer_low(left, right, mine, theirs):
    sent = outer_call(left, right, theirs)
    return outer_call(left, right, mine, swap(sent, "c", 1))


def outer_quarters_kernel(ids, which, left, right, *refs):
    (plain, flipped), refs = refs[-2:], refs[:-2]
    got, outs = (refs[:4], refs[4:]) if len(refs) > 1 else ((), refs)
    step, rows = pl.program_id(0), flipped.shape[0] // 2

    @pl.when(step == 0)
    def _():
        plain[...] = left[...].T
        for k, side in enumerate((ids[1], 1 - ids[1])):
            at = pl.multiple_of(side * rows, rows)
            flipped[k * rows : (k + 1) * rows, :] = plain[pl.ds(at, rows), :]

    for half in range(2):

        @pl.when(step % 2 == half)
        def _(half=half):
            for side in range(2):
                k = half + 2 * side
                total = tile_dot(flipped[side * rows : (side + 1) * rows, :], right[...])
                if got:
                    outs[k][...] = (total + got[k][...].astype(F32)).astype(BF)
                else:
                    outs[0][side] = total.astype(BF)


def outer_quarters(ids, which, left, right, *got, place=0):
    tokens, cut, cols = left.shape[0], left.shape[1] // 2, right.shape[1] // 2
    rows = cut // 2
    quarter = pl.BlockSpec((rows, cols), lambda i, ids, which: (0, 0))
    taken = [
        pl.BlockSpec((None, rows, cols), lambda i, ids, which, k=k: (2 * place + k // 2, 0, k % 2))
        for k in range(4)
    ]
    shape = jax.ShapeDtypeStruct((rows, cols), BF)
    return pl.pallas_call(
        outer_quarters_kernel,
        grid_spec=pltpu.PrefetchScalarGridSpec(
            num_scalar_prefetch=2,
            grid=(2,),
            in_specs=[
                pl.BlockSpec((tokens, cut), lambda i, ids, which: (0, which[0])),
                pl.BlockSpec((tokens, cols), lambda i, ids, which: (0, ids[3] ^ i)),
            ]
            + (taken if got else []),
            out_specs=[quarter] * 4
            if got
            else pl.BlockSpec((2, rows, cols), lambda i, ids, which: (0, 0, i)),
            scratch_shapes=[pltpu.VMEM((cut, tokens), BF)] * 2,
        ),
        out_shape=[shape] * 4 if got else jax.ShapeDtypeStruct((2, rows, 2 * cols), BF),
        compiler_params=kernel_params(),
        cost_estimate=LIGHT,
    )(ids, which, left, right, *got * 4)


def outer_pair_kernel(ids, which, left, right_a, right_b, made, plain, flipped):
    step, rows = pl.program_id(0), flipped.shape[0] // 2

    @pl.when(step == 0)
    def _():
        plain[...] = left[...].T
        for k, side in enumerate((ids[1], 1 - ids[1])):
            at = pl.multiple_of(side * rows, rows)
            flipped[k * rows : (k + 1) * rows, :] = plain[pl.ds(at, rows), :]

    for k, right in enumerate((right_a, right_b)):

        @pl.when(step // 2 == k)
        def _(right=right):
            for side in range(2):
                at = slice(side * rows, (side + 1) * rows)
                made[side] = tile_dot(flipped[at, :], right[...]).astype(BF)


def outer_pair(ids, which, left, right_a, right_b):
    tokens, cut, cols = left.shape[0], left.shape[1] // 2, right_a.shape[1] // 2
    rows = cut // 2
    return pl.pallas_call(
        outer_pair_kernel,
        grid_spec=pltpu.PrefetchScalarGridSpec(
            num_scalar_prefetch=2,
            grid=(4,),
            in_specs=[
                pl.BlockSpec((tokens, cut), lambda i, ids, which: (0, which[0])),
                pl.BlockSpec((tokens, cols), lambda i, ids, which: (0, ids[3] ^ jnp.minimum(i, 1))),
                pl.BlockSpec(
                    (tokens, cols), lambda i, ids, which: (0, ids[3] ^ jnp.maximum(i - 2, 0))
                ),
            ],
            out_specs=pl.BlockSpec((2, rows, cols), lambda i, ids, which: (i // 2, 0, i % 2)),
            scratch_shapes=[pltpu.VMEM((cut, tokens), BF)] * 2,
        ),
        out_shape=jax.ShapeDtypeStruct((4, rows, 2 * cols), BF),
        compiler_params=kernel_params(),
        cost_estimate=LIGHT,
    )(ids, which, left, right_a, right_b)


def outer_rows_kernel(ids, which, left_a, left_b, right_a, right_b, *refs):
    (plain, flipped), refs = refs[-2:], refs[:-2]
    got, outs = (refs[:4], refs[4:]) if len(refs) > 1 else ((), refs)
    step, last = pl.program_id(0), pl.num_programs(0) - 1
    rows = flipped.shape[0] // 8
    z, y = ids[0], ids[1]
    order = [4 * side + (z ^ k) for side in (1 - y, y) for k in (1, 3, 0, 2)]
    for left, when in ((left_a, 0), (left_b, last)):

        @pl.when(step == when)
        def _(left=left):
            plain[...] = left[...].T
            for k, block in enumerate(order):
                at = pl.multiple_of(block * rows, rows)
                flipped[k * rows : (k + 1) * rows, :] = plain[pl.ds(at, rows), :]

    def give(right):
        total = tile_dot(flipped[...], right[...])
        if not got:
            outs[0][...] = total.astype(BF)
        for k, piece in enumerate(got):
            part = total[2 * k * rows : (2 * k + 2) * rows, :]
            outs[k][...] = (part + piece[...].astype(F32)).astype(BF)

    @pl.when(step < last)
    def _():
        give(right_a)

    @pl.when(step == last)
    def _():
        give(right_b)


def outer_rows(ids, which, left_a, right_a, left_b, right_b, *got):
    tokens, cut = left_a.shape[0], left_a.shape[1] // 2
    tile = right_b.shape[1]
    cols = right_a.shape[1] + tile
    rows = cut // 4
    count = cols // tile
    half = pl.BlockSpec((tokens, cut), lambda i, ids, which: (0, which[0]))
    across = pl.BlockSpec((rows, tile), lambda i, ids, which: (0, i))
    taken = [pl.BlockSpec((rows, tile), lambda i, ids, which, k=k: (k, i)) for k in range(4)]
    return pl.pallas_call(
        outer_rows_kernel,
        grid_spec=pltpu.PrefetchScalarGridSpec(
            num_scalar_prefetch=2,
            grid=(count,),
            in_specs=[
                half,
                half,
                pl.BlockSpec((tokens, tile), lambda i, ids, which: (0, jnp.minimum(i, count - 2))),
                pl.BlockSpec((tokens, tile), lambda i, ids, which: (0, 0)),
            ]
            + (taken if got else []),
            out_specs=[across] * 4
            if got
            else pl.BlockSpec((cut, tile), lambda i, ids, which: (0, i)),
            scratch_shapes=[pltpu.VMEM((cut, tokens), BF)] * 2,
        ),
        out_shape=[jax.ShapeDtypeStruct((rows, cols), BF)] * 4
        if got
        else jax.ShapeDtypeStruct((cut, cols), BF),
        compiler_params=kernel_params(),
        cost_estimate=LIGHT,
    )(ids, which, left_a, left_b, right_a, right_b, *got * 4)


def assemble_kernel(counts, rows, cols, *refs):
    pieces, made = refs[:-1], refs[-1]
    step, first = pl.program_id(0), 0
    for piece, count in zip(pieces, counts):

        @pl.when((step >= first) & (step < first + count))
        def _(piece=piece):
            made[...] = piece[...].astype(made.dtype)

        first += count


def assemble(shape, block, placed, kind=BF):
    counts = [array.shape[0] // block[0] for _, _, array in placed]
    steps = [(row + k, col) for (row, col, _), n in zip(placed, counts) for k in range(n)]
    rows, cols = (jnp.stack([jnp.asarray(s[i], jnp.int32) for s in steps]) for i in range(2))
    specs, first = [], 0
    for count in counts:

        def at(step, rows, cols, first=first, count=count):
            return (jnp.clip(step - first, 0, count - 1), 0)

        specs.append(pl.BlockSpec(block, at))
        first += count
    return pl.pallas_call(
        functools.partial(assemble_kernel, counts),
        grid_spec=pltpu.PrefetchScalarGridSpec(
            num_scalar_prefetch=2,
            grid=(len(steps),),
            in_specs=specs,
            out_specs=pl.BlockSpec(block, lambda step, rows, cols: (rows[step], cols[step])),
        ),
        out_shape=jax.ShapeDtypeStruct(shape, kind),
        compiler_params=kernel_params(),
        cost_estimate=LIGHT,
    )(rows, cols, *[array for _, _, array in placed])


def gain_sum(parts):
    count = parts.shape[0]
    c_size, y_size, z_size = (lax.axis_size(axis) for axis in ("c", "y", "z"))
    parts = parts + swap(parts, "x", 1)
    parts = parts.reshape(count, c_size, y_size, z_size, -1).transpose(1, 2, 3, 0, 4)
    here = lax.axis_index("c")
    sent = lax.dynamic_index_in_dim(parts, 1 - here, 0, keepdims=False)
    return lax.dynamic_index_in_dim(parts, here, 0, keepdims=False) + swap(sent, "c", 1)


def gain_sum_last(parts):
    if lax.axis_size("y") == 2:
        here = lax.axis_index("y")
        sent = lax.dynamic_index_in_dim(parts, 1 - here, 0, keepdims=False)
        parts = lax.dynamic_index_in_dim(parts, here, 0, keepdims=False) + swap(sent, "y", 1)
    else:
        parts = lax.psum_scatter(parts, "y", scatter_dimension=0, tiled=True)[0]
    here = lax.axis_index("z")
    total = lax.dynamic_index_in_dim(parts, here, 0, keepdims=False)
    for k in (1, 2, 3):
        piece = lax.dynamic_index_in_dim(parts, here ^ k, 0, keepdims=False)
        total = total + swap(piece, "z", k)
    return total


def on_device(
    tokens,
    seg_lengths,
    parents,
    attn_gain,
    w_query,
    w_key,
    w_value,
    w_out,
    attn_post_gain,
    ffn_gain,
    w_gate,
    w_up,
    w_down,
    ffn_post_gain,
    out_grad,
):
    local_rows, width = tokens.shape
    z_size, y_size, c_size = lax.axis_size("z"), lax.axis_size("y"), lax.axis_size("c")
    shard = width // (z_size * y_size * c_size)
    group_rows = local_rows * lax.axis_size("x")
    head_cols = w_query.shape[1]
    kv_cols = w_key.shape[1]
    kv_here = kv_cols // HD
    ids = spread_ids()
    core_here, core_there = ids[2:3], 1 - ids[2:3]
    first_half, second_half = jnp.zeros(1, jnp.int32), jnp.ones(1, jnp.int32)

    def inward(values):
        lead = values.shape[:-1]
        cut = values.reshape(lead + (z_size, y_size, c_size, shard))
        count = len(lead)
        order = tuple(range(count)) + (count + 2, count + 1, count, count + 3)
        return cut.transpose(order).reshape(lead + (width,))

    def outward(values):
        lead = values.shape[:-1]
        cut = values.reshape(lead + (c_size, y_size, z_size, shard))
        count = len(lead)
        order = tuple(range(count)) + (count + 2, count + 1, count, count + 3)
        return cut.transpose(order).reshape(lead + (width,))

    pairs = y_size == 2
    row_axes = ("c", "y", "z")
    positions, allowed = tree_tables(seg_lengths[0], parents[0], group_rows)
    allowed = allowed.astype(jnp.int32)
    cosine, sine = rope_tables(positions, HD)
    attn_gain, attn_post_gain = inward(attn_gain), inward(attn_post_gain)
    ffn_gain, ffn_post_gain = inward(ffn_gain), inward(ffn_post_gain)
    state_in = inward(tokens).astype(F32)
    out_cotan = inward(out_grad).astype(F32)

    qkvo_here = jnp.concatenate(
        [
            weight[:, g * (weight.shape[1] // kv_here) : (g + 1) * (weight.shape[1] // kv_here)]
            for g in range(kv_here)
            for weight in (w_query, w_key, w_value, w_out.T)
        ],
        axis=1,
    )
    inverse_one = lax.rsqrt(jnp.mean(state_in * state_in, axis=-1, keepdims=True) + NORM_EPS)
    unit_one = state_in * inverse_one
    normed_here = (unit_one * attn_gain).astype(BF)

    qkvo_weight = lax.all_gather(qkvo_here, row_axes, axis=0, tiled=True)

    live = {"up": line_cuts(w_up), "down": line_cuts(w_down.T)}
    live["gate"] = line_swaps(line_cuts(w_gate))
    live["normed_one"] = [normed_here, swap(normed_here, "x", 1)]
    live = close(live)

    live["normed_one"] = pair_gather(*live["normed_one"])
    live["gate"] = cut_first(line_place(live["gate"]))
    live["up"] = line_swaps(live["up"])
    live = close(live)

    live["gate"] |= cut_over_x(live["gate"]) | cut_over_y(live["gate"])
    live["up"] = cut_first(line_place(live["up"]))
    live["down"] = line_swaps(live["down"])
    live = close(live)
    live["down"] = line_place(live["down"])

    live["up"] |= cut_over_x(live["up"]) | cut_over_y(live["up"])
    normed_one = live["normed_one"]
    query, key, value, attended, *live["branch"] = attention_call(
        ids, normed_one, qkvo_weight, cosine, sine, allowed, kv_here
    )
    live = close(live)

    sent, kept = live["branch"]
    live["branch"] = [kept, swap(sent, "x", 1)]
    live["gate"], live["up"] = cut_half(live["gate"]), cut_half(live["up"])
    live = close(live)
    down_weight = gather_cut(live.pop("down"))
    branch = live["branch"][0] + live["branch"][1].astype(F32)
    inverse_two = lax.rsqrt(jnp.mean(branch * branch, axis=-1, keepdims=True) + NORM_EPS)
    unit_two = branch * inverse_two
    hidden = state_in + unit_two * attn_post_gain
    inverse_three = lax.rsqrt(jnp.mean(hidden * hidden, axis=-1, keepdims=True) + NORM_EPS)
    unit_three = hidden * inverse_three


    live["normed_two"] = line_gather((unit_three * ffn_gain).astype(BF))
    live |= {name: [live[name], swap(live[name], "c", 1)] for name in ("gate", "up")}
    live = close(live)
    gate_weight, up_weight = Weight(*live["gate"]), Weight(*live["up"])
    down_weight, normed_two = Weight(down_weight), live["normed_two"]

    act, gate_proj, up_proj = ffn_call(
        up_kernel, ids, [normed_two], [gate_weight, up_weight], [], (BF, F32, F32), 256, 0
    )
    sums = ffn_call(down_kernel, ids, [], [down_weight], [act], (), 1152, width)
    live = {"act": act, "sums": line_sum_second(line_sum_first(sums))}
    live = close(live)
    ffn_out = line_total(live["sums"])
    inverse_four = lax.rsqrt(jnp.mean(ffn_out * ffn_out, axis=-1, keepdims=True) + NORM_EPS)
    unit_four = ffn_out * inverse_four
    mixed = (hidden + unit_four * ffn_post_gain).astype(BF)
    gain_four = jnp.sum(out_cotan * unit_four, axis=0)
    d_ffn = norm_back(out_cotan * ffn_post_gain, unit_four, inverse_four).astype(BF)
    live["d_ffn"] = line_gather(d_ffn)
    live = close(live)
    d_ffn, act = live["d_ffn"], live["act"]
    def product(left, right, *got, place=0):
        which = core_here if got else core_there
        if pairs:
            return outer_quarters(ids, which, left, right, *got, place=place)
        made = outer_halves(which, left, (right,), *got)
        return [made] if got else made

    def first_sums(quarters, rows):
        if not pairs:
            return quarters
        *quarters, across = quarters
        return [*quarters, *fold_first(across, rows)]

    def second_sums(quarters):
        if not pairs:
            return [sum_cut(*quarters)]
        own, over_x, over_y, *got = quarters
        over_x, over_y = fold_join({"x": over_x, "y": over_y}, got)
        return [own, swap(over_x, "x", 1), swap(over_y, "y", 1)]

    def over_line(terms):
        return line_swaps(line_chunks(line_total(terms).astype(BF)))

    live = {"down": product(d_ffn, act, swap(product(d_ffn, act), "c", 1))}
    weights = [gate_weight, up_weight, down_weight]
    d_gate, d_up, *sums = ffn_call(
        backward_kernel, ids, [d_ffn], weights, [gate_proj, up_proj], (BF, BF), 384, width
    )
    live = close(live | {"d_gate": d_gate, "d_up": d_up, "sums": sums})

    d_gate, d_up = live["d_gate"], live["d_up"]
    live["sums"] = line_sum_first(live["sums"])
    live["down"] = first_sums(live["down"], 2 * shard)
    if pairs:
        live["sent"] = [outer_pair(ids, core_there, normed_two, d_up, d_gate)]
    else:
        live["sent"] = [product(normed_two, d_up), product(normed_two, d_gate)]
    live = close(live)
    live["sums"] = line_sum_second(live["sums"])
    live["down"] = second_sums(live["down"])
    got = [swap(part, "c", 1) for part in live["sent"]]
    live["up"] = product(normed_two, live["d_up"], got[0], place=0)
    live["gate"] = product(normed_two, live["d_gate"], got[-1], place=1)
    live = close({k: live[k] for k in ("sums", "down", "up", "gate")})

    d_normed_two = line_total(live["sums"])
    gain_three = jnp.sum(d_normed_two * unit_three, axis=0)
    d_hidden = out_cotan + norm_back(d_normed_two * ffn_gain, unit_three, inverse_three)
    gain_two = jnp.sum(d_hidden * unit_two, axis=0)
    d_branch = norm_back(d_hidden * attn_post_gain, unit_two, inverse_two).astype(BF)
    live["d_branch"] = [d_branch, swap(d_branch, "x", 1)]
    live["up"] = first_sums(live["up"], 2 * shard)
    live["gate"] = first_sums(live["gate"], shard)
    live = close({k: live[k] for k in ("d_branch", "down", "up", "gate")})
    d_branch = pair_gather(*live["d_branch"])

    live = {k: live[k] for k in ("down", "up", "gate")}
    live["down"], live["up"] = over_line(live["down"]), second_sums(live["up"])
    d_qkv, d_sent, d_kept = attention_back_call(
        ids, d_branch, qkvo_weight, cosine, sine, allowed, query, key, value, kv_here
    )
    if pairs:
        live["rows"] = outer_rows(ids, core_there, normed_one, d_qkv, d_branch, attended)
    else:
        rows = [outer_dot(normed_one, d_qkv), outer_dot(d_branch, attended)]
        live["rows"] = jnp.concatenate(rows, axis=1).astype(BF)
    live = close(live | {"d_qkv": d_qkv, "d_normed_one": [d_kept, d_sent]})
    grad_down = line_columns(live["down"])

    live["up"], live["gate"] = over_line(live["up"]), second_sums(live["gate"])
    if pairs:
        products = (normed_one, live["d_qkv"], d_branch, attended)
        live["rows"] = outer_rows(ids, core_here, *products, swap(live["rows"], "c", 1))
    live = close({k: live[k] for k in ("up", "gate", "rows", "d_normed_one")})
    grad_up = line_columns(live["up"])

    d_kept, d_sent = live["d_normed_one"]
    live = {"gate": over_line(live["gate"]), "rows": live["rows"]}
    live["d_normed_one"] = [d_kept, swap(d_sent, "x", 1)]
    if pairs:
        far_sent, near_sent, far, near = live["rows"]
        live["rows"] = [near_sent, add_low(far, swap(far_sent, "y", 1)), near]
    live = close(live)
    grad_gate = line_columns(live["gate"])
    d_normed_one = live["d_normed_one"][0] + live["d_normed_one"][1].astype(F32)
    gain_one = jnp.sum(d_normed_one * unit_one, axis=0)
    grad_tokens = d_hidden + norm_back(d_normed_one * attn_gain, unit_one, inverse_one)
    gains = jnp.stack([gain_one, gain_two, gain_three, gain_four], axis=0)

    live = {"rows": live["rows"], "gains": gain_sum(gains)}
    if pairs:
        near_sent, far, near = live["rows"]
        live["rows"] = [near, swap(near_sent, "y", 1), swap(far, "z", 1)]
    live = close(live)

    gains = gain_sum_last(live["gains"])
    rows = live["rows"]
    if pairs:
        far = line_total([part[shard:] for part in rows]).astype(BF)
        grad_rows = line_total([part[:shard] for part in rows] + [swap(far, "z", 2)])
    else:
        grad_rows = lax.psum_scatter(rows, row_axes, scatter_dimension=0, tiled=True)
        grad_rows = grad_rows.astype(F32)
    out_from = grad_rows.shape[1] - attended.shape[1]
    grad_qkv, grad_out = grad_rows[:, :out_from], grad_rows[:, out_from:]
    cols = grad_qkv.shape[1] // kv_here
    cuts = (0, cols - 2 * HD, cols - HD, cols)
    grad_query, grad_key, grad_value = (
        jnp.concatenate(
            [grad_qkv[:, g * cols + cuts[i] : g * cols + cuts[i + 1]] for g in range(kv_here)],
            axis=1,
        )
        for i in range(3)
    )
    return (
        outward(mixed),
        outward(grad_tokens),
        gains[0],
        grad_query,
        grad_key,
        grad_value,
        grad_out.T,
        gains[1],
        gains[2],
        grad_gate,
        grad_up,
        grad_down.T,
        gains[3],
    )


def solution(mesh):
    count, pair = mesh.devices.shape
    grid = Mesh(mesh.devices.reshape(4, count // 8, 2, pair), ("z", "y", "c", "x"))
    rows = ("z", "y", "c")
    return jax.shard_map(
        on_device,
        mesh=grid,
        in_specs=(
            P(rows + ("x",), None),
            P(rows, None),
            P(rows, None),
            P(),
            P(rows, "x"),
            P(rows, "x"),
            P(rows, "x"),
            P("x", rows),
            P(),
            P(),
            P(rows, "x"),
            P(rows, "x"),
            P("x", rows),
            P(),
            P(rows + ("x",), None),
        ),
        out_specs=(
            P(rows + ("x",), None),
            P(rows + ("x",), None),
            P(rows),
            P(rows, "x"),
            P(rows, "x"),
            P(rows, "x"),
            P("x", rows),
            P(rows),
            P(rows),
            P(rows, "x"),
            P(rows, "x"),
            P("x", rows),
            P(rows),
        ),
        check_vma=False,
    )
```
